32 devices in a mesh: res: 8 (over z, y), head: 4 (over x, core).
Axes of the slice: x: 2, y: 2, z: 4, core: 2. Of those that a mesh axis runs over, the one named last changes fastest.
Arguments:
- pair_input: bfloat16 [2, 256, 256, 128], P(None, 'res'), may hold values from -6 to 6
- lengths: int32 [2], replicated, may hold values from 60 to 256, as said below
- distogram_bins: int32 [2, 256, 256], P(None, 'res'), may hold values from 0 to 63
- head_proj: float32 [128, 512], P(None, 'head'), may hold values from -0.5 to 0.5
- bias_proj: float32 [128, 4], P(None, 'head'), may hold values from -0.5 to 0.5
- output_proj: float32 [128, 128], P('head'), may hold values from -4 to 4
- expand_proj: float32 [128, 512], P(None, 'head'), may hold values from -0.5 to 0.5
- reduce_proj: float32 [512, 128], P('head'), may hold values from -0.25 to 0.25
- distogram_proj: float32 [128, 64], replicated, may hold values from -0.5 to 0.5
- small_params: float32 [320], replicated, may hold values from 0.5 to 1.5
- momentum_head: float32 [128, 512], P(None, 'head'), may hold values from -2e-05 to 2e-05
- momentum_bias: float32 [128, 4], P(None, 'head'), may hold values from -2e-05 to 2e-05
- momentum_output: float32 [128, 128], P('head'), may hold values from -2e-05 to 2e-05
- momentum_expand: float32 [128, 512], P(None, 'head'), may hold values from -2e-05 to 2e-05
- momentum_reduce: float32 [512, 128], P('head'), may hold values from -2e-05 to 2e-05
- momentum_distogram: float32 [128, 64], replicated, may hold values from -2e-05 to 2e-05
- momentum_small: float32 [320], replicated, may hold values from -5e-05 to 5e-05
- average_head: float32 [128, 512], P(None, 'head'), may hold values from -0.5 to 0.5
- average_bias: float32 [128, 4], P(None, 'head'), may hold values from -0.5 to 0.5
- average_output: float32 [128, 128], P('head'), may hold values from -4 to 4
- average_expand: float32 [128, 512], P(None, 'head'), may hold values from -0.5 to 0.5
- average_reduce: float32 [512, 128], P('head'), may hold values from -0.25 to 0.25
- average_distogram: float32 [128, 64], replicated, may hold values from -0.5 to 0.5
- average_small: float32 [320], replicated, may hold values from 0.5 to 1.5
Outputs:
- total_loss: float32 [], replicated
- gradient_norm: float32 [], replicated
- head_weight: float32 [128, 512], P(None, 'head')
- bias_weight: float32 [128, 4], P(None, 'head')
- output_weight: float32 [128, 128], P('head')
- expand_weight: float32 [128, 512], P(None, 'head')
- reduce_weight: float32 [512, 128], P('head')
- distogram_weight: float32 [128, 64], replicated
- small_weight: float32 [320], replicated
- head_velocity: float32 [128, 512], P(None, 'head')
- bias_velocity: float32 [128, 4], P(None, 'head')
- output_velocity: float32 [128, 128], P('head')
- expand_velocity: float32 [128, 512], P(None, 'head')
- reduce_velocity: float32 [512, 128], P('head')
- distogram_velocity: float32 [128, 64], replicated
- small_velocity: float32 [320], replicated
- head_average: float32 [128, 512], P(None, 'head')
- bias_average: float32 [128, 4], P(None, 'head')
- output_average: float32 [128, 128], P('head')
- expand_average: float32 [128, 512], P(None, 'head')
- reduce_average: float32 [512, 128], P('head')
- distogram_average: float32 [128, 64], replicated
- small_average: float32 [320], replicated
The draws below stay inside these ranges and needn't reach their ends.
Inputs may be any that keep to these rules, and one draw needn't show every extreme that they name: `lengths`: item 0 has length 256; the others lie between min(60, 256) and 256.
All inputs are finite; a program needn't handle non-finite values.
Results may differ from the reference program's by a relative error of at most 0.0085.
Values may be sent and summed in bfloat16 or wider, within the bound.
A program may use at most 192 MiB of HBM per device.

```python
from functools import partial
import jax
import jax.numpy as jnp
from jax import lax

C = 128
H = 4
HD = 32
HID = 512
BINS = 64
L = 256
ITEMS = 2


def draw_lengths(key, part):
    others = jax.random.randint(key, (ITEMS - 1,), min(60, L), L + 1)
    return jnp.concatenate([jnp.full((1,), L, jnp.int32), others.astype(jnp.int32)])


def with_ends(entries, rng, least, largest):
    index_at = [jax.random.randint(jax.random.fold_in(rng, axis), (), 0, length) for axis, length in enumerate(entries.shape)]
    main_axis = entries.shape.index(max(entries.shape))
    next_to = index_at[:main_axis] + [(index_at[main_axis] + 1) % entries.shape[main_axis]] + index_at[main_axis + 1:]
    return entries.at[tuple(index_at)].set(least).at[tuple(next_to)].set(largest)


def block_levels(key, shape, split, low, high):
    def one(dim, blocks):
        draws = jax.random.uniform(jax.random.fold_in(jax.random.fold_in(key, 6), dim), (blocks,), jnp.float32, low / len(split), high / len(split))
        return jnp.repeat(jnp.exp(draws), shape[dim] // blocks).reshape((-1,) + (1,) * (len(shape) - dim - 1))

    level = one(*split[0])
    for cut in split[1:]:
        level = level * one(*cut)
    return level


def normal_values(own_key, extent, scale, limit, cuts=(), held_as=jnp.bfloat16):
    values = scale * jax.random.normal(own_key, extent, jnp.float32)
    if cuts:
        values = values * block_levels(own_key, extent, cuts, -0.22, 0.18)
    return jnp.clip(values, -limit, limit).astype(held_as)


def setup_inputs(seed: int = 0) -> dict:
    streams_of = jax.random.split(jax.random.key(seed), 25)
    return {
        "pair_input": normal_values(streams_of[0], (ITEMS, L, L, C), 1.0, 6.0, ((1, 8),)),
        "lengths": draw_lengths(jax.random.fold_in(streams_of[24], 71), 0),
        "distogram_bins": with_ends(jax.random.randint(streams_of[2], (ITEMS, L, L), 0, BINS), jax.random.fold_in(streams_of[2], 1), 0, BINS - 1).astype(jnp.int32),
        "head_proj": normal_values(streams_of[3], (C, 4 * H * HD), C ** -0.5, 0.5, ((1, 4),), jnp.float32),
        "bias_proj": normal_values(streams_of[4], (C, H), C ** -0.5, 0.5, ((1, 4),), jnp.float32),
        "output_proj": normal_values(streams_of[5], (H * HD, C), 2 ** -0.5, 4.0, ((0, 4),), jnp.float32),
        "expand_proj": normal_values(streams_of[6], (C, HID), C ** -0.5, 0.5, ((1, 4),), jnp.float32),
        "reduce_proj": normal_values(streams_of[7], (HID, C), HID ** -0.5, 0.25, ((0, 4),), jnp.float32),
        "distogram_proj": normal_values(streams_of[8], (C, BINS), C ** -0.5, 0.5, (), jnp.float32),
        "small_params": jnp.clip(jax.random.uniform(streams_of[9], (2 * C + BINS,), jnp.float32, 0.5, 1.5), 0.5, 1.5),
        "momentum_head": normal_values(streams_of[10], (C, 4 * H * HD), 0.000004, 1.9999999494757503e-05, ((1, 4),), jnp.float32),
        "momentum_bias": normal_values(streams_of[11], (C, H), 0.000004, 1.9999999494757503e-05, ((1, 4),), jnp.float32),
        "momentum_output": normal_values(streams_of[12], (H * HD, C), 0.000004, 1.9999999494757503e-05, ((0, 4),), jnp.float32),
        "momentum_expand": normal_values(streams_of[13], (C, HID), 0.000004, 1.9999999494757503e-05, ((1, 4),), jnp.float32),
        "momentum_reduce": normal_values(streams_of[14], (HID, C), 0.000004, 1.9999999494757503e-05, ((0, 4),), jnp.float32),
        "momentum_distogram": normal_values(streams_of[15], (C, BINS), 0.000004, 1.9999999494757503e-05, (), jnp.float32),
        "momentum_small": normal_values(streams_of[16], (2 * C + BINS,), 0.00001, 4.999999873689376e-05, (), jnp.float32),
        "average_head": normal_values(streams_of[17], (C, 4 * H * HD), C ** -0.5, 0.5, ((1, 4),), jnp.float32),
        "average_bias": normal_values(streams_of[18], (C, H), C ** -0.5, 0.5, ((1, 4),), jnp.float32),
        "average_output": normal_values(streams_of[19], (H * HD, C), 2 ** -0.5, 4.0, ((0, 4),), jnp.float32),
        "average_expand": normal_values(streams_of[20], (C, HID), C ** -0.5, 0.5, ((1, 4),), jnp.float32),
        "average_reduce": normal_values(streams_of[21], (HID, C), HID ** -0.5, 0.25, ((0, 4),), jnp.float32),
        "average_distogram": normal_values(streams_of[22], (C, BINS), C ** -0.5, 0.5, (), jnp.float32),
        "average_small": jnp.clip(jax.random.uniform(streams_of[23], (2 * C + BINS,), jnp.float32, 0.5, 1.5), 0.5, 1.5),
    }


@jax.custom_vjp
def low(v):
    return lax.optimization_barrier(v.astype(jnp.bfloat16)).astype(jnp.float32)

@jax.custom_vjp
def low_back(v):
    return v

def low_keep(v):
    return (low(v), None)

def low_pass(kept, grad):
    return (grad,)

def back_keep(v):
    return (v, None)

def back_low(kept, grad):
    return (low(grad),)
low.defvjp(low_keep, low_pass)
low_back.defvjp(back_keep, back_low)
EPS = 1e-05
NEG = -1000000000.0
MOMENTUM = 0.9
RATE = 20000.0
KEEP = 0.9
CLIP = 0.002

def project(values, weight):
    return jnp.einsum('...c,cd->...d', values, weight, precision=lax.Precision.HIGHEST)

def layer_norm(values, gain):
    center = values - lax.optimization_barrier(jnp.mean(values, -1, keepdims=True))
    spread = lax.optimization_barrier(jnp.mean(center * center, -1, keepdims=True))
    return center * lax.rsqrt(spread + EPS) * gain

def attend_row(bias_heads, penalty, row):
    query, key, value, gate = row
    scores = jnp.einsum('jhd,khd->hjk', query, key, precision=lax.Precision.HIGHEST) * HD ** (-0.5)
    scores = low_back(scores + bias_heads + penalty)
    probs = jax.nn.softmax(scores, -1)
    mixed = low_back(jnp.einsum('hjk,khd->jhd', low(probs), value, precision=lax.Precision.HIGHEST))
    return low(mixed * jax.nn.sigmoid(gate))

def item_loss(params, pair, length, target, count):
    head_w, bias_w, out_w, expand_w, reduce_w, dist_w, small = params
    head_w, bias_w, out_w = (low(head_w), low(bias_w), low(out_w))
    expand_w, reduce_w, dist_w = (low(expand_w), low(reduce_w), low(dist_w))
    gain_one = small[:C]
    gain_two = small[C:2 * C]
    dist_bias = small[2 * C:]
    live = (jnp.arange(L) < length).astype(jnp.float32)
    penalty = (1.0 - live) * NEG
    normed = low(layer_norm(pair, gain_one))
    proj = low_back(project(normed, head_w)).reshape(L, L, H, 4, HD)
    query = low(proj[:, :, :, 0])
    key = low(proj[:, :, :, 1])
    value = low(proj[:, :, :, 2])
    gate = proj[:, :, :, 3]
    pair_bias = low_back(low(project(normed, bias_w)))
    bias_heads = jnp.transpose(pair_bias, (2, 0, 1))
    row_fn = jax.checkpoint(partial(attend_row, bias_heads, penalty))
    gated = lax.map(row_fn, (query, key, value, gate))
    first = pair + low_back(project(gated.reshape(L, L, H * HD), out_w))
    widened = low(layer_norm(first, gain_two))
    pre = low_back(project(widened, expand_w))
    hidden = low(jnp.maximum(pre, 0.0))
    second = first + low_back(project(hidden, reduce_w))
    half = low_back(project(low(second), dist_w))
    logits = half + jnp.swapaxes(half, 0, 1) + dist_bias
    logp = jax.nn.log_softmax(logits, -1)
    picked = jnp.take_along_axis(logp, target[:, :, None].astype(jnp.int32), -1)[:, :, 0]
    weight = live[:, None] * live[None, :]
    return -jnp.sum(picked * weight) / count

def reference(pair_input, lengths, distogram_bins, head_proj, bias_proj, output_proj, expand_proj, reduce_proj, distogram_proj, small_params, momentum_head, momentum_bias, momentum_output, momentum_expand, momentum_reduce, momentum_distogram, momentum_small, average_head, average_bias, average_output, average_expand, average_reduce, average_distogram, average_small):
    params = (head_proj, bias_proj, output_proj, expand_proj, reduce_proj, distogram_proj, small_params)
    momenta = (momentum_head, momentum_bias, momentum_output, momentum_expand, momentum_reduce, momentum_distogram, momentum_small)
    averages = (average_head, average_bias, average_output, average_expand, average_reduce, average_distogram, average_small)
    size_f = lengths.astype(jnp.float32)
    count = jnp.sum(size_f * size_f)
    pair_f = pair_input.astype(jnp.float32)

    def total(weights):
        result = item_loss(weights, pair_f[0], lengths[0], distogram_bins[0], count)
        for item in range(1, ITEMS):
            result = result + item_loss(weights, pair_f[item], lengths[item], distogram_bins[item], count)
        return result
    loss, pull = jax.vjp(total, params)
    grads = pull(jnp.ones_like(loss))[0]
    squares = jnp.zeros((), jnp.float32)
    for grad in grads:
        squares = squares + jnp.sum(grad * grad)
    grad_norm = jnp.sqrt(squares)
    factor = CLIP / jnp.maximum(grad_norm, CLIP)
    new_w, new_m, new_a = ([], [], [])
    for weight, moment, average, grad in zip(params, momenta, averages, grads):
        clipped = grad * factor
        velocity = MOMENTUM * moment + clipped
        fresh = weight - RATE * (clipped + MOMENTUM * velocity)
        new_w.append(fresh)
        new_m.append(velocity)
        new_a.append(KEEP * average + (1.0 - KEEP) * fresh)
    return (loss, grad_norm, new_w[0], new_w[1], new_w[2], new_w[3], new_w[4], new_w[5], new_w[6], new_m[0], new_m[1], new_m[2], new_m[3], new_m[4], new_m[5], new_m[6], new_a[0], new_a[1], new_a[2], new_a[3], new_a[4], new_a[5], new_a[6])
```

```python
from functools import partial

import jax
import jax.numpy as jnp
from jax import lax
from jax.experimental import pallas as pl
from jax.experimental.pallas import tpu as pltpu
from jax.sharding import PartitionSpec as P

EPS = 1e-05
NEG = -1000000000.0
MOMENTUM = 0.9
RATE = 20000.0
KEEP = 0.9
CLIP = 0.002


def project(values, weight):
    return jnp.einsum("rjc,cd->rjd", values, weight, preferred_element_type=jnp.float32)


def layer_norm(values, gain):
    center = values - jnp.mean(values, -1, keepdims=True)
    spread = jnp.mean(center * center, -1, keepdims=True)
    return center * lax.rsqrt(spread + EPS) * gain


def norm_back(values, gain, grad_out):
    result, pull = jax.vjp(layer_norm, values, gain)
    return pull(grad_out)


def row_scores(query, key, bias_full, penalty, scale):
    scores = jnp.dot(query, key.T, preferred_element_type=jnp.float32) * scale
    return scores + bias_full.astype(jnp.float32) + penalty[None, :]


def forward_row(bias_full, penalty, scale, row):
    query, key, value, gate = row
    scores = row_scores(query, key, bias_full, penalty, scale)
    peak = jnp.max(scores, -1, keepdims=True)
    expo = jnp.exp(scores - peak)
    summed = jnp.sum(expo, -1, keepdims=True)
    probs = (expo / summed).astype(jnp.bfloat16)
    mixed = jnp.dot(probs, value, preferred_element_type=jnp.float32)
    gated = (mixed * jax.nn.sigmoid(gate)).astype(jnp.bfloat16)
    return (gated, (peak + jnp.log(summed))[:, 0])


def backward_row(bias_full, penalty, scale, carry, row):
    query, key, value, gate, dgated, logsum = row
    scores = row_scores(query, key, bias_full, penalty, scale)
    exact = jnp.exp(scores - logsum[:, None])
    probs = exact.astype(jnp.bfloat16)
    mixed = jnp.dot(probs, value, preferred_element_type=jnp.float32)
    sigma = jax.nn.sigmoid(gate)
    dmixed = (dgated * sigma).astype(jnp.bfloat16)
    dgate = dgated * mixed * sigma * (1.0 - sigma)
    dvalue = jnp.dot(probs.T, dmixed, preferred_element_type=jnp.float32)
    dprobs = jnp.dot(dmixed, value.T, preferred_element_type=jnp.float32)
    inner = jnp.sum(dprobs * exact, -1, keepdims=True)
    dscores = (exact * (dprobs - inner)).astype(jnp.bfloat16)
    dquery = jnp.dot(dscores, key, preferred_element_type=jnp.float32) * scale
    dkey = jnp.dot(dscores.T, query, preferred_element_type=jnp.float32) * scale
    grads = jnp.concatenate([dquery, dkey, dvalue, dgate], -1)
    return (carry + dscores.astype(jnp.float32), grads)


def advance(weight, moment, average, grad):
    velocity = MOMENTUM * moment + grad
    fresh = weight - RATE * (grad + MOMENTUM * velocity)
    return (fresh, velocity, KEEP * average + (1.0 - KEEP) * fresh)


def general_body(
    pair_input,
    lengths,
    distogram_bins,
    head_proj,
    bias_proj,
    output_proj,
    expand_proj,
    reduce_proj,
    distogram_proj,
    small_params,
    momentum_head,
    momentum_bias,
    momentum_output,
    momentum_expand,
    momentum_reduce,
    momentum_distogram,
    momentum_small,
    average_head,
    average_bias,
    average_output,
    average_expand,
    average_reduce,
    average_distogram,
    average_small,
):
    weights = (
        head_proj,
        bias_proj,
        output_proj,
        expand_proj,
        reduce_proj,
        distogram_proj,
        small_params,
    )
    momenta = (
        momentum_head,
        momentum_bias,
        momentum_output,
        momentum_expand,
        momentum_reduce,
        momentum_distogram,
        momentum_small,
    )
    averages = (
        average_head,
        average_bias,
        average_output,
        average_expand,
        average_reduce,
        average_distogram,
        average_small,
    )
    head_w, bias_w, out_w, expand_w, reduce_w, dist_w = [
        w.astype(jnp.bfloat16) for w in weights[:6]
    ]
    items, rows, length, channels = pair_input.shape
    width = output_proj.shape[0]
    scale = width ** (-0.5)
    gain_one = small_params[:channels]
    gain_two = small_params[channels : 2 * channels]
    dist_bias = small_params[2 * channels :]
    positions = jnp.arange(length)
    first_row = lax.axis_index("res") * rows
    size_f = lengths.astype(jnp.float32)
    count = jnp.sum(size_f * size_f)
    grads = [jnp.zeros_like(w) for w in weights]
    loss_part = jnp.zeros((), jnp.float32)
    for item in range(items):
        live = (positions < lengths[item]).astype(jnp.float32)
        penalty = (1.0 - live) * NEG
        row_live = lax.dynamic_slice_in_dim(live, first_row, rows)
        start = pair_input[item].astype(jnp.float32)
        normed = layer_norm(start, gain_one).astype(jnp.bfloat16)
        proj = project(normed, head_w)
        query = proj[..., :width].astype(jnp.bfloat16)
        key = proj[..., width : 2 * width].astype(jnp.bfloat16)
        value = proj[..., 2 * width : 3 * width].astype(jnp.bfloat16)
        gate = proj[..., 3 * width :]
        bias_local = project(normed, bias_w)[..., 0].astype(jnp.bfloat16)
        bias_full = lax.all_gather(bias_local, "res", axis=0, tiled=True)
        gated, logsum = lax.map(
            partial(forward_row, bias_full, penalty, scale), (query, key, value, gate)
        )
        first = start + lax.psum(project(gated, out_w), "head")
        widened = layer_norm(first, gain_two).astype(jnp.bfloat16)
        pre = project(widened, expand_w)
        hidden = jnp.maximum(pre, 0.0).astype(jnp.bfloat16)
        second = first + lax.psum(project(hidden, reduce_w).astype(jnp.bfloat16), "head").astype(
            jnp.float32
        )
        second_low = second.astype(jnp.bfloat16)
        half = project(second_low, dist_w)
        mirror = lax.all_to_all(
            half.astype(jnp.bfloat16), "res", split_axis=1, concat_axis=0, tiled=True
        ).astype(half.dtype)
        logits = half + jnp.transpose(mirror, (1, 0, 2)) + dist_bias
        peak = jnp.max(logits, -1, keepdims=True)
        logp = logits - peak - jnp.log(jnp.sum(jnp.exp(logits - peak), -1, keepdims=True))
        onehot = (distogram_bins[item][:, :, None] == jnp.arange(logits.shape[2])).astype(
            jnp.float32
        )
        weight = (row_live[:, None] * live[None, :])[:, :, None]
        loss_part = loss_part - jnp.sum(logp * onehot * weight) / count
        dlogits = (jnp.exp(logp) - onehot) * weight / count
        back = lax.all_to_all(
            dlogits.astype(jnp.bfloat16), "res", split_axis=1, concat_axis=0, tiled=True
        ).astype(dlogits.dtype)
        dhalf = (dlogits + jnp.transpose(back, (1, 0, 2))).astype(jnp.bfloat16)
        grads[5] = grads[5] + jnp.einsum(
            "rjc,rjb->cb", second_low, dhalf, preferred_element_type=jnp.float32
        )
        dist_grad = jnp.sum(dlogits, (0, 1))
        dsecond = jnp.einsum("rjb,cb->rjc", dhalf, dist_w, preferred_element_type=jnp.float32)
        dtrans = dsecond.astype(jnp.bfloat16)
        grads[4] = grads[4] + jnp.einsum(
            "rjh,rjc->hc", hidden, dtrans, preferred_element_type=jnp.float32
        )
        dhidden = jnp.einsum("rjc,hc->rjh", dtrans, reduce_w, preferred_element_type=jnp.float32)
        dpre = jnp.where(pre > 0, dhidden, 0.0).astype(jnp.bfloat16)
        grads[3] = grads[3] + jnp.einsum(
            "rjc,rjh->ch", widened, dpre, preferred_element_type=jnp.float32
        )
        dwidened = lax.psum(
            jnp.einsum("rjh,ch->rjc", dpre, expand_w, preferred_element_type=jnp.float32).astype(
                jnp.bfloat16
            ),
            "head",
        ).astype(jnp.float32)
        dfirst_norm, gain_two_grad = norm_back(first, gain_two, dwidened)
        dout = (dsecond + dfirst_norm).astype(jnp.bfloat16)
        grads[2] = grads[2] + jnp.einsum(
            "rjd,rjc->dc", gated, dout, preferred_element_type=jnp.float32
        )
        dgated = jnp.einsum("rjc,dc->rjd", dout, out_w, preferred_element_type=jnp.float32)
        bias_terms, dproj = lax.scan(
            partial(backward_row, bias_full, penalty, scale),
            jnp.zeros((length, length), jnp.float32),
            (query, key, value, gate, dgated, logsum),
        )
        dproj = dproj.astype(jnp.bfloat16)
        dbias = lax.psum_scatter(bias_terms, "res", scatter_dimension=0, tiled=True).astype(
            jnp.bfloat16
        )
        grads[0] = grads[0] + jnp.einsum(
            "rjc,rjd->cd", normed, dproj, preferred_element_type=jnp.float32
        )
        grads[1] = (
            grads[1]
            + jnp.einsum("rjc,rj->c", normed, dbias, preferred_element_type=jnp.float32)[:, None]
        )
        dnormed_part = jnp.einsum("rjd,cd->rjc", dproj, head_w, preferred_element_type=jnp.float32)
        dnormed_part = dnormed_part + dbias.astype(jnp.float32)[:, :, None] * bias_w[:, 0].astype(
            jnp.float32
        )
        dnormed = lax.psum(dnormed_part.astype(jnp.bfloat16), "head").astype(jnp.float32)
        unused, gain_one_grad = norm_back(start, gain_one, dnormed)
        grads[6] = grads[6] + jnp.concatenate([gain_one_grad, gain_two_grad, dist_grad])
    summed = lax.psum(
        (grads[0], grads[1], grads[2], grads[3], grads[4], grads[5], grads[6], loss_part), "res"
    )
    total_grads = summed[:7]
    total_loss = summed[7]
    owned = jnp.zeros((), jnp.float32)
    for grad in total_grads[:5]:
        owned = owned + jnp.sum(grad * grad)
    shared = jnp.sum(total_grads[5] * total_grads[5]) + jnp.sum(total_grads[6] * total_grads[6])
    grad_norm = jnp.sqrt(shared + lax.psum(owned, "head"))
    factor = CLIP / jnp.maximum(grad_norm, CLIP)
    results = [
        advance(w, m, a, g * factor) for w, m, a, g in zip(weights, momenta, averages, total_grads)
    ]
    new_w = [r[0] for r in results]
    new_m = [r[1] for r in results]
    new_a = [r[2] for r in results]
    return (
        total_loss,
        grad_norm,
        new_w[0],
        new_w[1],
        new_w[2],
        new_w[3],
        new_w[4],
        new_w[5],
        new_w[6],
        new_m[0],
        new_m[1],
        new_m[2],
        new_m[3],
        new_m[4],
        new_m[5],
        new_m[6],
        new_a[0],
        new_a[1],
        new_a[2],
        new_a[3],
        new_a[4],
        new_a[5],
        new_a[6],
    )


NT = (((1,), (1,)), ((), ()))
NN = (((1,), (0,)), ((), ()))
F32 = jnp.float32
LOW = jnp.bfloat16
LOG2E = 1.4426950408889634


def dot(left, right, dims=NN):
    return lax.dot_general(left, right, dims, preferred_element_type=F32)


def iota(shape, dim):
    return lax.broadcasted_iota(jnp.int32, shape, dim)


def eye(size):
    return (iota((size, size), 0) == iota((size, size), 1)).astype(F32).astype(LOW)


def sigmoid(x):
    return 0.5 * jnp.tanh(0.5 * x) + 0.5


def step_kernel(groups, heads, *refs):
    (
        pair, lengths, bins, head_w, bias_w, out_w, exp_w, red_w, dist_w, small,
        o_head, o_block, o_dist, o_small,
        normed, tok, qkv, sig, expo, mixed, rinv,
        wc, wt, we, wet, wr, wrt, wo, wot, wd, wdt, gain_col, dist_col,
        bias_f, bias_send, bias_all, bias_t, bins_low, bins_in, bins_own, bins_t,
        gated, gall, xhat, rstd, widened, hidden, slow, halves, pack_f, half_send, half_in, mirror,
        dpre_s, dg_send, dg_in, g_out, g_red, g_exp, g_dist, loss_acc, dist_acc,
        block_send, block_in, block_sum,
        db_acc, db_send, db_in, g_head, g_bias, head_in, head_sum, small_own, small_in, card, card_in,
        sem_bias_s, sem_bias_r, sem_bins_s, sem_bins_r, sem_w_s, sem_w_r,
        sem_gat_s, sem_gat_r, sem_half_s, sem_half_r, sem_dg_s, sem_dg_r,
        sem_blk_s, sem_blk_r, sem_gath_s, sem_gath_r, sem_db_s, sem_db_r,
        sem_head_s, sem_head_r, sem_small_s, sem_small_r, sem_card_s, sem_card_r, sem_fin_s, sem_fin_r,
    ) = refs
    items, rows, length, chan = pair.shape
    width = out_w.shape[0]
    nbins = dist_w.shape[1]
    unit = exp_w.shape[1]
    own = rows // heads
    half_own = own // 2
    total = groups * heads
    scale = width ** (-0.5)
    my_r = lax.axis_index("res")
    my_h = lax.axis_index("head")
    me = my_r * heads + my_h

    def device(r, h):
        return {"res": r, "head": h}

    def send(src, dst, ssem, rsem, r, h):
        return pltpu.make_async_remote_copy(
            src_ref=src, dst_ref=dst, send_sem=ssem, recv_sem=rsem,
            device_id=device(r, h), device_id_type=pl.DeviceIdType.MESH,
        )

    def res_peer(o):
        return lax.rem(my_r + o, groups)

    def head_peer(o):
        return lax.rem(my_h + o, heads)

    def any_peer(o):
        d = lax.rem(me + o, total)
        return d, d // heads, lax.rem(d, heads)

    def each(count, make, act):
        def one(o, carry):
            act(make(o))
            return carry
        lax.fori_loop(1, count, one, 0)

    start = lambda c: c.start()
    wait_in = lambda c: c.wait_recv()
    wait_out = lambda c: c.wait_send()

    barrier = pltpu.get_barrier_semaphore()

    def greet(o, carry):
        d, r, h = any_peer(o)
        pl.semaphore_signal(barrier, inc=1, device_id=device(r, h), device_id_type=pl.DeviceIdType.MESH)
        return carry

    lax.fori_loop(1, total, greet, 0)

    hw = head_w[...]
    hw_low = hw.astype(LOW)
    wc[0 : 4 * width] = jnp.transpose(hw).astype(LOW)
    brow = bias_w[...].astype(LOW).astype(F32)
    wc[4 * width :] = jnp.where(iota((16, chan), 0) == 0, brow, 0.0).astype(LOW)
    src_col = iota((4 * width, 4 * width), 0)
    dst_col = iota((4 * width, 4 * width), 1)
    want = jnp.where(
        dst_col < width, dst_col + width, jnp.where(dst_col < 3 * width, dst_col, -1)
    )
    wt[...] = dot(hw_low, (src_col == want).astype(F32).astype(LOW)).astype(LOW)
    ident = eye(chan)
    ident_l = eye(length)
    gain_one = small[:, 0:chan]
    gain_two = small[:, chan : 2 * chan]
    gain_col[...] = jnp.transpose(jnp.broadcast_to(gain_two, (chan, chan)))
    dist_col[...] = jnp.transpose(jnp.broadcast_to(small[:, 2 * chan : 3 * chan], (chan, chan)))[:nbins]
    we[:, pl.ds(pl.multiple_of(my_h * unit, unit), unit)] = exp_w[...].astype(LOW)
    wr[pl.ds(pl.multiple_of(my_h * unit, unit), unit), :] = red_w[...].astype(LOW)
    wo[pl.ds(pl.multiple_of(my_h * width, width), width), :] = out_w[...].astype(LOW)
    wd[...] = dist_w[...].astype(LOW)
    wdt[...] = dot(eye(nbins), wd[...], NT).astype(LOW)
    bins_low[...] = bins[...].astype(F32).astype(LOW)
    bins_own[...] = bins[:, pl.ds(pl.multiple_of(my_h * own, own), own), :].astype(F32)
    one_lane = (iota((1, 4 * width), 1) >= 3 * width).astype(F32)

    def before(item):
        def row(r, carry):
            x = pair[item, r].astype(F32)
            center = x - jnp.mean(x, -1, keepdims=True)
            spread = jnp.mean(center * center, -1, keepdims=True)
            low = (center * lax.rsqrt(spread + EPS) * gain_one).astype(LOW)
            normed[item, r] = low
            ch = dot(wc[...], low, NT)
            qkv[item, r] = ch[: 3 * width].astype(LOW)
            sig[item, r] = sigmoid(ch[3 * width : 4 * width])
            bias_f[pl.ds(r, 1), :] = ch[4 * width : 4 * width + 1]
            tok[item, r] = (dot(low, wt[...]) + one_lane).astype(LOW)
            return carry
        lax.fori_loop(0, rows, row, 0, unroll=2)
        bias_send[item] = bias_f[...].astype(LOW)
        bias_all[item, pl.ds(pl.multiple_of(my_r * rows, rows), rows), :] = bias_f[...].astype(LOW)

    def bias_copy(item):
        def make(o):
            return send(
                bias_send.at[item],
                bias_all.at[item, pl.ds(pl.multiple_of(my_r * rows, rows), rows), :],
                sem_bias_s.at[item, o], sem_bias_r.at[item, o], res_peer(o), my_h,
            )
        return make

    def bins_block(r):
        return pl.ds(pl.multiple_of((r * rows) // 128 * 128, 128), 128)

    def bins_copy(o):
        return send(
            bins_low.at[:, :, bins_block(res_peer(o))], bins_in.at[my_r],
            sem_bins_s.at[o], sem_bins_r.at[o], res_peer(o), my_h,
        )

    def we_copy(o):
        at = (slice(None), pl.ds(pl.multiple_of(my_h * unit, unit), unit))
        return send(we.at[at], we.at[at], sem_w_s.at[0, o], sem_w_r.at[0, o], my_r, head_peer(o))

    def wr_copy(o):
        at = pl.ds(pl.multiple_of(my_h * unit, unit), unit)
        return send(wr.at[at], wr.at[at], sem_w_s.at[1, o], sem_w_r.at[1, o], my_r, head_peer(o))

    def wo_copy(o):
        at = pl.ds(pl.multiple_of(my_h * width, width), width)
        return send(wo.at[at], wo.at[at], sem_w_s.at[2, o], sem_w_r.at[2, o], my_r, head_peer(o))

    def gated_copy(item):
        def make(o):
            p = head_peer(o)
            return send(
                gated.at[item, pl.ds(p * own, own)],
                gall.at[item, :, pl.ds(pl.multiple_of(my_h * width, width), width), :],
                sem_gat_s.at[item, o], sem_gat_r.at[item, o], my_r, p,
            )
        return make

    def attend(item):
        live = iota((length, length), 0) < lengths[item]
        bt = dot(ident_l, bias_all[item], NT) * LOG2E
        bias_t[...] = bt + jnp.where(live, 0.0, NEG * LOG2E)

        def row(r):
            q = qkv[item, r, 0:width].astype(F32) * (scale * LOG2E)
            hi = q.astype(LOW)
            lo = (q - hi.astype(F32)).astype(LOW)
            rhs = jnp.concatenate([hi, lo, jnp.zeros((2 * width, length), LOW)], 0)
            s = dot(tok[item, r], rhs) + bias_t[...]
            e = jnp.exp2(s - jnp.max(s, 0, keepdims=True)).astype(LOW)
            expo[item, r] = e
            lhs = jnp.concatenate(
                [qkv[item, r, 2 * width : 3 * width], jnp.ones((16, length), LOW)], 0
            )
            o = dot(lhs, e)
            inv = 1.0 / o[width : width + 1]
            rinv[item, pl.ds(r, 1), :] = inv
            m = o[:width] * inv
            mixed[item, r] = m
            gated[item, r] = (m * sig[item, r]).astype(LOW)

        def chunk(o, carry):
            p = head_peer(o)

            def one(k, c):
                row(p * own + k)
                return c
            lax.fori_loop(0, own, one, 0, unroll=4)

            @pl.when(o < heads)
            def _():
                gated_copy(item)(o).start()
            return carry
        lax.fori_loop(1, heads + 1, chunk, 0)
        gall[item, :, pl.ds(pl.multiple_of(my_h * width, width), width), :] = gated[
            item, pl.ds(my_h * own, own)
        ]

    def pair_of(ref, item, t):
        return jnp.concatenate([ref[item, t], ref[item, t + half_own]], 1)

    sel_row = iota((total * half_own, length), 0)
    sel_col = iota((total * half_own, length), 1)
    sel_at = sel_row // half_own * own + lax.rem(sel_row, half_own)
    sel_a = (sel_col == sel_at).astype(F32).astype(LOW)
    sel_b = (sel_col == sel_at + half_own).astype(F32).astype(LOW)

    def forward(item):
        def tile(t, carry):
            g2 = pair_of(gall, item, t)
            base = my_h * own + t
            first = jnp.concatenate(
                [dot(ident, pair[item, base], NT), dot(ident, pair[item, base + half_own], NT)], 1
            ) + dot(wot[...], g2)
            center = first - jnp.mean(first, 0, keepdims=True)
            rs = lax.rsqrt(jnp.mean(center * center, 0, keepdims=True) + EPS)
            xh = center * rs
            xhat[item, t] = xh
            rstd[item, t] = jnp.broadcast_to(rs, (8, 2 * length))
            gc = jnp.concatenate([gain_col[...]] * (2 * length // chan), 1)
            wid = (xh * gc).astype(LOW)
            widened[item, t] = wid
            for b in range(heads):
                hidden[item, t, b * unit : (b + 1) * unit] = jnp.maximum(
                    dot(wet[b * unit : (b + 1) * unit], wid), 0.0
                ).astype(LOW)
            second = (first + dot(wrt[...], hidden[item, t])).astype(LOW)
            slow[item, t] = second
            half = dot(wdt[...], second)
            zero = jnp.zeros((nbins, length), LOW)
            for k in range(2):
                part = half[:, k * length : (k + 1) * length]
                halves[item, t + k * half_own] = part
                part = part.astype(LOW)
                packed = dot(sel_a, jnp.concatenate([part, zero], 0), NT) + dot(
                    sel_b, jnp.concatenate([zero, part], 0), NT
                )
                pack_f[pl.ds(t + k * half_own, total * half_own, own), :] = packed
            return carry
        lax.fori_loop(0, half_own, tile, 0)
        half_send[item] = pack_f[...].reshape(half_send.shape[1:]).astype(LOW)
        half_in[item, me] = half_send[item, me]

    def half_copy(item):
        def make(o):
            d, r, h = any_peer(o)
            return send(
                half_send.at[item, d], half_in.at[item, me],
                sem_half_s.at[item, o], sem_half_r.at[item, o], r, h,
            )
        return make

    size_sum = jnp.zeros((1, length), F32)
    for item in range(items):
        size = lengths[item]
        size_sum = size_sum + (jnp.zeros((1, length), jnp.int32) + size * size).astype(F32)

    def backward(item):
        mirror[...] = half_in[item].astype(F32)
        live = (iota((1, length), 1) < lengths[item]).astype(F32) / size_sum
        levels = iota((nbins, length), 0).astype(F32)[None]

        def tile(t, carry):
            flip = mirror[:, pl.ds(pl.multiple_of(t * own, own), own), :].reshape(length, 2 * nbins)
            flip = dot(eye(2 * nbins), flip.astype(LOW), NT)
            here = jnp.concatenate([halves[item, t], halves[item, t + half_own]], 0)
            logits = (here + flip).reshape(2, nbins, length) + jnp.concatenate(
                [dist_col[...]] * (length // chan), 1
            )[None]
            peak = jnp.max(logits, 1, keepdims=True)
            ex = jnp.exp(logits - peak)
            tot = jnp.sum(ex, 1, keepdims=True)
            prob = ex * (1.0 / tot)

            def two(ref):
                return jnp.concatenate(
                    [ref[item, pl.ds(t, 1), :][None], ref[item, pl.ds(t + half_own, 1), :][None]], 0
                )
            hot = (two(bins_own) == levels).astype(F32)
            hot_t = (two(bins_t) == levels).astype(F32)
            at = me * own + t + iota((2, 1, length), 0) * half_own
            weight = jnp.where(at < lengths[item], 1.0, 0.0) * live[None]
            picked = jnp.sum(hot * logits, 1, keepdims=True)
            lost = weight * (peak + jnp.log(tot) - picked)
            loss_acc[...] += lost[0] + lost[1]
            short = prob - hot
            dl = short * weight
            dist_acc[...] += dl[0] + dl[1]
            dh = ((short + prob - hot_t) * weight).astype(LOW)
            dh2 = jnp.concatenate([dh[0], dh[1]], 1)
            low2 = slow[item, t]
            g_dist[...] += dot(dh2, low2, NT)
            dsec = dot(wd[...], dh2)
            dtr = dsec.astype(LOW)
            wid = widened[item, t]
            for b in range(heads):
                at_b = slice(b * unit, (b + 1) * unit)
                hid = hidden[item, t, at_b]
                dp = jnp.where(hid.astype(F32) > 0.0, dot(wr[at_b], dtr), 0.0).astype(LOW)
                g_red[at_b] += dot(hid, dtr, NT)
                g_exp[at_b] += dot(dp, wid, NT)
                dpre_s[at_b] = dp
            gc = jnp.concatenate([gain_col[...]] * (2 * length // chan), 1)
            dxh = dot(we[...], dpre_s[...]) * gc
            xh = xhat[item, t]
            m1 = jnp.mean(dxh, 0, keepdims=True)
            m2 = jnp.mean(dxh * xh, 0, keepdims=True)
            dout = (dsec + rstd[item, t, 0:1] * (dxh - m1 - xh * m2)).astype(LOW)
            g_out[...] += dot(pair_of(gall, item, t), dout, NT)
            dg = dot(wo[...], dout).astype(LOW)
            for h in range(heads):
                for k in range(2):
                    dg_send[item, h, t + k * half_own] = dg[
                        h * width : (h + 1) * width, k * length : (k + 1) * length
                    ]
            return carry
        lax.fori_loop(0, half_own, tile, 0)
        dg_in[item, pl.ds(my_h * own, own)] = dg_send[item, my_h]

    def dg_copy(item):
        def make(o):
            p = head_peer(o)
            return send(
                dg_send.at[item, p], dg_in.at[item, pl.ds(my_h * own, own)],
                sem_dg_s.at[item, o], sem_dg_r.at[item, o], my_r, p,
            )
        return make

    def attend_back(item):
        db_acc[...] = jnp.zeros_like(db_acc)
        tail_row = iota((16, length), 0)

        def row(r, carry):
            s = sig[item, r]
            m = mixed[item, r]
            dg = dg_in[item, r].astype(F32)
            dm = (dg * s * rinv[item, pl.ds(r, 1), :]).astype(LOW)
            inner = -jnp.sum(dm.astype(F32) * m, 0, keepdims=True)
            hi = inner.astype(LOW).astype(F32)
            lo = inner - hi
            tail = jnp.where(tail_row == 0, hi, jnp.where(tail_row == 1, lo, 0.0)).astype(LOW)
            rhs = jnp.concatenate(
                [jnp.zeros((2 * width, length), LOW), dm, tail, jnp.zeros((width - 16, length), LOW)], 0
            )
            e = expo[item, r]
            ds = e.astype(F32) * dot(tok[item, r], rhs)
            db_acc[...] += ds
            ds = ds.astype(LOW)
            dq = dot(qkv[item, r, width : 2 * width], ds) * scale
            dk = dot(qkv[item, r, 0:width], ds, NT) * scale
            dv = dot(dm, e, NT)
            dproj = jnp.concatenate([dq, dk, dv, dg * m * s * (1.0 - s)], 0).astype(LOW)
            g_head[...] += dot(dproj, normed[item, r])
            return carry
        lax.fori_loop(0, rows, row, 0, unroll=4)
        db_send[item] = dot(ident_l, db_acc[...].astype(LOW), NT).astype(LOW)
        db_in[item, my_r] = db_send[item, pl.ds(pl.multiple_of(my_r * rows, rows), rows), :]

    def db_copy(item):
        def make(o):
            p = res_peer(o)
            return send(
                db_send.at[item, pl.ds(pl.multiple_of(p * rows, rows), rows), :], db_in.at[item, my_r],
                sem_db_s.at[item, o], sem_db_r.at[item, o], p, my_h,
            )
        return make

    def bias_back(item):
        db = db_in[item, 0].astype(F32)
        for s in range(1, groups):
            db = db + db_in[item, s].astype(F32)
        db = db.astype(LOW).astype(F32)
        at = iota((rows, length), 0)

        def row(r, acc):
            return acc + dot(jnp.where(at == r, db, 0.0).astype(LOW), normed[item, r])
        acc = lax.fori_loop(0, rows, row, jnp.zeros((rows, chan), F32), unroll=4)
        g_bias[...] += jnp.sum(acc, 0, keepdims=True)

    def block_copy(o):
        d, r, h = any_peer(o)
        return send(block_send.at[d], block_in.at[me], sem_blk_s.at[o], sem_blk_r.at[o], r, h)

    def gather_copy(o):
        return send(block_sum, o_block.at[my_r], sem_gath_s.at[o], sem_gath_r.at[o], res_peer(o), my_h)

    ru, rw, rb = unit // groups, width // groups, nbins // total

    def block_make():
        for r in range(groups):
            for h in range(heads):
                d = r * heads + h
                at = h * unit + r * ru
                block_send[d, 0:ru] = g_red[at : at + ru]
                block_send[d, ru : 2 * ru] = g_exp[at : at + ru]
                at = h * width + r * rw
                block_send[d, 2 * ru : 2 * ru + rw] = g_out[at : at + rw]
                block_send[d, 2 * ru + rw : 2 * ru + rw + rb] = g_dist[d * rb : (d + 1) * rb]
                block_send[d, 2 * ru + rw + rb :] = jnp.zeros((8 - rw - rb, chan), F32)
        block_in[me] = block_send[me]

    def block_add():
        acc = block_in[0]
        for d in range(1, total):
            acc = acc + block_in[d]
        block_sum[...] = acc
        o_block[my_r] = acc

    def head_copy(o):
        p = res_peer(o)
        return send(
            g_head.at[pl.ds(pl.multiple_of(p * (4 * width // groups), 4 * width // groups), 4 * width // groups), :],
            head_in.at[my_r], sem_head_s.at[o], sem_head_r.at[o], p, my_h,
        )

    def small_copy(o):
        return send(small_own, small_in.at[my_r], sem_small_s.at[o], sem_small_r.at[o], res_peer(o), my_h)

    def card_copy(o):
        d, r, h = any_peer(o)
        return send(card, card_in.at[me], sem_card_s.at[o], sem_card_r.at[o], r, h)

    def fin_copy(o):
        return send(head_sum, o_head.at[my_r], sem_fin_s.at[o], sem_fin_r.at[o], res_peer(o), my_h)

    for ref in (g_out, g_red, g_exp, g_dist, loss_acc, dist_acc, g_head, g_bias):
        ref[...] = jnp.zeros_like(ref)
    before(0)
    pl.semaphore_wait(barrier, total - 1)
    each(groups, bias_copy(0), start)
    for make in (we_copy, wr_copy, wo_copy):
        each(heads, make, start)
    for item in range(1, items):
        before(item)
        each(groups, bias_copy(item), start)
    each(groups, bins_copy, start)
    bins_in[my_r] = bins_low[:, :, bins_block(my_r)]
    for item in range(items):
        each(groups, bias_copy(item), wait_in)
        attend(item)
    for make in (we_copy, wr_copy, wo_copy):
        each(heads, make, wait_in)
    for b in range(heads):
        at = slice(b * unit, (b + 1) * unit)
        wet[at] = dot(ident, we[:, at], NT).astype(LOW)
        wrt[:, at] = dot(ident, wr[at], NT).astype(LOW)
    wot[...] = dot(ident, wo[...], NT).astype(LOW)
    for item in range(items):
        each(heads, gated_copy(item), wait_in)
        forward(item)
        each(total, half_copy(item), start)
    each(groups, bins_copy, wait_in)
    lane = my_r * rows + my_h * own - (my_r * rows) // 128 * 128
    pick = (iota((16, 128), 1) == iota((16, 128), 0) + lane).astype(F32).astype(LOW)
    for item in range(items):
        bins_t[item] = dot(pick, bins_in[:, item].reshape(groups * rows, 128), NT)
    for item in range(items):
        each(total, half_copy(item), wait_in)
        backward(item)
        each(heads, dg_copy(item), start)
    block_make()
    each(total, block_copy, start)
    for item in range(items):
        each(heads, dg_copy(item), wait_in)
        attend_back(item)
        each(groups, db_copy(item), start)
        if item == 0:
            each(total, block_copy, wait_in)
            block_add()
            each(groups, gather_copy, start)
    each(groups, head_copy, start)
    sh = 4 * width // groups
    head_in[my_r] = g_head[pl.ds(pl.multiple_of(my_r * sh, sh), sh), :]
    for item in range(items):
        each(groups, db_copy(item), wait_in)
        bias_back(item)
    gb = g_bias[...]
    up_one = jnp.sum(wc[0 : 4 * width].astype(F32) * g_head[...], 0, keepdims=True) + brow * gb
    up_two = jnp.sum(wet[...].astype(F32) * g_exp[...], 0, keepdims=True)
    dacc = dist_acc[:, 0:chan]
    lacc = loss_acc[:, 0:chan]
    for k in range(1, length // chan):
        dacc = dacc + dist_acc[:, k * chan : (k + 1) * chan]
        lacc = lacc + loss_acc[:, k * chan : (k + 1) * chan]
    dacc = jnp.transpose(jnp.concatenate([dacc, jnp.zeros((chan - nbins, chan), F32)], 0))
    small_own[0:1] = gb
    small_own[1:2] = up_one / gain_one
    small_own[2:3] = up_two / gain_two
    small_own[3:4] = jnp.sum(dacc, 0, keepdims=True)
    small_own[4:5] = lacc
    small_own[5:8] = jnp.zeros((3, chan), F32)
    small_in[my_r] = small_own[...]
    each(groups, small_copy, start)
    each(groups, head_copy, wait_in)
    acc = head_in[0]
    for s in range(1, groups):
        acc = acc + head_in[s]
    head_sum[...] = acc
    o_head[my_r] = acc
    each(groups, fin_copy, start)
    each(groups, small_copy, wait_in)
    tiny = small_in[0]
    for s in range(1, groups):
        tiny = tiny + small_in[s]
    blocks = block_sum[...]
    squares = jnp.sum(acc * acc, 0, keepdims=True) + jnp.sum(blocks * blocks, 0, keepdims=True)
    card[...] = tiny
    card[5:6] = squares
    card[6:8] = blocks[2 * ru + rw : 2 * ru + rw + rb]
    card_in[me] = card[...]
    each(total, card_copy, start)
    each(total, card_copy, wait_in)
    every = card_in[0]
    for d in range(1, total):
        every = every + card_in[d]
    mine = [card_in[my_r * heads + h] for h in range(heads)]
    summed = mine[0]
    bias_sq = mine[0] * mine[0]
    for h in range(1, heads):
        summed = summed + mine[h]
        bias_sq = bias_sq + mine[h] * mine[h]
    norm_sq = every[5:6] + bias_sq[0:1]
    for k in (1, 2, 3):
        norm_sq = norm_sq + summed[k : k + 1] * summed[k : k + 1]
    norm = jnp.sqrt(jnp.sum(norm_sq, -1, keepdims=True))
    o_small[...] = summed
    o_small[0:1] = card[0:1]
    o_small[4:5] = jnp.broadcast_to(jnp.sum(summed[4:5], -1, keepdims=True), (1, chan))
    o_small[5:6] = jnp.broadcast_to(norm, (1, chan))
    o_small[6:7] = jnp.broadcast_to(CLIP / jnp.maximum(norm, CLIP), (1, chan))
    for d in range(total):
        o_dist[d * rb : (d + 1) * rb] = card_in[d, 6 : 6 + rb]
    each(groups, gather_copy, wait_in)
    each(groups, fin_copy, wait_in)
    for item in range(items):
        each(groups, bias_copy(item), wait_out)
        each(heads, gated_copy(item), wait_out)
        each(total, half_copy(item), wait_out)
        each(heads, dg_copy(item), wait_out)
        each(groups, db_copy(item), wait_out)
    for make in (we_copy, wr_copy, wo_copy):
        each(heads, make, wait_out)
    for make in (bins_copy, gather_copy, head_copy, small_copy, fin_copy):
        each(groups, make, wait_out)
    for make in (block_copy, card_copy):
        each(total, make, wait_out)


def update_kernel(groups, *refs):
    g_head, g_block, g_dist, g_small = refs[:4]
    weights, momenta, averages = refs[4:11], refs[11:18], refs[18:25]
    loss, norm = refs[25:27]
    new_w, new_m, new_a = refs[27:34], refs[34:41], refs[41:48]
    loss[...] = g_small[4:5, 0:1]
    norm[...] = g_small[5:6, 0:1]
    factor = g_small[6:7, 0:1]
    unit = weights[4].shape[0]
    width = weights[2].shape[0]
    ru, rw = unit // groups, width // groups
    chan = g_small.shape[1]

    def put(k, grad, at=(slice(None), slice(None))):
        fresh, velocity, average = advance(
            weights[k][at], momenta[k][at], averages[k][at], grad * factor
        )
        new_w[k][at] = fresh
        new_m[k][at] = velocity
        new_a[k][at] = average

    put(0, jnp.transpose(g_head[...].reshape(weights[0].shape[1], chan)))
    put(1, g_small[0:1])
    put(3, jnp.transpose(g_block[:, ru : 2 * ru].reshape(unit, chan)))
    put(4, g_block[:, 0:ru].reshape(unit, chan))
    for r in range(groups):
        put(2, g_block[r, 2 * ru : 2 * ru + rw], (slice(r * rw, (r + 1) * rw), slice(None)))
    nbins = weights[5].shape[1]
    put(5, jnp.transpose(jnp.concatenate([g_dist[...], jnp.zeros((chan - nbins, chan), F32)], 0))[:, :nbins])
    put(6, g_small[1:2], (slice(None), slice(0, chan)))
    put(6, g_small[2:3], (slice(None), slice(chan, 2 * chan)))
    put(6, g_small[3:4, 0:nbins], (slice(None), slice(2 * chan, 2 * chan + nbins)))


def fused_body(groups, heads, *args):
    pair_input, lengths, distogram_bins = args[:3]
    weights, momenta, averages = list(args[3:10]), list(args[10:17]), list(args[17:24])
    items, rows, length, chan = pair_input.shape
    width = weights[2].shape[0]
    unit = weights[3].shape[1]
    nbins = weights[5].shape[1]
    own, total = rows // heads, groups * heads
    half_own = own // 2
    for group in (weights, momenta, averages):
        group[1] = group[1].reshape(1, chan)
        group[6] = group[6].reshape(1, -1)
    small = jnp.pad(weights[6], ((0, 0), (0, 3 * chan - weights[6].shape[1])))
    vmem = pl.BlockSpec(memory_space=pltpu.VMEM)
    block_rows = 2 * (unit // groups) + 8
    sh = 4 * width // groups
    V = pltpu.VMEM
    dma = pltpu.SemaphoreType.DMA
    scratch = [
        V((items, rows, length, chan), LOW),
        V((items, rows, length, 4 * width), LOW),
        V((items, rows, 3 * width, length), LOW),
        V((items, rows, width, length), F32),
        V((items, rows, length, length), LOW),
        V((items, rows, width, length), F32),
        V((items, rows, length), F32),
        V((4 * width + 16, chan), LOW),
        V((chan, 4 * width), LOW),
        V((chan, heads * unit), LOW),
        V((heads * unit, chan), LOW),
        V((heads * unit, chan), LOW),
        V((chan, heads * unit), LOW),
        V((heads * width, chan), LOW),
        V((chan, heads * width), LOW),
        V((chan, nbins), LOW),
        V((nbins, chan), LOW),
        V((chan, chan), F32),
        V((nbins, chan), F32),
        V((rows, length), F32),
        V((items, rows, length), LOW),
        V((items, length, length), LOW),
        V((length, length), F32),
        V((items, rows, length), LOW),
        V((groups, items, rows, 128), LOW),
        V((items, own, length), F32),
        V((items, 16, length), F32),
        V((items, rows, width, length), LOW),
        V((items, own, heads * width, length), LOW),
        V((items, half_own, chan, 2 * length), F32),
        V((items, half_own, 8, 2 * length), F32),
        V((items, half_own, chan, 2 * length), LOW),
        V((items, half_own, heads * unit, 2 * length), LOW),
        V((items, half_own, chan, 2 * length), LOW),
        V((items, own, nbins, length), F32),
        V((total * half_own * own, 2 * nbins), F32),
        V((items, total, half_own * own, 2 * nbins), LOW),
        V((items, total, half_own * own, 2 * nbins), LOW),
        V((total, half_own * own, 2 * nbins), F32),
        V((heads * unit, 2 * length), LOW),
        V((items, heads, own, width, length), LOW),
        V((items, rows, width, length), LOW),
        V((heads * width, chan), F32),
        V((heads * unit, chan), F32),
        V((heads * unit, chan), F32),
        V((nbins, chan), F32),
        V((1, length), F32),
        V((nbins, length), F32),
        V((total, block_rows, chan), F32),
        V((total, block_rows, chan), F32),
        V((block_rows, chan), F32),
        V((length, length), F32),
        V((items, length, length), LOW),
        V((items, groups, rows, length), LOW),
        V((4 * width, chan), F32),
        V((1, chan), F32),
        V((groups, sh, chan), F32),
        V((sh, chan), F32),
        V((8, chan), F32),
        V((groups, 8, chan), F32),
        V((8, chan), F32),
        V((total, 8, chan), F32),
    ]
    for shape in (
        (items, groups), (groups,), (3, heads), (items, heads), (items, total), (items, heads),
        (total,), (groups,), (items, groups), (groups,), (groups,), (total,), (groups,),
    ):
        scratch += [dma(shape), dma(shape)]
    grads = pl.pallas_call(
        partial(step_kernel, groups, heads),
        out_shape=[
            jax.ShapeDtypeStruct((groups, sh, chan), F32),
            jax.ShapeDtypeStruct((groups, block_rows, chan), F32),
            jax.ShapeDtypeStruct((nbins, chan), F32),
            jax.ShapeDtypeStruct((8, chan), F32),
        ],
        in_specs=[vmem, pl.BlockSpec(memory_space=pltpu.SMEM)] + [vmem] * 8,
        out_specs=[vmem] * 4,
        scratch_shapes=scratch,
        compiler_params=pltpu.CompilerParams(
            collective_id=0, has_side_effects=True, vmem_limit_bytes=60 * 2**20
        ),
        name="step",
    )(pair_input, lengths, distogram_bins, *weights[:6], small)
    like = lambda group: [jax.ShapeDtypeStruct(w.shape, F32) for w in group]
    outs = pl.pallas_call(
        partial(update_kernel, groups),
        out_shape=[jax.ShapeDtypeStruct((1, 1), F32)] * 2 + like(weights) * 3,
        in_specs=[vmem] * 25,
        out_specs=[vmem] * 23,
        name="update",
    )(*grads, *weights, *momenta, *averages)
    outs = list(outs)
    outs[0], outs[1] = outs[0].reshape(()), outs[1].reshape(())
    for k in (2, 9, 16):
        outs[k + 1] = outs[k + 1].reshape(chan, 1)
        outs[k + 6] = outs[k + 6].reshape(-1)
    return tuple(outs)


def body(groups, heads, *args):
    items, rows, length, channels = args[0].shape
    own = rows // heads
    if own == 8 and rows % 16 == 0 and length % 128 == 0:
        return fused_body(groups, heads, *args)
    return general_body(*args)


def solution(mesh):
    in_specs = (
        P(None, "res", None, None),
        P(),
        P(None, "res", None),
        P(None, "head"),
        P(None, "head"),
        P("head", None),
        P(None, "head"),
        P("head", None),
        P(),
        P(),
        P(None, "head"),
        P(None, "head"),
        P("head", None),
        P(None, "head"),
        P("head", None),
        P(),
        P(),
        P(None, "head"),
        P(None, "head"),
        P("head", None),
        P(None, "head"),
        P("head", None),
        P(),
        P(),
    )
    out_specs = (
        P(),
        P(),
        P(None, "head"),
        P(None, "head"),
        P("head", None),
        P(None, "head"),
        P("head", None),
        P(),
        P(),
        P(None, "head"),
        P(None, "head"),
        P("head", None),
        P(None, "head"),
        P("head", None),
        P(),
        P(),
        P(None, "head"),
        P(None, "head"),
        P("head", None),
        P(None, "head"),
        P("head", None),
        P(),
        P(),
    )
    return jax.shard_map(
        partial(body, mesh.shape["res"], mesh.shape["head"]), mesh=mesh, in_specs=in_specs, out_specs=out_specs, check_vma=False)
```

```python
from functools import partial

import jax
import jax.numpy as jnp
from jax import lax
from jax.experimental import pallas as pl
from jax.experimental.pallas import tpu as pltpu
from jax.sharding import PartitionSpec as P

EPS = 1e-05
NEG = -1000000000.0
MOMENTUM = 0.9
RATE = 20000.0
KEEP = 0.9
CLIP = 0.002


def project(values, weight):
    return jnp.einsum("rjc,cd->rjd", values, weight, preferred_element_type=jnp.float32)


def layer_norm(values, gain):
    center = values - jnp.mean(values, -1, keepdims=True)
    spread = jnp.mean(center * center, -1, keepdims=True)
    return center * lax.rsqrt(spread + EPS) * gain


def norm_back(values, gain, grad_out):
    result, pull = jax.vjp(layer_norm, values, gain)
    return pull(grad_out)


def row_scores(query, key, bias_full, penalty, scale):
    scores = jnp.dot(query, key.T, preferred_element_type=jnp.float32) * scale
    return scores + bias_full.astype(jnp.float32) + penalty[None, :]


def forward_row(bias_full, penalty, scale, row):
    query, key, value, gate = row
    scores = row_scores(query, key, bias_full, penalty, scale)
    peak = jnp.max(scores, -1, keepdims=True)
    expo = jnp.exp(scores - peak)
    summed = jnp.sum(expo, -1, keepdims=True)
    probs = (expo / summed).astype(jnp.bfloat16)
    mixed = jnp.dot(probs, value, preferred_element_type=jnp.float32)
    gated = (mixed * jax.nn.sigmoid(gate)).astype(jnp.bfloat16)
    return (gated, (peak + jnp.log(summed))[:, 0])


def backward_row(bias_full, penalty, scale, carry, row):
    query, key, value, gate, dgated, logsum = row
    scores = row_scores(query, key, bias_full, penalty, scale)
    exact = jnp.exp(scores - logsum[:, None])
    probs = exact.astype(jnp.bfloat16)
    mixed = jnp.dot(probs, value, preferred_element_type=jnp.float32)
    sigma = jax.nn.sigmoid(gate)
    dmixed = (dgated * sigma).astype(jnp.bfloat16)
    dgate = dgated * mixed * sigma * (1.0 - sigma)
    dvalue = jnp.dot(probs.T, dmixed, preferred_element_type=jnp.float32)
    dprobs = jnp.dot(dmixed, value.T, preferred_element_type=jnp.float32)
    inner = jnp.sum(dprobs * exact, -1, keepdims=True)
    dscores = (exact * (dprobs - inner)).astype(jnp.bfloat16)
    dquery = jnp.dot(dscores, key, preferred_element_type=jnp.float32) * scale
    dkey = jnp.dot(dscores.T, query, preferred_element_type=jnp.float32) * scale
    grads = jnp.concatenate([dquery, dkey, dvalue, dgate], -1)
    return (carry + dscores.astype(jnp.float32), grads)


def advance(weight, moment, average, grad):
    velocity = MOMENTUM * moment + grad
    fresh = weight - RATE * (grad + MOMENTUM * velocity)
    return (fresh, velocity, KEEP * average + (1.0 - KEEP) * fresh)


def general_body(
    pair_input,
    lengths,
    distogram_bins,
    head_proj,
    bias_proj,
    output_proj,
    expand_proj,
    reduce_proj,
    distogram_proj,
    small_params,
    momentum_head,
    momentum_bias,
    momentum_output,
    momentum_expand,
    momentum_reduce,
    momentum_distogram,
    momentum_small,
    average_head,
    average_bias,
    average_output,
    average_expand,
    average_reduce,
    average_distogram,
    average_small,
):
    weights = (
        head_proj,
        bias_proj,
        output_proj,
        expand_proj,
        reduce_proj,
        distogram_proj,
        small_params,
    )
    momenta = (
        momentum_head,
        momentum_bias,
        momentum_output,
        momentum_expand,
        momentum_reduce,
        momentum_distogram,
        momentum_small,
    )
    averages = (
        average_head,
        average_bias,
        average_output,
        average_expand,
        average_reduce,
        average_distogram,
        average_small,
    )
    head_w, bias_w, out_w, expand_w, reduce_w, dist_w = [
        w.astype(jnp.bfloat16) for w in weights[:6]
    ]
    items, rows, length, channels = pair_input.shape
    width = output_proj.shape[0]
    scale = width ** (-0.5)
    gain_one = small_params[:channels]
    gain_two = small_params[channels : 2 * channels]
    dist_bias = small_params[2 * channels :]
    positions = jnp.arange(length)
    first_row = lax.axis_index("res") * rows
    size_f = lengths.astype(jnp.float32)
    count = jnp.sum(size_f * size_f)
    grads = [jnp.zeros_like(w) for w in weights]
    loss_part = jnp.zeros((), jnp.float32)
    for item in range(items):
        live = (positions < lengths[item]).astype(jnp.float32)
        penalty = (1.0 - live) * NEG
        row_live = lax.dynamic_slice_in_dim(live, first_row, rows)
        start = pair_input[item].astype(jnp.float32)
        normed = layer_norm(start, gain_one).astype(jnp.bfloat16)
        proj = project(normed, head_w)
        query = proj[..., :width].astype(jnp.bfloat16)
        key = proj[..., width : 2 * width].astype(jnp.bfloat16)
        value = proj[..., 2 * width : 3 * width].astype(jnp.bfloat16)
        gate = proj[..., 3 * width :]
        bias_local = project(normed, bias_w)[..., 0].astype(jnp.bfloat16)
        bias_full = lax.all_gather(bias_local, "res", axis=0, tiled=True)
        gated, logsum = lax.map(
            partial(forward_row, bias_full, penalty, scale), (query, key, value, gate)
        )
        first = start + lax.psum(project(gated, out_w), "head")
        widened = layer_norm(first, gain_two).astype(jnp.bfloat16)
        pre = project(widened, expand_w)
        hidden = jnp.maximum(pre, 0.0).astype(jnp.bfloat16)
        second = first + lax.psum(project(hidden, reduce_w).astype(jnp.bfloat16), "head").astype(
            jnp.float32
        )
        second_low = second.astype(jnp.bfloat16)
        half = project(second_low, dist_w)
        mirror = lax.all_to_all(
            half.astype(jnp.bfloat16), "res", split_axis=1, concat_axis=0, tiled=True
        ).astype(half.dtype)
        logits = half + jnp.transpose(mirror, (1, 0, 2)) + dist_bias
        peak = jnp.max(logits, -1, keepdims=True)
        logp = logits - peak - jnp.log(jnp.sum(jnp.exp(logits - peak), -1, keepdims=True))
        onehot = (distogram_bins[item][:, :, None] == jnp.arange(logits.shape[2])).astype(
            jnp.float32
        )
        weight = (row_live[:, None] * live[None, :])[:, :, None]
        loss_part = loss_part - jnp.sum(logp * onehot * weight) / count
        dlogits = (jnp.exp(logp) - onehot) * weight / count
        back = lax.all_to_all(
            dlogits.astype(jnp.bfloat16), "res", split_axis=1, concat_axis=0, tiled=True
        ).astype(dlogits.dtype)
        dhalf = (dlogits + jnp.transpose(back, (1, 0, 2))).astype(jnp.bfloat16)
        grads[5] = grads[5] + jnp.einsum(
            "rjc,rjb->cb", second_low, dhalf, preferred_element_type=jnp.float32
        )
        dist_grad = jnp.sum(dlogits, (0, 1))
        dsecond = jnp.einsum("rjb,cb->rjc", dhalf, dist_w, preferred_element_type=jnp.float32)
        dtrans = dsecond.astype(jnp.bfloat16)
        grads[4] = grads[4] + jnp.einsum(
            "rjh,rjc->hc", hidden, dtrans, preferred_element_type=jnp.float32
        )
        dhidden = jnp.einsum("rjc,hc->rjh", dtrans, reduce_w, preferred_element_type=jnp.float32)
        dpre = jnp.where(pre > 0, dhidden, 0.0).astype(jnp.bfloat16)
        grads[3] = grads[3] + jnp.einsum(
            "rjc,rjh->ch", widened, dpre, preferred_element_type=jnp.float32
        )
        dwidened = lax.psum(
            jnp.einsum("rjh,ch->rjc", dpre, expand_w, preferred_element_type=jnp.float32).astype(
                jnp.bfloat16
            ),
            "head",
        ).astype(jnp.float32)
        dfirst_norm, gain_two_grad = norm_back(first, gain_two, dwidened)
        dout = (dsecond + dfirst_norm).astype(jnp.bfloat16)
        grads[2] = grads[2] + jnp.einsum(
            "rjd,rjc->dc", gated, dout, preferred_element_type=jnp.float32
        )
        dgated = jnp.einsum("rjc,dc->rjd", dout, out_w, preferred_element_type=jnp.float32)
        bias_terms, dproj = lax.scan(
            partial(backward_row, bias_full, penalty, scale),
            jnp.zeros((length, length), jnp.float32),
            (query, key, value, gate, dgated, logsum),
        )
        dproj = dproj.astype(jnp.bfloat16)
        dbias = lax.psum_scatter(bias_terms, "res", scatter_dimension=0, tiled=True).astype(
            jnp.bfloat16
        )
        grads[0] = grads[0] + jnp.einsum(
            "rjc,rjd->cd", normed, dproj, preferred_element_type=jnp.float32
        )
        grads[1] = (
            grads[1]
            + jnp.einsum("rjc,rj->c", normed, dbias, preferred_element_type=jnp.float32)[:, None]
        )
        dnormed_part = jnp.einsum("rjd,cd->rjc", dproj, head_w, preferred_element_type=jnp.float32)
        dnormed_part = dnormed_part + dbias.astype(jnp.float32)[:, :, None] * bias_w[:, 0].astype(
            jnp.float32
        )
        dnormed = lax.psum(dnormed_part.astype(jnp.bfloat16), "head").astype(jnp.float32)
        unused, gain_one_grad = norm_back(start, gain_one, dnormed)
        grads[6] = grads[6] + jnp.concatenate([gain_one_grad, gain_two_grad, dist_grad])
    summed = lax.psum(
        (grads[0], grads[1], grads[2], grads[3], grads[4], grads[5], grads[6], loss_part), "res"
    )
    total_grads = summed[:7]
    total_loss = summed[7]
    owned = jnp.zeros((), jnp.float32)
    for grad in total_grads[:5]:
        owned = owned + jnp.sum(grad * grad)
    shared = jnp.sum(total_grads[5] * total_grads[5]) + jnp.sum(total_grads[6] * total_grads[6])
    grad_norm = jnp.sqrt(shared + lax.psum(owned, "head"))
    factor = CLIP / jnp.maximum(grad_norm, CLIP)
    results = [
        advance(w, m, a, g * factor) for w, m, a, g in zip(weights, momenta, averages, total_grads)
    ]
    new_w = [r[0] for r in results]
    new_m = [r[1] for r in results]
    new_a = [r[2] for r in results]
    return (
        total_loss,
        grad_norm,
        new_w[0],
        new_w[1],
        new_w[2],
        new_w[3],
        new_w[4],
        new_w[5],
        new_w[6],
        new_m[0],
        new_m[1],
        new_m[2],
        new_m[3],
        new_m[4],
        new_m[5],
        new_m[6],
        new_a[0],
        new_a[1],
        new_a[2],
        new_a[3],
        new_a[4],
        new_a[5],
        new_a[6],
    )


NT = (((1,), (1,)), ((), ()))
NN = (((1,), (0,)), ((), ()))
F32 = jnp.float32
LOW = jnp.bfloat16
LOG2E = 1.4426950408889634


def dot(left, right, dims=NN):
    return lax.dot_general(left, right, dims, preferred_element_type=F32)


def iota(shape, dim):
    return lax.broadcasted_iota(jnp.int32, shape, dim)


def eye(size):
    return (iota((size, size), 0) == iota((size, size), 1)).astype(F32).astype(LOW)


def sigmoid(x):
    return 0.5 * jnp.tanh(0.5 * x) + 0.5


def staged(count, stages, lag):
    for step in range(count + lag * (len(stages) - 1)):
        for k, stage in enumerate(stages):
            if 0 <= step - k * lag < count:
                stage(step - k * lag)


def step_kernel(groups, heads, *refs):
    (
        pair, lengths, bins, head_w, bias_w, out_w, exp_w, red_w, dist_w, small,
        o_head, o_block, o_dist, o_small,
        normed, tok, qkv, sig, expo, mixed, rinv,
        wc, wt, we, wet, wr, wrt, wo, wot, wd, wdt, gain_col, dist_col,
        bias_f, bias_send, bias_all, bias_t, bins_low, bins_in, bins_own, bins_t,
        gated, gall, xhat, rstd, widened, hidden, slow, halves, pack_f, half_send, half_in, mirror,
        dpre_s, first_s, dh_s, dsec_s, dtr_s, dout_s, dg_send, dg_in, g_out, g_red, g_exp, g_dist, loss_acc, dist_acc,
        block_send, block_in, block_sum,
        db_acc, ds_s, dm_s, dproj_s, db_send, db_in, g_head, g_bias, head_in, head_sum, small_own, small_in, card, card_in,
        sem_bias_s, sem_bias_r, sem_bins_s, sem_bins_r, sem_w_s, sem_w_r,
        sem_gat_s, sem_gat_r, sem_half_s, sem_half_r, sem_dg_s, sem_dg_r,
        sem_blk_s, sem_blk_r, sem_gath_s, sem_gath_r, sem_db_s, sem_db_r,
        sem_head_s, sem_head_r, sem_small_s, sem_small_r, sem_card_s, sem_card_r, sem_fin_s, sem_fin_r,
    ) = refs
    items, rows, length, chan = pair.shape
    width = out_w.shape[0]
    nbins = dist_w.shape[0]
    unit = exp_w.shape[1]
    own = rows // heads
    half_own = own // 2
    total = groups * heads
    scale = width ** (-0.5)
    my_r = lax.axis_index("res")
    my_h = lax.axis_index("head")
    me = my_r * heads + my_h

    def device(r, h):
        return {"res": r, "head": h}

    def send(src, dst, ssem, rsem, r, h):
        return pltpu.make_async_remote_copy(
            src_ref=src, dst_ref=dst, send_sem=ssem, recv_sem=rsem,
            device_id=device(r, h), device_id_type=pl.DeviceIdType.MESH,
        )

    def res_peer(o):
        return lax.rem(my_r + o, groups)

    def head_peer(o):
        return lax.rem(my_h + o, heads)

    def any_peer(o):
        d = lax.rem(me + o, total)
        return d, d // heads, lax.rem(d, heads)

    def each(count, make, act):
        def one(o, carry):
            act(make(o))
            return carry
        lax.fori_loop(1, count, one, 0)

    start = lambda c: c.start()
    wait_in = lambda c: c.wait_recv()
    wait_out = lambda c: c.wait_send()

    barrier = pltpu.get_barrier_semaphore()

    def greet(o, carry):
        d, r, h = any_peer(o)
        pl.semaphore_signal(barrier, inc=1, device_id=device(r, h), device_id_type=pl.DeviceIdType.MESH)
        return carry

    lax.fori_loop(1, total, greet, 0)

    hw = head_w[...]
    hw_low = hw.astype(LOW)
    wc[0 : 4 * width] = jnp.transpose(hw).astype(LOW)
    brow = bias_w[...].astype(LOW).astype(F32)
    wc[4 * width :] = jnp.where(iota((16, chan), 0) == 0, brow, 0.0).astype(LOW)
    src_col = iota((4 * width, 4 * width), 0)
    dst_col = iota((4 * width, 4 * width), 1)
    want = jnp.where(
        dst_col < width, dst_col + width, jnp.where(dst_col < 3 * width, dst_col, -1)
    )
    wt[...] = dot(hw_low, (src_col == want).astype(F32).astype(LOW)).astype(LOW)
    ident = eye(chan)
    ident_l = eye(length)
    center_by = (ident.astype(F32) - 1.0 / chan).astype(LOW)
    gain_one = small[0:chan].reshape(1, chan)
    gain_two = small[chan : 2 * chan].reshape(1, chan)
    bins_row = jnp.concatenate(
        [small[2 * chan : 2 * chan + nbins].reshape(1, nbins), jnp.zeros((1, chan - nbins), F32)], 1
    )
    gain_col[...] = jnp.transpose(jnp.broadcast_to(gain_two, (chan, chan)))
    dist_col[...] = jnp.transpose(jnp.broadcast_to(bins_row, (chan, chan)))[:nbins]
    we[:, pl.ds(pl.multiple_of(my_h * unit, unit), unit)] = exp_w[...].astype(LOW)
    wr[pl.ds(pl.multiple_of(my_h * unit, unit), unit), :] = red_w[...].astype(LOW)
    wo[pl.ds(pl.multiple_of(my_h * width, width), width), :] = out_w[...].astype(LOW)
    wdt[...] = dist_w[...].astype(LOW)
    wd[...] = dot(ident, wdt[...], NT).astype(LOW)
    bins_low[...] = bins[...].astype(F32).astype(LOW)
    bins_own[...] = bins[:, pl.ds(pl.multiple_of(my_h * own, own), own), :].astype(F32)
    one_lane = (iota((1, 4 * width), 1) >= 3 * width).astype(F32)

    def before(item):
        def norm(r):
            center = dot(pair[item, r], center_by)
            spread = jnp.mean(center * center, -1, keepdims=True)
            normed[item, r] = (center * lax.rsqrt(spread + EPS) * gain_one).astype(LOW)

        def mult(r):
            low = normed[item, r]
            ch = dot(wc[...], low, NT)
            qkv[item, r] = ch[: 3 * width].astype(LOW)
            sig[item, r] = sigmoid(ch[3 * width : 4 * width])
            bias_f[pl.ds(r, 1), :] = ch[4 * width : 4 * width + 1]
            tok[item, r] = (dot(low, wt[...]) + one_lane).astype(LOW)

        def group(t, carry):
            for k in range(8 + 8):
                if k < 8:
                    norm(t * 8 + k)
                if k >= 8:
                    mult(t * 8 + k - 8)
            return carry
        lax.fori_loop(0, rows // 8, group, 0)
        bias_send[item] = bias_f[...].astype(LOW)
        bias_all[item, pl.ds(pl.multiple_of(my_r * rows, rows), rows), :] = bias_f[...].astype(LOW)

    def bias_copy(item):
        def make(o):
            return send(
                bias_send.at[item],
                bias_all.at[item, pl.ds(pl.multiple_of(my_r * rows, rows), rows), :],
                sem_bias_s.at[item, o], sem_bias_r.at[item, o], res_peer(o), my_h,
            )
        return make

    def bins_block(r):
        return pl.ds(pl.multiple_of((r * rows) // 128 * 128, 128), 128)

    def bins_copy(o):
        return send(
            bins_low.at[:, :, bins_block(res_peer(o))], bins_in.at[my_r],
            sem_bins_s.at[o], sem_bins_r.at[o], res_peer(o), my_h,
        )

    def we_copy(o):
        at = (slice(None), pl.ds(pl.multiple_of(my_h * unit, unit), unit))
        return send(we.at[at], we.at[at], sem_w_s.at[0, o], sem_w_r.at[0, o], my_r, head_peer(o))

    def wr_copy(o):
        at = pl.ds(pl.multiple_of(my_h * unit, unit), unit)
        return send(wr.at[at], wr.at[at], sem_w_s.at[1, o], sem_w_r.at[1, o], my_r, head_peer(o))

    def wo_copy(o):
        at = pl.ds(pl.multiple_of(my_h * width, width), width)
        return send(wo.at[at], wo.at[at], sem_w_s.at[2, o], sem_w_r.at[2, o], my_r, head_peer(o))

    def gated_copy(item):
        def make(o):
            p = head_peer(o)
            return send(
                gated.at[item, pl.ds(p * own, own)],
                gall.at[item, :, pl.ds(pl.multiple_of(my_h * width, width), width), :],
                sem_gat_s.at[item, o], sem_gat_r.at[item, o], my_r, p,
            )
        return make

    def attend(item):
        live = iota((length, length), 0) < lengths[item]
        bt = dot(ident_l, bias_all[item], NT) * LOG2E
        bias_t[...] = bt + jnp.where(live, 0.0, NEG * LOG2E)

        def scores(r):
            q = qkv[item, r, 0:width].astype(F32) * (scale * LOG2E)
            hi = q.astype(LOW)
            lo = (q - hi.astype(F32)).astype(LOW)
            rhs = jnp.concatenate([hi, lo, jnp.zeros((2 * width, length), LOW)], 0)
            s = dot(tok[item, r], rhs) + bias_t[...]
            expo[item, r] = jnp.exp2(s - jnp.max(s, 0, keepdims=True)).astype(LOW)

        def gather(r):
            lhs = jnp.concatenate(
                [qkv[item, r, 2 * width : 3 * width], jnp.ones((16, length), LOW)], 0
            )
            o = dot(lhs, expo[item, r])
            inv = 1.0 / o[width : width + 1]
            rinv[item, pl.ds(r, 1), :] = inv
            m = o[:width] * inv
            mixed[item, r] = m
            gated[item, r] = (m * sig[item, r]).astype(LOW)

        def chunk(o, carry):
            p = head_peer(o)
            base = p * own

            def one(t, c):
                for k in range(8 + 4):
                    if k < 8:
                        scores(base + t * 8 + k)
                    if k >= 4:
                        gather(base + t * 8 + k - 4)
                return c
            lax.fori_loop(0, own // 8, one, 0, unroll=1)

            @pl.when(o < heads)
            def _():
                gated_copy(item)(o).start()
            return carry
        lax.fori_loop(1, heads + 1, chunk, 0)
        gall[item, :, pl.ds(pl.multiple_of(my_h * width, width), width), :] = gated[
            item, pl.ds(my_h * own, own)
        ]

    def pair_of(ref, item, t):
        return jnp.concatenate([ref[item, t], ref[item, t + half_own]], 1)

    sel_row = iota((total * half_own, length), 0)
    sel_col = iota((total * half_own, length), 1)
    sel_at = sel_row // half_own * own + lax.rem(sel_row, half_own)
    sel_a = (sel_col == sel_at).astype(F32).astype(LOW)
    sel_b = (sel_col == sel_at + half_own).astype(F32).astype(LOW)

    def forward(item):
        gc = jnp.concatenate([gain_col[...]] * (2 * length // chan), 1)
        zero = jnp.zeros((nbins, length), LOW)

        def enter(t):
            g2 = pair_of(gall, item, t)
            base = my_h * own + t
            first = jnp.concatenate(
                [dot(ident, pair[item, base], NT), dot(ident, pair[item, base + half_own], NT)], 1
            ) + dot(wot[...], g2)
            first_s[t] = first
            center = first - jnp.mean(first, 0, keepdims=True)
            rs = lax.rsqrt(jnp.mean(center * center, 0, keepdims=True) + EPS)
            xh = center * rs
            xhat[item, t] = xh
            rstd[item, t] = jnp.broadcast_to(rs, (8, 2 * length))
            widened[item, t] = (xh * gc).astype(LOW)

        def expand(t):
            for b in range(heads):
                hidden[item, t, b * unit : (b + 1) * unit] = jnp.maximum(
                    dot(wet[b * unit : (b + 1) * unit], widened[item, t]), 0.0
                ).astype(LOW)

        def reduce(t):
            slow[item, t] = (first_s[t] + dot(wrt[...], hidden[item, t])).astype(LOW)

        def project_half(t):
            half = dot(wdt[...], slow[item, t])
            halves[item, t] = half[:, :length]
            halves[item, t + half_own] = half[:, length:]

        def pack(t):
            for k in range(2):
                part = halves[item, t + k * half_own].astype(LOW)
                packed = dot(sel_a, jnp.concatenate([part, zero], 0), NT) + dot(
                    sel_b, jnp.concatenate([zero, part], 0), NT
                )
                pack_f[pl.ds(t + k * half_own, total * half_own, own), :] = packed

        staged(half_own, (enter, expand, reduce, project_half, pack), 2)
        half_send[item] = pack_f[...].reshape(half_send.shape[1:]).astype(LOW)
        half_in[item, me] = half_send[item, me]

    def half_copy(item):
        def make(o):
            d, r, h = any_peer(o)
            return send(
                half_send.at[item, d], half_in.at[item, me],
                sem_half_s.at[item, o], sem_half_r.at[item, o], r, h,
            )
        return make

    size_sum = jnp.zeros((1, length), F32)
    for item in range(items):
        size = lengths[item]
        size_sum = size_sum + (jnp.zeros((1, length), jnp.int32) + size * size).astype(F32)

    def backward(item):
        mirror[...] = half_in[item].astype(F32)
        live = (iota((1, length), 1) < lengths[item]).astype(F32) / size_sum
        levels = iota((nbins, length), 0).astype(F32)[None]

        gc = jnp.concatenate([gain_col[...]] * (2 * length // chan), 1)
        dist_c = jnp.concatenate([dist_col[...]] * (length // chan), 1)[None]

        def two(ref, t):
            return jnp.concatenate(
                [ref[item, pl.ds(t, 1), :][None], ref[item, pl.ds(t + half_own, 1), :][None]], 0
            )

        def loss_grad(t):
            flip = mirror[:, t * own : (t + 1) * own, :].reshape(length, 2 * nbins)
            flip = dot(eye(2 * nbins), flip.astype(LOW), NT)
            here = jnp.concatenate([halves[item, t], halves[item, t + half_own]], 0)
            logits = (here + flip).reshape(2, nbins, length) + dist_c
            peak = jnp.max(logits, 1, keepdims=True)
            ex = jnp.exp(logits - peak)
            tot = jnp.sum(ex, 1, keepdims=True)
            prob = ex * (1.0 / tot)
            hot = (two(bins_own, t) == levels).astype(F32)
            hot_t = (two(bins_t, t) == levels).astype(F32)
            at = me * own + t + iota((2, 1, length), 0) * half_own
            weight = jnp.where(at < lengths[item], 1.0, 0.0) * live[None]
            picked = jnp.sum(hot * logits, 1, keepdims=True)
            lost = weight * (peak + jnp.log(tot) - picked)
            loss_acc[...] += lost[0] + lost[1]
            short = prob - hot
            dl = short * weight
            dist_acc[...] += dl[0] + dl[1]
            dh = ((short + prob - hot_t) * weight).astype(LOW)
            dh_s[t] = jnp.concatenate([dh[0], dh[1]], 1)

        def enter(t):
            dsec = dot(wd[...], dh_s[t])
            dsec_s[t] = dsec
            dtr_s[t] = dsec.astype(LOW)
            g_dist[...] += dot(dh_s[t], slow[item, t], NT)

        def through(t):
            for b in range(heads):
                at_b = slice(b * unit, (b + 1) * unit)
                hid = hidden[item, t, at_b]
                dpre_s[t, at_b] = jnp.where(
                    hid.astype(F32) > 0.0, dot(wr[at_b], dtr_s[t]), 0.0
                ).astype(LOW)

        def weights_back(t):
            for b in range(heads):
                at_b = slice(b * unit, (b + 1) * unit)
                g_red[at_b] += dot(hidden[item, t, at_b], dtr_s[t], NT)
                g_exp[at_b] += dot(dpre_s[t, at_b], widened[item, t], NT)

        def leave(t):
            dxh = dot(we[...], dpre_s[t]) * gc
            xh = xhat[item, t]
            m1 = jnp.mean(dxh, 0, keepdims=True)
            m2 = jnp.mean(dxh * xh, 0, keepdims=True)
            dout_s[t] = (dsec_s[t] + rstd[item, t, 0:1] * (dxh - m1 - xh * m2)).astype(LOW)

        def output_back(t):
            dg = dot(wo[...], dout_s[t]).astype(LOW)
            for h in range(heads):
                for k in range(2):
                    dg_send[item, h, t + k * half_own] = dg[
                        h * width : (h + 1) * width, k * length : (k + 1) * length
                    ]
            g_out[...] += dot(pair_of(gall, item, t), dout_s[t], NT)

        staged(half_own, (loss_grad, enter, through, weights_back, leave, output_back), 2)
        dg_in[item, pl.ds(my_h * own, own)] = dg_send[item, my_h]

    def dg_copy(item):
        def make(o):
            p = head_peer(o)
            return send(
                dg_send.at[item, p], dg_in.at[item, pl.ds(my_h * own, own)],
                sem_dg_s.at[item, o], sem_dg_r.at[item, o], my_r, p,
            )
        return make

    def attend_back(item):
        db_acc[...] = jnp.zeros_like(db_acc)
        tail_row = iota((16, length), 0)

        def first(r, k, tot):
            s = sig[item, r]
            m = mixed[item, r]
            dg = dg_in[item, r].astype(F32)
            dm = (dg * s * rinv[item, pl.ds(r, 1), :]).astype(LOW)
            inner = -jnp.sum(dm.astype(F32) * m, 0, keepdims=True)
            hi = inner.astype(LOW).astype(F32)
            lo = inner - hi
            tail = jnp.where(tail_row == 0, hi, jnp.where(tail_row == 1, lo, 0.0)).astype(LOW)
            rhs = jnp.concatenate(
                [jnp.zeros((2 * width, length), LOW), dm, tail, jnp.zeros((width - 16, length), LOW)], 0
            )
            dm_s[k] = dm
            dproj_s[3 * width :, k * length : (k + 1) * length] = (dg * m * s * (1.0 - s)).astype(LOW)
            ds = expo[item, r].astype(F32) * dot(tok[item, r], rhs)
            db_acc[...] += ds
            ds_s[k] = ds.astype(LOW)
            return None

        def second(r, k):
            at = slice(k * length, (k + 1) * length)
            ds = ds_s[k]
            dproj_s[0:width, at] = (dot(qkv[item, r, width : 2 * width], ds) * scale).astype(LOW)
            dproj_s[width : 2 * width, at] = (dot(qkv[item, r, 0:width], ds, NT) * scale).astype(LOW)
            dproj_s[2 * width : 3 * width, at] = dot(dm_s[k], expo[item, r], NT).astype(LOW)

        def group(t, carry):
            tot = None
            for k in range(8 + 4):
                if k < 8:
                    tot = first(t * 8 + k, k, tot)
                if k >= 4:
                    second(t * 8 + k - 4, k - 4)
            g_head[...] += dot(dproj_s[...], normed[item, pl.ds(t * 8, 8)].reshape(8 * length, chan))
            return carry
        lax.fori_loop(0, rows // 8, group, 0)
        db_send[item] = dot(ident_l, db_acc[...].astype(LOW), NT).astype(LOW)
        db_in[item, my_r] = db_send[item, pl.ds(pl.multiple_of(my_r * rows, rows), rows), :]

    def db_copy(item):
        def make(o):
            p = res_peer(o)
            return send(
                db_send.at[item, pl.ds(pl.multiple_of(p * rows, rows), rows), :], db_in.at[item, my_r],
                sem_db_s.at[item, o], sem_db_r.at[item, o], p, my_h,
            )
        return make

    def bias_back(item):
        db = db_in[item, 0].astype(F32)
        for s in range(1, groups):
            db = db + db_in[item, s].astype(F32)
        db = db.astype(LOW).astype(F32)
        at = iota((rows, length), 0)

        def row(r, acc):
            return acc + dot(jnp.where(at == r, db, 0.0).astype(LOW), normed[item, r])
        acc = lax.fori_loop(0, rows, row, jnp.zeros((rows, chan), F32), unroll=4)
        g_bias[...] += jnp.sum(acc, 0, keepdims=True)

    def block_copy(o):
        d, r, h = any_peer(o)
        return send(block_send.at[d], block_in.at[me], sem_blk_s.at[o], sem_blk_r.at[o], r, h)

    def gather_copy(o):
        return send(block_sum, o_block.at[my_r], sem_gath_s.at[o], sem_gath_r.at[o], res_peer(o), my_h)

    ru, rw, rb = unit // groups, width // groups, nbins // total

    def block_make():
        for r in range(groups):
            for h in range(heads):
                d = r * heads + h
                at = h * unit + r * ru
                block_send[d, 0:ru] = g_red[at : at + ru]
                block_send[d, ru : 2 * ru] = g_exp[at : at + ru]
                at = h * width + r * rw
                block_send[d, 2 * ru : 2 * ru + rw] = g_out[at : at + rw]
                block_send[d, 2 * ru + rw : 2 * ru + rw + rb] = g_dist[d * rb : (d + 1) * rb]
                block_send[d, 2 * ru + rw + rb :] = jnp.zeros((8 - rw - rb, chan), F32)
        block_in[me] = block_send[me]

    def block_add():
        acc = block_in[0]
        for d in range(1, total):
            acc = acc + block_in[d]
        block_sum[...] = acc
        o_block[my_r] = acc

    def head_copy(o):
        p = res_peer(o)
        return send(
            g_head.at[pl.ds(pl.multiple_of(p * (4 * width // groups), 4 * width // groups), 4 * width // groups), :],
            head_in.at[my_r], sem_head_s.at[o], sem_head_r.at[o], p, my_h,
        )

    def small_copy(o):
        return send(small_own, small_in.at[my_r], sem_small_s.at[o], sem_small_r.at[o], res_peer(o), my_h)

    def card_copy(o):
        d, r, h = any_peer(o)
        return send(card, card_in.at[me], sem_card_s.at[o], sem_card_r.at[o], r, h)

    def fin_copy(o):
        return send(head_sum, o_head.at[my_r], sem_fin_s.at[o], sem_fin_r.at[o], res_peer(o), my_h)

    for ref in (g_out, g_red, g_exp, g_dist, loss_acc, dist_acc, g_head, g_bias):
        ref[...] = jnp.zeros_like(ref)
    before(0)
    pl.semaphore_wait(barrier, total - 1)
    each(groups, bias_copy(0), start)
    for make in (we_copy, wr_copy, wo_copy):
        each(heads, make, start)
    for item in range(1, items):
        before(item)
        each(groups, bias_copy(item), start)
    each(groups, bins_copy, start)
    bins_in[my_r] = bins_low[:, :, bins_block(my_r)]
    for item in range(items):
        each(groups, bias_copy(item), wait_in)
        attend(item)
    for make in (we_copy, wr_copy, wo_copy):
        each(heads, make, wait_in)
    for b in range(heads):
        at = slice(b * unit, (b + 1) * unit)
        wet[at] = dot(ident, we[:, at], NT).astype(LOW)
        wrt[:, at] = dot(ident, wr[at], NT).astype(LOW)
    wot[...] = dot(ident, wo[...], NT).astype(LOW)
    for item in range(items):
        each(heads, gated_copy(item), wait_in)
        forward(item)
        each(total, half_copy(item), start)
    each(groups, bins_copy, wait_in)
    lane = my_r * rows + my_h * own - (my_r * rows) // 128 * 128
    pick = (iota((16, 128), 1) == iota((16, 128), 0) + lane).astype(F32).astype(LOW)
    for item in range(items):
        bins_t[item] = dot(pick, bins_in[:, item].reshape(groups * rows, 128), NT)
    for item in range(items):
        each(total, half_copy(item), wait_in)
        backward(item)
        each(heads, dg_copy(item), start)
    block_make()
    each(total, block_copy, start)
    for item in range(items):
        each(heads, dg_copy(item), wait_in)
        attend_back(item)
        each(groups, db_copy(item), start)
        if item == 0:
            each(total, block_copy, wait_in)
            block_add()
            each(groups, gather_copy, start)
    each(groups, head_copy, start)
    sh = 4 * width // groups
    head_in[my_r] = g_head[pl.ds(pl.multiple_of(my_r * sh, sh), sh), :]
    for item in range(items):
        each(groups, db_copy(item), wait_in)
        bias_back(item)
    gb = g_bias[...]
    up_one = jnp.sum(wc[0 : 4 * width].astype(F32) * g_head[...], 0, keepdims=True) + brow * gb
    up_two = jnp.sum(wet[...].astype(F32) * g_exp[...], 0, keepdims=True)
    dacc = dist_acc[:, 0:chan]
    lacc = loss_acc[:, 0:chan]
    for k in range(1, length // chan):
        dacc = dacc + dist_acc[:, k * chan : (k + 1) * chan]
        lacc = lacc + loss_acc[:, k * chan : (k + 1) * chan]
    dacc = jnp.transpose(jnp.concatenate([dacc, jnp.zeros((chan - nbins, chan), F32)], 0))
    small_own[0:1] = gb
    small_own[1:2] = up_one / gain_one
    small_own[2:3] = up_two / gain_two
    small_own[3:4] = jnp.sum(dacc, 0, keepdims=True)
    small_own[4:5] = lacc
    small_own[5:8] = jnp.zeros((3, chan), F32)
    small_in[my_r] = small_own[...]
    each(groups, small_copy, start)
    each(groups, head_copy, wait_in)
    acc = head_in[0]
    for s in range(1, groups):
        acc = acc + head_in[s]
    head_sum[...] = acc
    o_head[my_r] = acc
    each(groups, fin_copy, start)
    each(groups, small_copy, wait_in)
    tiny = small_in[0]
    for s in range(1, groups):
        tiny = tiny + small_in[s]
    blocks = block_sum[...]
    squares = jnp.sum(acc * acc, 0, keepdims=True) + jnp.sum(blocks * blocks, 0, keepdims=True)
    card[...] = tiny
    card[5:6] = squares
    card[6:8] = blocks[2 * ru + rw : 2 * ru + rw + rb]
    card_in[me] = card[...]
    each(total, card_copy, start)
    each(total, card_copy, wait_in)
    every = card_in[0]
    for d in range(1, total):
        every = every + card_in[d]
    mine = [card_in[my_r * heads + h] for h in range(heads)]
    summed = mine[0]
    bias_sq = mine[0] * mine[0]
    for h in range(1, heads):
        summed = summed + mine[h]
        bias_sq = bias_sq + mine[h] * mine[h]
    norm_sq = every[5:6] + bias_sq[0:1]
    for k in (1, 2, 3):
        norm_sq = norm_sq + summed[k : k + 1] * summed[k : k + 1]
    norm = jnp.sqrt(jnp.sum(norm_sq, -1, keepdims=True))
    o_small[...] = summed
    o_small[0:1] = card[0:1]
    o_small[4:5] = jnp.broadcast_to(jnp.sum(summed[4:5], -1, keepdims=True), (1, chan))
    o_small[5:6] = jnp.broadcast_to(norm, (1, chan))
    o_small[6:7] = jnp.broadcast_to(CLIP / jnp.maximum(norm, CLIP), (1, chan))
    for d in range(total):
        o_dist[d * rb : (d + 1) * rb] = card_in[d, 6 : 6 + rb]
    each(groups, gather_copy, wait_in)
    each(groups, fin_copy, wait_in)
    for item in range(items):
        each(groups, bias_copy(item), wait_out)
        each(heads, gated_copy(item), wait_out)
        each(total, half_copy(item), wait_out)
        each(heads, dg_copy(item), wait_out)
        each(groups, db_copy(item), wait_out)
    for make in (we_copy, wr_copy, wo_copy):
        each(heads, make, wait_out)
    for make in (bins_copy, gather_copy, head_copy, small_copy, fin_copy):
        each(groups, make, wait_out)
    for make in (block_copy, card_copy):
        each(total, make, wait_out)


def update_kernel(groups, *refs):
    g_head, g_block, g_dist, g_small = refs[:4]
    weights, momenta, averages = refs[4:11], refs[11:18], refs[18:25]
    loss, norm = refs[25:27]
    new_w, new_m, new_a = refs[27:34], refs[34:41], refs[41:48]
    loss[...] = g_small[4:5, 0:1]
    norm[...] = g_small[5:6, 0:1]
    factor = g_small[6:7, 0:1]
    unit = weights[4].shape[0]
    width = weights[2].shape[0]
    ru, rw = unit // groups, width // groups
    chan = g_small.shape[1]

    def put(k, grad, at=(slice(None), slice(None))):
        fresh, velocity, average = advance(
            weights[k][at], momenta[k][at], averages[k][at], grad * (factor if grad.ndim > 1 else factor[0])
        )
        new_w[k][at] = fresh
        new_m[k][at] = velocity
        new_a[k][at] = average

    put(0, jnp.transpose(g_head[...].reshape(weights[0].shape[1], chan)))
    put(1, g_small[0:1])
    put(3, jnp.transpose(g_block[:, ru : 2 * ru].reshape(unit, chan)))
    put(4, g_block[:, 0:ru].reshape(unit, chan))
    for r in range(groups):
        put(2, g_block[r, 2 * ru : 2 * ru + rw], (slice(r * rw, (r + 1) * rw), slice(None)))
    nbins = weights[5].shape[0]
    put(5, g_dist[...])
    put(6, g_small[1], (slice(0, chan),))
    put(6, g_small[2], (slice(chan, 2 * chan),))
    put(6, g_small[3, 0:nbins], (slice(2 * chan, 2 * chan + nbins),))


def fused_body(groups, heads, *args):
    pair_input, lengths, distogram_bins = args[:3]
    weights, momenta, averages = list(args[3:10]), list(args[10:17]), list(args[17:24])
    items, rows, length, chan = pair_input.shape
    width = weights[2].shape[0]
    unit = weights[3].shape[1]
    nbins = weights[5].shape[1]
    own, total = rows // heads, groups * heads
    half_own = own // 2
    for group in (weights, momenta, averages):
        group[1] = group[1].reshape(1, chan)
        group[5] = group[5].T
    vmem = pl.BlockSpec(memory_space=pltpu.VMEM)
    block_rows = 2 * (unit // groups) + 8
    sh = 4 * width // groups
    V = pltpu.VMEM
    dma = pltpu.SemaphoreType.DMA
    scratch = [
        V((items, rows, length, chan), LOW),
        V((items, rows, length, 4 * width), LOW),
        V((items, rows, 3 * width, length), LOW),
        V((items, rows, width, length), F32),
        V((items, rows, length, length), LOW),
        V((items, rows, width, length), F32),
        V((items, rows, length), F32),
        V((4 * width + 16, chan), LOW),
        V((chan, 4 * width), LOW),
        V((chan, heads * unit), LOW),
        V((heads * unit, chan), LOW),
        V((heads * unit, chan), LOW),
        V((chan, heads * unit), LOW),
        V((heads * width, chan), LOW),
        V((chan, heads * width), LOW),
        V((chan, nbins), LOW),
        V((nbins, chan), LOW),
        V((chan, chan), F32),
        V((nbins, chan), F32),
        V((rows, length), F32),
        V((items, rows, length), LOW),
        V((items, length, length), LOW),
        V((length, length), F32),
        V((items, rows, length), LOW),
        V((groups, items, rows, 128), LOW),
        V((items, own, length), F32),
        V((items, 16, length), F32),
        V((items, rows, width, length), LOW),
        V((items, own, heads * width, length), LOW),
        V((items, half_own, chan, 2 * length), F32),
        V((items, half_own, 8, 2 * length), F32),
        V((items, half_own, chan, 2 * length), LOW),
        V((items, half_own, heads * unit, 2 * length), LOW),
        V((items, half_own, chan, 2 * length), LOW),
        V((items, own, nbins, length), F32),
        V((total * half_own * own, 2 * nbins), F32),
        V((items, total, half_own * own, 2 * nbins), LOW),
        V((items, total, half_own * own, 2 * nbins), LOW),
        V((total, half_own * own, 2 * nbins), F32),
        V((half_own, heads * unit, 2 * length), LOW),
        V((half_own, chan, 2 * length), F32),
        V((half_own, nbins, 2 * length), LOW),
        V((half_own, chan, 2 * length), F32),
        V((half_own, chan, 2 * length), LOW),
        V((half_own, chan, 2 * length), LOW),
        V((items, heads, own, width, length), LOW),
        V((items, rows, width, length), LOW),
        V((heads * width, chan), F32),
        V((heads * unit, chan), F32),
        V((heads * unit, chan), F32),
        V((nbins, chan), F32),
        V((1, length), F32),
        V((nbins, length), F32),
        V((total, block_rows, chan), F32),
        V((total, block_rows, chan), F32),
        V((block_rows, chan), F32),
        V((length, length), F32),
        V((8, length, length), LOW),
        V((8, width, length), LOW),
        V((4 * width, 8 * length), LOW),
        V((items, length, length), LOW),
        V((items, groups, rows, length), LOW),
        V((4 * width, chan), F32),
        V((1, chan), F32),
        V((groups, sh, chan), F32),
        V((sh, chan), F32),
        V((8, chan), F32),
        V((groups, 8, chan), F32),
        V((8, chan), F32),
        V((total, 8, chan), F32),
    ]
    for shape in (
        (items, groups), (groups,), (3, heads), (items, heads), (items, total), (items, heads),
        (total,), (groups,), (items, groups), (groups,), (groups,), (total,), (groups,),
    ):
        scratch += [dma(shape), dma(shape)]
    grads = pl.pallas_call(
        partial(step_kernel, groups, heads),
        out_shape=[
            jax.ShapeDtypeStruct((groups, sh, chan), F32),
            jax.ShapeDtypeStruct((groups, block_rows, chan), F32),
            jax.ShapeDtypeStruct((nbins, chan), F32),
            jax.ShapeDtypeStruct((8, chan), F32),
        ],
        in_specs=[vmem, pl.BlockSpec(memory_space=pltpu.SMEM)] + [vmem] * 8,
        out_specs=[vmem] * 4,
        scratch_shapes=scratch,
        compiler_params=pltpu.CompilerParams(
            collective_id=0, has_side_effects=True, vmem_limit_bytes=60 * 2**20
        ),
        name="step",
    )(pair_input, lengths, distogram_bins, *weights)
    like = lambda group: [jax.ShapeDtypeStruct(w.shape, F32) for w in group]
    outs = pl.pallas_call(
        partial(update_kernel, groups),
        out_shape=[jax.ShapeDtypeStruct((1, 1), F32)] * 2 + like(weights) * 3,
        in_specs=[vmem] * 25,
        out_specs=[vmem] * 23,
        name="update",
    )(*grads, *weights, *momenta, *averages)
    outs = list(outs)
    outs[0], outs[1] = outs[0].reshape(()), outs[1].reshape(())
    for k in (2, 9, 16):
        outs[k + 1] = outs[k + 1].reshape(chan, 1)
        outs[k + 5] = outs[k + 5].T
    return tuple(outs)


def body(groups, heads, *args):
    items, rows, length, channels = args[0].shape
    own = rows // heads
    if own == 8 and rows % 16 == 0 and length % 128 == 0:
        return fused_body(groups, heads, *args)
    return general_body(*args)


def solution(mesh):
    in_specs = (
        P(None, "res", None, None),
        P(),
        P(None, "res", None),
        P(None, "head"),
        P(None, "head"),
        P("head", None),
        P(None, "head"),
        P("head", None),
        P(),
        P(),
        P(None, "head"),
        P(None, "head"),
        P("head", None),
        P(None, "head"),
        P("head", None),
        P(),
        P(),
        P(None, "head"),
        P(None, "head"),
        P("head", None),
        P(None, "head"),
        P("head", None),
        P(),
        P(),
    )
    out_specs = (
        P(),
        P(),
        P(None, "head"),
        P(None, "head"),
        P("head", None),
        P(None, "head"),
        P("head", None),
        P(),
        P(),
        P(None, "head"),
        P(None, "head"),
        P("head", None),
        P(None, "head"),
        P("head", None),
        P(),
        P(),
        P(None, "head"),
        P(None, "head"),
        P("head", None),
        P(None, "head"),
        P("head", None),
        P(),
        P(),
    )
    return jax.shard_map(
        partial(body, mesh.shape["res"], mesh.shape["head"]), mesh=mesh, in_specs=in_specs, out_specs=out_specs, check_vma=False)
```

```python
from functools import partial

import jax
import jax.numpy as jnp
from jax import lax
from jax.experimental import pallas as pl
from jax.experimental.pallas import tpu as pltpu
from jax.sharding import PartitionSpec as P

EPS = 1e-05
NEG = -1000000000.0
MOMENTUM = 0.9
RATE = 20000.0
KEEP = 0.9
CLIP = 0.002


def project(values, weight):
    return jnp.einsum("rjc,cd->rjd", values, weight, preferred_element_type=jnp.float32)


def layer_norm(values, gain):
    center = values - jnp.mean(values, -1, keepdims=True)
    spread = jnp.mean(center * center, -1, keepdims=True)
    return center * lax.rsqrt(spread + EPS) * gain


def norm_back(values, gain, grad_out):
    result, pull = jax.vjp(layer_norm, values, gain)
    return pull(grad_out)


def row_scores(query, key, bias_full, penalty, scale):
    scores = jnp.dot(query, key.T, preferred_element_type=jnp.float32) * scale
    return scores + bias_full.astype(jnp.float32) + penalty[None, :]


def forward_row(bias_full, penalty, scale, row):
    query, key, value, gate = row
    scores = row_scores(query, key, bias_full, penalty, scale)
    peak = jnp.max(scores, -1, keepdims=True)
    expo = jnp.exp(scores - peak)
    summed = jnp.sum(expo, -1, keepdims=True)
    probs = (expo / summed).astype(jnp.bfloat16)
    mixed = jnp.dot(probs, value, preferred_element_type=jnp.float32)
    gated = (mixed * jax.nn.sigmoid(gate)).astype(jnp.bfloat16)
    return (gated, (peak + jnp.log(summed))[:, 0])


def backward_row(bias_full, penalty, scale, carry, row):
    query, key, value, gate, dgated, logsum = row
    scores = row_scores(query, key, bias_full, penalty, scale)
    exact = jnp.exp(scores - logsum[:, None])
    probs = exact.astype(jnp.bfloat16)
    mixed = jnp.dot(probs, value, preferred_element_type=jnp.float32)
    sigma = jax.nn.sigmoid(gate)
    dmixed = (dgated * sigma).astype(jnp.bfloat16)
    dgate = dgated * mixed * sigma * (1.0 - sigma)
    dvalue = jnp.dot(probs.T, dmixed, preferred_element_type=jnp.float32)
    dprobs = jnp.dot(dmixed, value.T, preferred_element_type=jnp.float32)
    inner = jnp.sum(dprobs * exact, -1, keepdims=True)
    dscores = (exact * (dprobs - inner)).astype(jnp.bfloat16)
    dquery = jnp.dot(dscores, key, preferred_element_type=jnp.float32) * scale
    dkey = jnp.dot(dscores.T, query, preferred_element_type=jnp.float32) * scale
    grads = jnp.concatenate([dquery, dkey, dvalue, dgate], -1)
    return (carry + dscores.astype(jnp.float32), grads)


def advance(weight, moment, average, grad):
    velocity = MOMENTUM * moment + grad
    fresh = weight - RATE * (grad + MOMENTUM * velocity)
    return (fresh, velocity, KEEP * average + (1.0 - KEEP) * fresh)


def general_body(
    pair_input,
    lengths,
    distogram_bins,
    head_proj,
    bias_proj,
    output_proj,
    expand_proj,
    reduce_proj,
    distogram_proj,
    small_params,
    momentum_head,
    momentum_bias,
    momentum_output,
    momentum_expand,
    momentum_reduce,
    momentum_distogram,
    momentum_small,
    average_head,
    average_bias,
    average_output,
    average_expand,
    average_reduce,
    average_distogram,
    average_small,
):
    weights = (
        head_proj,
        bias_proj,
        output_proj,
        expand_proj,
        reduce_proj,
        distogram_proj,
        small_params,
    )
    momenta = (
        momentum_head,
        momentum_bias,
        momentum_output,
        momentum_expand,
        momentum_reduce,
        momentum_distogram,
        momentum_small,
    )
    averages = (
        average_head,
        average_bias,
        average_output,
        average_expand,
        average_reduce,
        average_distogram,
        average_small,
    )
    head_w, bias_w, out_w, expand_w, reduce_w, dist_w = [
        w.astype(jnp.bfloat16) for w in weights[:6]
    ]
    items, rows, length, channels = pair_input.shape
    width = output_proj.shape[0]
    scale = width ** (-0.5)
    gain_one = small_params[:channels]
    gain_two = small_params[channels : 2 * channels]
    dist_bias = small_params[2 * channels :]
    positions = jnp.arange(length)
    first_row = lax.axis_index("res") * rows
    size_f = lengths.astype(jnp.float32)
    count = jnp.sum(size_f * size_f)
    grads = [jnp.zeros_like(w) for w in weights]
    loss_part = jnp.zeros((), jnp.float32)
    for item in range(items):
        live = (positions < lengths[item]).astype(jnp.float32)
        penalty = (1.0 - live) * NEG
        row_live = lax.dynamic_slice_in_dim(live, first_row, rows)
        start = pair_input[item].astype(jnp.float32)
        normed = layer_norm(start, gain_one).astype(jnp.bfloat16)
        proj = project(normed, head_w)
        query = proj[..., :width].astype(jnp.bfloat16)
        key = proj[..., width : 2 * width].astype(jnp.bfloat16)
        value = proj[..., 2 * width : 3 * width].astype(jnp.bfloat16)
        gate = proj[..., 3 * width :]
        bias_local = project(normed, bias_w)[..., 0].astype(jnp.bfloat16)
        bias_full = lax.all_gather(bias_local, "res", axis=0, tiled=True)
        gated, logsum = lax.map(
            partial(forward_row, bias_full, penalty, scale), (query, key, value, gate)
        )
        first = start + lax.psum(project(gated, out_w), "head")
        widened = layer_norm(first, gain_two).astype(jnp.bfloat16)
        pre = project(widened, expand_w)
        hidden = jnp.maximum(pre, 0.0).astype(jnp.bfloat16)
        second = first + lax.psum(project(hidden, reduce_w).astype(jnp.bfloat16), "head").astype(
            jnp.float32
        )
        second_low = second.astype(jnp.bfloat16)
        half = project(second_low, dist_w)
        mirror = lax.all_to_all(
            half.astype(jnp.bfloat16), "res", split_axis=1, concat_axis=0, tiled=True
        ).astype(half.dtype)
        logits = half + jnp.transpose(mirror, (1, 0, 2)) + dist_bias
        peak = jnp.max(logits, -1, keepdims=True)
        logp = logits - peak - jnp.log(jnp.sum(jnp.exp(logits - peak), -1, keepdims=True))
        onehot = (distogram_bins[item][:, :, None] == jnp.arange(logits.shape[2])).astype(
            jnp.float32
        )
        weight = (row_live[:, None] * live[None, :])[:, :, None]
        loss_part = loss_part - jnp.sum(logp * onehot * weight) / count
        dlogits = (jnp.exp(logp) - onehot) * weight / count
        back = lax.all_to_all(
            dlogits.astype(jnp.bfloat16), "res", split_axis=1, concat_axis=0, tiled=True
        ).astype(dlogits.dtype)
        dhalf = (dlogits + jnp.transpose(back, (1, 0, 2))).astype(jnp.bfloat16)
        grads[5] = grads[5] + jnp.einsum(
            "rjc,rjb->cb", second_low, dhalf, preferred_element_type=jnp.float32
        )
        dist_grad = jnp.sum(dlogits, (0, 1))
        dsecond = jnp.einsum("rjb,cb->rjc", dhalf, dist_w, preferred_element_type=jnp.float32)
        dtrans = dsecond.astype(jnp.bfloat16)
        grads[4] = grads[4] + jnp.einsum(
            "rjh,rjc->hc", hidden, dtrans, preferred_element_type=jnp.float32
        )
        dhidden = jnp.einsum("rjc,hc->rjh", dtrans, reduce_w, preferred_element_type=jnp.float32)
        dpre = jnp.where(pre > 0, dhidden, 0.0).astype(jnp.bfloat16)
        grads[3] = grads[3] + jnp.einsum(
            "rjc,rjh->ch", widened, dpre, preferred_element_type=jnp.float32
        )
        dwidened = lax.psum(
            jnp.einsum("rjh,ch->rjc", dpre, expand_w, preferred_element_type=jnp.float32).astype(
                jnp.bfloat16
            ),
            "head",
        ).astype(jnp.float32)
        dfirst_norm, gain_two_grad = norm_back(first, gain_two, dwidened)
        dout = (dsecond + dfirst_norm).astype(jnp.bfloat16)
        grads[2] = grads[2] + jnp.einsum(
            "rjd,rjc->dc", gated, dout, preferred_element_type=jnp.float32
        )
        dgated = jnp.einsum("rjc,dc->rjd", dout, out_w, preferred_element_type=jnp.float32)
        bias_terms, dproj = lax.scan(
            partial(backward_row, bias_full, penalty, scale),
            jnp.zeros((length, length), jnp.float32),
            (query, key, value, gate, dgated, logsum),
        )
        dproj = dproj.astype(jnp.bfloat16)
        dbias = lax.psum_scatter(bias_terms, "res", scatter_dimension=0, tiled=True).astype(
            jnp.bfloat16
        )
        grads[0] = grads[0] + jnp.einsum(
            "rjc,rjd->cd", normed, dproj, preferred_element_type=jnp.float32
        )
        grads[1] = (
            grads[1]
            + jnp.einsum("rjc,rj->c", normed, dbias, preferred_element_type=jnp.float32)[:, None]
        )
        dnormed_part = jnp.einsum("rjd,cd->rjc", dproj, head_w, preferred_element_type=jnp.float32)
        dnormed_part = dnormed_part + dbias.astype(jnp.float32)[:, :, None] * bias_w[:, 0].astype(
            jnp.float32
        )
        dnormed = lax.psum(dnormed_part.astype(jnp.bfloat16), "head").astype(jnp.float32)
        unused, gain_one_grad = norm_back(start, gain_one, dnormed)
        grads[6] = grads[6] + jnp.concatenate([gain_one_grad, gain_two_grad, dist_grad])
    summed = lax.psum(
        (grads[0], grads[1], grads[2], grads[3], grads[4], grads[5], grads[6], loss_part), "res"
    )
    total_grads = summed[:7]
    total_loss = summed[7]
    owned = jnp.zeros((), jnp.float32)
    for grad in total_grads[:5]:
        owned = owned + jnp.sum(grad * grad)
    shared = jnp.sum(total_grads[5] * total_grads[5]) + jnp.sum(total_grads[6] * total_grads[6])
    grad_norm = jnp.sqrt(shared + lax.psum(owned, "head"))
    factor = CLIP / jnp.maximum(grad_norm, CLIP)
    results = [
        advance(w, m, a, g * factor) for w, m, a, g in zip(weights, momenta, averages, total_grads)
    ]
    new_w = [r[0] for r in results]
    new_m = [r[1] for r in results]
    new_a = [r[2] for r in results]
    return (
        total_loss,
        grad_norm,
        new_w[0],
        new_w[1],
        new_w[2],
        new_w[3],
        new_w[4],
        new_w[5],
        new_w[6],
        new_m[0],
        new_m[1],
        new_m[2],
        new_m[3],
        new_m[4],
        new_m[5],
        new_m[6],
        new_a[0],
        new_a[1],
        new_a[2],
        new_a[3],
        new_a[4],
        new_a[5],
        new_a[6],
    )


NT = (((1,), (1,)), ((), ()))
NN = (((1,), (0,)), ((), ()))
F32 = jnp.float32
LOW = jnp.bfloat16
LOG2E = 1.4426950408889634


def dot(left, right, dims=NN):
    return lax.dot_general(left, right, dims, preferred_element_type=F32)


def iota(shape, dim):
    return lax.broadcasted_iota(jnp.int32, shape, dim)


def eye(size):
    return (iota((size, size), 0) == iota((size, size), 1)).astype(F32).astype(LOW)


def sigmoid(x):
    return 0.5 * jnp.tanh(0.5 * x) + 0.5


def staged(count, stages, lag):
    for step in range(count + lag * (len(stages) - 1)):
        for k, stage in enumerate(stages):
            if 0 <= step - k * lag < count:
                stage(step - k * lag)


def step_kernel(groups, heads, *refs):
    (
        pair_hbm, lengths, bins, head_w, bias_w, out_w, exp_w, red_w, dist_w, small,
        o_head, o_block, o_dist, o_small,
        pair, normed, tok, qkv, sig, expo, mixed, rinv,
        wc, wt, we, wet, wr, wrt, wo, wot, wd, wdt, gain_col, dist_col, sel_a, sel_b,
        bias_f, bias_send, bias_all, bias_t, bins_low, bins_in, bins_own, bins_t,
        gated, gall, xhat, rstd, widened, hidden, slow, halves, pack_f, half_send, half_in, mirror,
        dpre_s, first_s, dh_s, dsec_s, dtr_s, dout_s, dg_send, dg_in,
        g_out, g_red, g_exp, g_dist, loss_acc, dist_acc,
        block_own, block_send, block_in, part_own, part_in, block_sum,
        db_acc, ds_s, dm_s, dproj_s, db_send, db_in, g_head, g_bias, head_in, head_sum, card, card_in,
        sem_pair, sem_bias, sem_bins, sem_w, sem_gat, sem_half, sem_dg,
        sem_blk, sem_part, sem_gath, sem_db, sem_head, sem_card, sem_fin,
    ) = refs
    items, rows, length, chan = pair.shape
    group_rows = 8
    width = out_w.shape[0]
    nbins = dist_w.shape[0]
    unit = exp_w.shape[1]
    own = rows // heads
    half_own = own // 2
    total = groups * heads
    scale = width ** (-0.5)
    my_r = lax.axis_index("res")
    my_h = lax.axis_index("head")
    me = my_r * heads + my_h

    def device(r, h):
        return {"res": r, "head": h}

    def send(src, dst, sem, r, h):
        return pltpu.make_async_remote_copy(
            src_ref=src, dst_ref=dst, send_sem=sem.at[0], recv_sem=sem.at[1],
            device_id=device(r, h), device_id_type=pl.DeviceIdType.MESH,
        )

    def res_peer(o):
        return lax.rem(my_r + o, groups)

    def head_peer(o):
        return lax.rem(my_h + o, heads)

    def any_peer(o):
        d = lax.rem(me + o, total)
        return d, d // heads, lax.rem(d, heads)

    def start(count, make):
        def one(o, carry):
            make(o).start()
            return carry
        lax.fori_loop(1, count, one, 0)

    def wait_in(ref, sem):
        send(ref, ref, sem, res_peer(1), my_h).wait_recv()

    def wait_out(ref, sem):
        send(ref, ref, sem, res_peer(1), my_h).wait_send()

    def load(item, t):
        at = pl.ds(t * group_rows, group_rows)
        return pltpu.make_async_copy(pair_hbm.at[item, at], pair.at[item, at], sem_pair.at[item, t])

    barrier = pltpu.get_barrier_semaphore()

    def greet(o, carry):
        d, r, h = any_peer(o)
        pl.semaphore_signal(barrier, inc=1, device_id=device(r, h), device_id_type=pl.DeviceIdType.MESH)
        return carry

    lax.fori_loop(1, total, greet, 0)

    for item in range(items):
        for t in range(rows // group_rows):
            load(item, t).start()

    brow = bias_w[...].astype(LOW).astype(F32)
    gain_one = small[0:chan].reshape(1, chan)
    gain_two = small[chan : 2 * chan].reshape(1, chan)
    ident = eye(chan)
    ident_l = eye(length)
    center_by = (ident.astype(F32) - 1.0 / chan).astype(LOW)
    one_lane = (iota((1, 4 * width), 1) >= 3 * width).astype(F32)

    def prepare_first():
        hw = head_w[...]
        wc[0 : 4 * width] = jnp.transpose(hw).astype(LOW)
        wc[4 * width :] = jnp.where(iota((16, chan), 0) == 0, brow, 0.0).astype(LOW)
        src_col = iota((4 * width, 4 * width), 0)
        dst_col = iota((4 * width, 4 * width), 1)
        want = jnp.where(
            dst_col < width, dst_col + width, jnp.where(dst_col < 3 * width, dst_col, -1)
        )
        wt[...] = dot(hw.astype(LOW), (src_col == want).astype(F32).astype(LOW)).astype(LOW)

    def prepare_weights():
        we[:, pl.ds(pl.multiple_of(my_h * unit, unit), unit)] = exp_w[...].astype(LOW)
        wr[pl.ds(pl.multiple_of(my_h * unit, unit), unit), :] = red_w[...].astype(LOW)
        wo[pl.ds(pl.multiple_of(my_h * width, width), width), :] = out_w[...].astype(LOW)

    def prepare_rest():
        bins_row = jnp.concatenate(
            [small[2 * chan : 2 * chan + nbins].reshape(1, nbins), jnp.zeros((1, chan - nbins), F32)], 1
        )
        gain_col[...] = jnp.transpose(jnp.broadcast_to(gain_two, (chan, chan)))
        dist_col[...] = jnp.transpose(jnp.broadcast_to(bins_row, (chan, chan)))[:nbins]
        wdt[...] = dist_w[...].astype(LOW)
        wd[...] = dot(ident, wdt[...], NT).astype(LOW)
        bins_low[...] = bins[...].astype(F32).astype(LOW)
        bins_own[...] = bins[:, pl.ds(pl.multiple_of(my_h * own, own), own), :].astype(F32)
        sel_row = iota((total * half_own, length), 0)
        sel_col = iota((total * half_own, length), 1)
        sel_at = sel_row // half_own * own + lax.rem(sel_row, half_own)
        sel_a[...] = (sel_col == sel_at).astype(F32).astype(LOW)
        sel_b[...] = (sel_col == sel_at + half_own).astype(F32).astype(LOW)
        for ref in (g_out, g_red, g_exp, g_dist, loss_acc, dist_acc, g_head, g_bias):
            ref[...] = jnp.zeros_like(ref)

    def before(item):
        def norm(r):
            center = dot(pair[item, r], center_by)
            spread = jnp.mean(center * center, -1, keepdims=True)
            normed[item, r] = (center * lax.rsqrt(spread + EPS) * gain_one).astype(LOW)

        def mult(r):
            low = normed[item, r]
            ch = dot(wc[...], low, NT)
            qkv[item, r] = ch[: 3 * width].astype(LOW)
            sig[item, r] = sigmoid(ch[3 * width : 4 * width])
            bias_f[pl.ds(r, 1), :] = ch[4 * width : 4 * width + 1]
            tok[item, r] = (dot(low, wt[...]) + one_lane).astype(LOW)

        def group(t, carry):
            load(item, t).wait()
            for k in range(8 + 8):
                if k < 8:
                    norm(t * 8 + k)
                if k >= 8:
                    mult(t * 8 + k - 8)
            return carry
        lax.fori_loop(0, rows // 8, group, 0)
        bias_send[item] = bias_f[...].astype(LOW)
        bias_all[item, pl.ds(pl.multiple_of(my_r * rows, rows), rows), :] = bias_f[...].astype(LOW)

    def bias_copy(item):
        def make(o):
            return send(
                bias_send.at[item],
                bias_all.at[item, pl.ds(pl.multiple_of(my_r * rows, rows), rows), :],
                sem_bias.at[item], res_peer(o), my_h,
            )
        return make

    def bins_block(r):
        return pl.ds(pl.multiple_of((r * rows) // 128 * 128, 128), 128)

    def bins_copy(o):
        return send(
            bins_low.at[:, :, bins_block(res_peer(o))], bins_in.at[my_r],
            sem_bins, res_peer(o), my_h,
        )

    def we_copy(o):
        at = (slice(None), pl.ds(pl.multiple_of(my_h * unit, unit), unit))
        return send(we.at[at], we.at[at], sem_w.at[0], my_r, head_peer(o))

    def wr_copy(o):
        at = pl.ds(pl.multiple_of(my_h * unit, unit), unit)
        return send(wr.at[at], wr.at[at], sem_w.at[1], my_r, head_peer(o))

    def wo_copy(o):
        at = pl.ds(pl.multiple_of(my_h * width, width), width)
        return send(wo.at[at], wo.at[at], sem_w.at[2], my_r, head_peer(o))

    def gated_copy(item):
        def make(o):
            p = head_peer(o)
            return send(
                gated.at[item, pl.ds(p * own, own)],
                gall.at[item, :, pl.ds(pl.multiple_of(my_h * width, width), width), :],
                sem_gat.at[item], my_r, p,
            )
        return make

    def attend(item):
        live = iota((length, length), 0) < lengths[item]
        bt = dot(ident_l, bias_all[item], NT) * LOG2E
        bias_t[...] = bt + jnp.where(live, 0.0, NEG * LOG2E)

        def scores(r):
            q = qkv[item, r, 0:width].astype(F32) * (scale * LOG2E)
            hi = q.astype(LOW)
            lo = (q - hi.astype(F32)).astype(LOW)
            rhs = jnp.concatenate([hi, lo, jnp.zeros((2 * width, length), LOW)], 0)
            s = dot(tok[item, r], rhs) + bias_t[...]
            expo[item, r] = jnp.exp2(s - jnp.max(s, 0, keepdims=True)).astype(LOW)

        def gather(r):
            lhs = jnp.concatenate(
                [qkv[item, r, 2 * width : 3 * width], jnp.ones((16, length), LOW)], 0
            )
            o = dot(lhs, expo[item, r])
            inv = 1.0 / o[width : width + 1]
            rinv[item, pl.ds(r, 1), :] = inv
            m = o[:width] * inv
            mixed[item, r] = m
            gated[item, r] = (m * sig[item, r]).astype(LOW)

        def chunk(o, carry):
            p = head_peer(o)
            base = p * own

            def one(t, c):
                for k in range(8 + 4):
                    if k < 8:
                        scores(base + t * 8 + k)
                    if k >= 4:
                        gather(base + t * 8 + k - 4)
                return c
            lax.fori_loop(0, own // 8, one, 0, unroll=1)

            @pl.when(o < heads)
            def _():
                gated_copy(item)(o).start()
            return carry
        lax.fori_loop(1, heads + 1, chunk, 0)
        gall[item, :, pl.ds(pl.multiple_of(my_h * width, width), width), :] = gated[
            item, pl.ds(my_h * own, own)
        ]

    def pair_of(ref, item, t):
        return jnp.concatenate([ref[item, t], ref[item, t + half_own]], 1)

    def forward(item):
        gc = jnp.concatenate([gain_col[...]] * (2 * length // chan), 1)
        zero = jnp.zeros((nbins, length), LOW)

        def enter(t):
            g2 = pair_of(gall, item, t)
            base = my_h * own + t
            first = jnp.concatenate(
                [dot(ident, pair[item, base], NT), dot(ident, pair[item, base + half_own], NT)], 1
            ) + dot(wot[...], g2)
            first_s[t] = first
            center = first - jnp.mean(first, 0, keepdims=True)
            rs = lax.rsqrt(jnp.mean(center * center, 0, keepdims=True) + EPS)
            xh = center * rs
            xhat[item, t] = xh
            rstd[item, t] = jnp.broadcast_to(rs, (8, 2 * length))
            widened[item, t] = (xh * gc).astype(LOW)

        def expand(t):
            for b in range(heads):
                hidden[item, t, b * unit : (b + 1) * unit] = jnp.maximum(
                    dot(wet[b * unit : (b + 1) * unit], widened[item, t]), 0.0
                ).astype(LOW)

        def reduce(t):
            slow[item, t] = (first_s[t] + dot(wrt[...], hidden[item, t])).astype(LOW)

        def project_half(t):
            half = dot(wdt[...], slow[item, t])
            halves[item, t] = half[:, :length]
            halves[item, t + half_own] = half[:, length:]

        def pack(t):
            for k in range(2):
                part = halves[item, t + k * half_own].astype(LOW)
                packed = dot(sel_a[...], jnp.concatenate([part, zero], 0), NT) + dot(
                    sel_b[...], jnp.concatenate([zero, part], 0), NT
                )
                pack_f[pl.ds(t + k * half_own, total * half_own, own), :] = packed

        staged(half_own, (enter, expand, reduce, project_half, pack), 2)
        half_send[item] = pack_f[...].reshape(half_send.shape[1:]).astype(LOW)
        half_in[item, me] = half_send[item, me]

    def half_copy(item):
        def make(o):
            d, r, h = any_peer(o)
            return send(
                half_send.at[item, d], half_in.at[item, me],
                sem_half.at[item], r, h,
            )
        return make

    size_sum = jnp.zeros((1, length), F32)
    for item in range(items):
        size = lengths[item]
        size_sum = size_sum + (jnp.zeros((1, length), jnp.int32) + size * size).astype(F32)

    def backward(item):
        mirror[...] = half_in[item].astype(F32)
        live = (iota((1, length), 1) < lengths[item]).astype(F32) / size_sum
        levels = iota((nbins, length), 0).astype(F32)[None]

        gc = jnp.concatenate([gain_col[...]] * (2 * length // chan), 1)
        dist_c = jnp.concatenate([dist_col[...]] * (length // chan), 1)[None]

        def two(ref, t):
            return jnp.concatenate(
                [ref[item, pl.ds(t, 1), :][None], ref[item, pl.ds(t + half_own, 1), :][None]], 0
            )

        def loss_grad(t):
            flip = mirror[:, t * own : (t + 1) * own, :].reshape(length, 2 * nbins)
            flip = dot(eye(2 * nbins), flip.astype(LOW), NT)
            here = jnp.concatenate([halves[item, t], halves[item, t + half_own]], 0)
            logits = (here + flip).reshape(2, nbins, length) + dist_c
            peak = jnp.max(logits, 1, keepdims=True)
            ex = jnp.exp(logits - peak)
            tot = jnp.sum(ex, 1, keepdims=True)
            prob = ex * (1.0 / tot)
            hot = (two(bins_own, t) == levels).astype(F32)
            hot_t = (two(bins_t, t) == levels).astype(F32)
            at = me * own + t + iota((2, 1, length), 0) * half_own
            weight = jnp.where(at < lengths[item], 1.0, 0.0) * live[None]
            picked = jnp.sum(hot * logits, 1, keepdims=True)
            lost = weight * (peak + jnp.log(tot) - picked)
            loss_acc[...] += lost[0] + lost[1]
            short = prob - hot
            dl = short * weight
            dist_acc[...] += dl[0] + dl[1]
            dh = ((short + prob - hot_t) * weight).astype(LOW)
            dh_s[t] = jnp.concatenate([dh[0], dh[1]], 1)

        def enter(t):
            dsec = dot(wd[...], dh_s[t])
            dsec_s[t] = dsec
            dtr_s[t] = dsec.astype(LOW)
            g_dist[...] += dot(dh_s[t], slow[item, t], NT)

        def through(t):
            for b in range(heads):
                at_b = slice(b * unit, (b + 1) * unit)
                hid = hidden[item, t, at_b]
                dpre_s[t, at_b] = jnp.where(
                    hid.astype(F32) > 0.0, dot(wr[at_b], dtr_s[t]), 0.0
                ).astype(LOW)

        def weights_back(t):
            for b in range(heads):
                at_b = slice(b * unit, (b + 1) * unit)
                g_red[at_b] += dot(hidden[item, t, at_b], dtr_s[t], NT)
                g_exp[at_b] += dot(dpre_s[t, at_b], widened[item, t], NT)

        def leave(t):
            dxh = dot(we[...], dpre_s[t]) * gc
            xh = xhat[item, t]
            m1 = jnp.mean(dxh, 0, keepdims=True)
            m2 = jnp.mean(dxh * xh, 0, keepdims=True)
            dout_s[t] = (dsec_s[t] + rstd[item, t, 0:1] * (dxh - m1 - xh * m2)).astype(LOW)

        def output_back(t):
            dg = dot(wo[...], dout_s[t]).astype(LOW)
            for h in range(heads):
                for k in range(2):
                    dg_send[item, h, t + k * half_own] = dg[
                        h * width : (h + 1) * width, k * length : (k + 1) * length
                    ]
            g_out[...] += dot(pair_of(gall, item, t), dout_s[t], NT)

        staged(half_own, (loss_grad, enter, through, weights_back, leave, output_back), 2)
        dg_in[item, pl.ds(my_h * own, own)] = dg_send[item, my_h]

    def dg_copy(item):
        def make(o):
            p = head_peer(o)
            return send(
                dg_send.at[item, p], dg_in.at[item, pl.ds(my_h * own, own)],
                sem_dg.at[item], my_r, p,
            )
        return make

    def attend_back(item):
        db_acc[...] = jnp.zeros_like(db_acc)
        tail_row = iota((16, length), 0)

        def first(r, k, tot):
            s = sig[item, r]
            m = mixed[item, r]
            dg = dg_in[item, r].astype(F32)
            dm = (dg * s * rinv[item, pl.ds(r, 1), :]).astype(LOW)
            inner = -jnp.sum(dm.astype(F32) * m, 0, keepdims=True)
            hi = inner.astype(LOW).astype(F32)
            lo = inner - hi
            tail = jnp.where(tail_row == 0, hi, jnp.where(tail_row == 1, lo, 0.0)).astype(LOW)
            rhs = jnp.concatenate(
                [jnp.zeros((2 * width, length), LOW), dm, tail, jnp.zeros((width - 16, length), LOW)], 0
            )
            dm_s[k] = dm
            dproj_s[3 * width :, k * length : (k + 1) * length] = (dg * m * s * (1.0 - s)).astype(LOW)
            ds = expo[item, r].astype(F32) * dot(tok[item, r], rhs)
            db_acc[...] += ds
            ds_s[k] = ds.astype(LOW)
            return None

        def second(r, k):
            at = slice(k * length, (k + 1) * length)
            ds = ds_s[k]
            dproj_s[0:width, at] = (dot(qkv[item, r, width : 2 * width], ds) * scale).astype(LOW)
            dproj_s[width : 2 * width, at] = (dot(qkv[item, r, 0:width], ds, NT) * scale).astype(LOW)
            dproj_s[2 * width : 3 * width, at] = dot(dm_s[k], expo[item, r], NT).astype(LOW)

        def group(t, carry):
            tot = None
            for k in range(8 + 4):
                if k < 8:
                    tot = first(t * 8 + k, k, tot)
                if k >= 4:
                    second(t * 8 + k - 4, k - 4)
            g_head[...] += dot(dproj_s[...], normed[item, pl.ds(t * 8, 8)].reshape(8 * length, chan))
            return carry
        lax.fori_loop(0, rows // 8, group, 0)
        db_send[item] = dot(ident_l, db_acc[...].astype(LOW), NT).astype(LOW)
        db_in[item, my_r] = db_send[item, pl.ds(pl.multiple_of(my_r * rows, rows), rows), :]

    def db_copy(item):
        def make(o):
            p = res_peer(o)
            return send(
                db_send.at[item, pl.ds(pl.multiple_of(p * rows, rows), rows), :], db_in.at[item, my_r],
                sem_db.at[item], p, my_h,
            )
        return make

    def bias_back(item):
        db = db_in[item, 0].astype(F32)
        for s in range(1, groups):
            db = db + db_in[item, s].astype(F32)
        db = db.astype(LOW).astype(F32)
        at = iota((8, length), 0)
        acc = jnp.zeros((8, chan), F32)
        for g in range(rows // 8):
            part = db[8 * g : 8 * g + 8]
            spread = jnp.concatenate([jnp.where(at == q, part, 0.0) for q in range(8)], 1)
            acc = acc + dot(
                spread.astype(LOW), normed[item, 8 * g : 8 * g + 8].reshape(8 * length, chan)
            )
        g_bias[...] += jnp.sum(acc, 0, keepdims=True)

    ru, rw, rb = unit // groups, width // groups, nbins // total
    piece = 2 * ru + 8

    def block_copy(o):
        p = head_peer(o)
        return send(block_send.at[p], block_in.at[my_h], sem_blk, my_r, p)

    def part_copy(o):
        p = res_peer(o)
        return send(
            part_own.at[pl.ds(pl.multiple_of(p * piece, 8), piece), :], part_in.at[my_r], sem_part, p, my_h
        )

    def gather_copy(o):
        return send(block_sum, o_block.at[my_r], sem_gath, res_peer(o), my_h)

    def block_make():
        for h in range(heads):
            for r in range(groups):
                base = r * piece
                at = h * unit + r * ru
                block_own[h, base : base + ru] = g_red[at : at + ru]
                block_own[h, base + ru : base + 2 * ru] = g_exp[at : at + ru]
                at = h * width + r * rw
                base += 2 * ru
                block_own[h, base : base + rw] = g_out[at : at + rw]
                at = (r * heads + h) * rb
                block_own[h, base + rw : base + rw + rb] = g_dist[at : at + rb]
                block_own[h, base + rw + rb : base + 8] = jnp.zeros((8 - rw - rb, chan), F32)
            block_send[h] = block_own[h].astype(LOW)

    def part_make():
        acc = block_own[my_h]
        for o in range(1, heads):
            acc = acc + block_in[head_peer(o)].astype(F32)
        part_own[...] = acc
        part_in[my_r] = part_own[pl.ds(pl.multiple_of(my_r * piece, 8), piece), :]

    def block_add():
        acc = part_in[0]
        for r in range(1, groups):
            acc = acc + part_in[r]
        block_sum[...] = acc
        o_block[my_r] = acc

    def head_copy(o):
        p = res_peer(o)
        return send(
            g_head.at[pl.ds(pl.multiple_of(p * (4 * width // groups), 4 * width // groups), 4 * width // groups), :],
            head_in.at[my_r], sem_head, p, my_h,
        )

    def card_copy(o):
        d, r, h = any_peer(o)
        return send(card, card_in.at[me], sem_card, r, h)

    def fin_copy(o):
        return send(head_sum, o_head.at[my_r], sem_fin, res_peer(o), my_h)

    all_but = lambda ref, item, count: ref.at[item, pl.ds(0, count)]
    bias_part = lambda item: all_but(bias_all, item, (groups - 1) * rows)
    gat_part = lambda item: all_but(gated, item, (heads - 1) * own)
    dg_part = lambda item: all_but(dg_in, item, (heads - 1) * own)
    half_part = lambda item: all_but(half_in, item, total - 1)
    db_part = lambda item: all_but(db_in, item, groups - 1)
    bins_part = bins_in.at[pl.ds(0, groups - 1)]
    w_parts = (
        we.at[:, pl.ds(0, (heads - 1) * unit)], wr.at[pl.ds(0, (heads - 1) * unit)],
        wo.at[pl.ds(0, (heads - 1) * width)],
    )
    blk_part = block_in.at[pl.ds(0, heads - 1)]
    part_part = part_in.at[pl.ds(0, groups - 1)]
    gath_part = o_block.at[pl.ds(0, groups - 1)]
    head_part = head_in.at[pl.ds(0, groups - 1)]
    fin_part = o_head.at[pl.ds(0, groups - 1)]
    card_part = card_in.at[pl.ds(0, total - 1)]

    prepare_first()
    before(0)
    pl.semaphore_wait(barrier, total - 1)
    start(groups, bias_copy(0))
    prepare_weights()
    for make in (we_copy, wr_copy, wo_copy):
        start(heads, make)
    for item in range(1, items):
        before(item)
        start(groups, bias_copy(item))
    prepare_rest()
    start(groups, bins_copy)
    bins_in[my_r] = bins_low[:, :, bins_block(my_r)]
    for item in range(items):
        wait_in(bias_part(item), sem_bias.at[item])
        attend(item)
    for k in range(3):
        wait_in(w_parts[k], sem_w.at[k])
    for b in range(heads):
        at = slice(b * unit, (b + 1) * unit)
        wet[at] = dot(ident, we[:, at], NT).astype(LOW)
        wrt[:, at] = dot(ident, wr[at], NT).astype(LOW)
    wot[...] = dot(ident, wo[...], NT).astype(LOW)
    for item in range(items):
        wait_in(gat_part(item), sem_gat.at[item])
        forward(item)
        start(total, half_copy(item))
    wait_in(bins_part, sem_bins)
    lane = my_r * rows + my_h * own - (my_r * rows) // 128 * 128
    pick = (iota((16, 128), 1) == iota((16, 128), 0) + lane).astype(F32).astype(LOW)
    for item in range(items):
        bins_t[item] = dot(pick, bins_in[:, item].reshape(groups * rows, 128), NT)
    for item in range(items):
        wait_in(half_part(item), sem_half.at[item])
        backward(item)
        start(heads, dg_copy(item))
    block_make()
    start(heads, block_copy)
    for item in range(items):
        wait_in(dg_part(item), sem_dg.at[item])
        attend_back(item)
        start(groups, db_copy(item))
        if item == 0:
            wait_in(blk_part, sem_blk)
            part_make()
            start(groups, part_copy)
    start(groups, head_copy)
    sh = 4 * width // groups
    head_in[my_r] = g_head[pl.ds(pl.multiple_of(my_r * sh, sh), sh), :]
    wait_in(part_part, sem_part)
    block_add()
    start(groups, gather_copy)
    for item in range(items - 1):
        wait_in(db_part(item), sem_db.at[item])
        bias_back(item)
    wait_in(head_part, sem_head)
    acc = head_in[0]
    for r in range(1, groups):
        acc = acc + head_in[r]
    head_sum[...] = acc
    o_head[my_r] = acc
    start(groups, fin_copy)
    up_one = jnp.sum(wc[0 : 4 * width].astype(F32) * g_head[...], 0, keepdims=True)
    up_two = jnp.sum(wet[...].astype(F32) * g_exp[...], 0, keepdims=True)
    dacc = dist_acc[:, 0:chan]
    lacc = loss_acc[:, 0:chan]
    for k in range(1, length // chan):
        dacc = dacc + dist_acc[:, k * chan : (k + 1) * chan]
        lacc = lacc + loss_acc[:, k * chan : (k + 1) * chan]
    dacc = jnp.transpose(jnp.concatenate([dacc, jnp.zeros((chan - nbins, chan), F32)], 0))
    blocks = block_sum[...]
    card[2:3] = up_two / gain_two
    card[3:4] = jnp.sum(dacc, 0, keepdims=True)
    card[4:5] = lacc
    card[5:6] = jnp.sum(acc * acc, 0, keepdims=True) + jnp.sum(blocks * blocks, 0, keepdims=True)
    card[6:8] = blocks[2 * ru + rw : 2 * ru + rw + rb]
    wait_in(db_part(items - 1), sem_db.at[items - 1])
    bias_back(items - 1)
    gb = g_bias[...]
    card[0:1] = gb
    card[1:2] = (up_one + brow * gb) / gain_one
    card_in[me] = card[...]
    start(total, card_copy)
    wait_in(card_part, sem_card)
    by_head = [card_in[h] for h in range(heads)]
    for r in range(1, groups):
        by_head = [a + card_in[r * heads + h] for h, a in enumerate(by_head)]
    every = by_head[0]
    bias_sq = by_head[0] * by_head[0]
    for a in by_head[1:]:
        every = every + a
        bias_sq = bias_sq + a * a
    norm_sq = every[5:6] + bias_sq[0:1]
    for k in (1, 2, 3):
        norm_sq = norm_sq + every[k : k + 1] * every[k : k + 1]
    norm = jnp.sqrt(jnp.sum(norm_sq, -1, keepdims=True))
    o_small[...] = every
    mine = card_in[my_h]
    for r in range(1, groups):
        mine = mine + card_in[r * heads + my_h]
    o_small[0:1] = mine[0:1]
    o_small[4:5] = jnp.broadcast_to(jnp.sum(every[4:5], -1, keepdims=True), (1, chan))
    o_small[5:6] = jnp.broadcast_to(norm, (1, chan))
    o_small[6:7] = jnp.broadcast_to(CLIP / jnp.maximum(norm, CLIP), (1, chan))
    for d in range(total):
        o_dist[d * rb : (d + 1) * rb] = card_in[d, 6 : 6 + rb]
    wait_in(gath_part, sem_gath)
    wait_in(fin_part, sem_fin)
    for item in range(items):
        wait_out(bias_part(item), sem_bias.at[item])
        wait_out(gat_part(item), sem_gat.at[item])
        wait_out(half_part(item), sem_half.at[item])
        wait_out(dg_part(item), sem_dg.at[item])
        wait_out(db_part(item), sem_db.at[item])
    for k in range(3):
        wait_out(w_parts[k], sem_w.at[k])
    for ref, sem in (
        (bins_part, sem_bins), (blk_part, sem_blk), (part_part, sem_part), (gath_part, sem_gath),
        (head_part, sem_head), (fin_part, sem_fin), (card_part, sem_card),
    ):
        wait_out(ref, sem)


def update_kernel(groups, *refs):
    g_head, g_block, g_dist, g_small = refs[:4]
    weights, momenta, averages = refs[4:11], refs[11:18], refs[18:25]
    loss, norm = refs[25:27]
    new_w, new_m, new_a = refs[27:34], refs[34:41], refs[41:48]
    loss[...] = g_small[4:5, 0:1]
    norm[...] = g_small[5:6, 0:1]
    factor = g_small[6:7, 0:1]
    unit = weights[4].shape[0]
    width = weights[2].shape[0]
    ru, rw = unit // groups, width // groups
    chan = g_small.shape[1]

    def put(k, grad, at=(slice(None), slice(None))):
        fresh, velocity, average = advance(
            weights[k][at], momenta[k][at], averages[k][at], grad * (factor if grad.ndim > 1 else factor[0])
        )
        new_w[k][at] = fresh
        new_m[k][at] = velocity
        new_a[k][at] = average

    put(0, jnp.transpose(g_head[...].reshape(weights[0].shape[1], chan)))
    put(1, g_small[0:1])
    put(3, jnp.transpose(g_block[:, ru : 2 * ru].reshape(unit, chan)))
    put(4, g_block[:, 0:ru].reshape(unit, chan))
    for r in range(groups):
        put(2, g_block[r, 2 * ru : 2 * ru + rw], (slice(r * rw, (r + 1) * rw), slice(None)))
    nbins = weights[5].shape[0]
    put(5, g_dist[...])
    put(6, g_small[1], (slice(0, chan),))
    put(6, g_small[2], (slice(chan, 2 * chan),))
    put(6, g_small[3, 0:nbins], (slice(2 * chan, 2 * chan + nbins),))


def fused_body(groups, heads, *args):
    pair_input, lengths, distogram_bins = args[:3]
    weights, momenta, averages = list(args[3:10]), list(args[10:17]), list(args[17:24])
    items, rows, length, chan = pair_input.shape
    width = weights[2].shape[0]
    unit = weights[3].shape[1]
    nbins = weights[5].shape[1]
    own, total = rows // heads, groups * heads
    half_own = own // 2
    for group in (weights, momenta, averages):
        group[1] = group[1].reshape(1, chan)
        group[5] = group[5].T
    vmem = pl.BlockSpec(memory_space=pltpu.VMEM)
    block_rows = 2 * (unit // groups) + 8
    sh = 4 * width // groups
    V = pltpu.VMEM
    dma = pltpu.SemaphoreType.DMA
    scratch = [
        V((items, rows, length, chan), LOW),
        V((items, rows, length, chan), LOW),
        V((items, rows, length, 4 * width), LOW),
        V((items, rows, 3 * width, length), LOW),
        V((items, rows, width, length), F32),
        V((items, rows, length, length), LOW),
        V((items, rows, width, length), F32),
        V((items, rows, length), F32),
        V((4 * width + 16, chan), LOW),
        V((chan, 4 * width), LOW),
        V((chan, heads * unit), LOW),
        V((heads * unit, chan), LOW),
        V((heads * unit, chan), LOW),
        V((chan, heads * unit), LOW),
        V((heads * width, chan), LOW),
        V((chan, heads * width), LOW),
        V((chan, nbins), LOW),
        V((nbins, chan), LOW),
        V((chan, chan), F32),
        V((nbins, chan), F32),
        V((total * half_own, length), LOW),
        V((total * half_own, length), LOW),
        V((rows, length), F32),
        V((items, rows, length), LOW),
        V((items, length, length), LOW),
        V((length, length), F32),
        V((items, rows, length), LOW),
        V((groups, items, rows, 128), LOW),
        V((items, own, length), F32),
        V((items, 16, length), F32),
        V((items, rows, width, length), LOW),
        V((items, own, heads * width, length), LOW),
        V((items, half_own, chan, 2 * length), F32),
        V((items, half_own, 8, 2 * length), F32),
        V((items, half_own, chan, 2 * length), LOW),
        V((items, half_own, heads * unit, 2 * length), LOW),
        V((items, half_own, chan, 2 * length), LOW),
        V((items, own, nbins, length), F32),
        V((total * half_own * own, 2 * nbins), F32),
        V((items, total, half_own * own, 2 * nbins), LOW),
        V((items, total, half_own * own, 2 * nbins), LOW),
        V((total, half_own * own, 2 * nbins), F32),
        V((half_own, heads * unit, 2 * length), LOW),
        V((half_own, chan, 2 * length), F32),
        V((half_own, nbins, 2 * length), LOW),
        V((half_own, chan, 2 * length), F32),
        V((half_own, chan, 2 * length), LOW),
        V((half_own, chan, 2 * length), LOW),
        V((items, heads, own, width, length), LOW),
        V((items, rows, width, length), LOW),
        V((heads * width, chan), F32),
        V((heads * unit, chan), F32),
        V((heads * unit, chan), F32),
        V((nbins, chan), F32),
        V((1, length), F32),
        V((nbins, length), F32),
        V((heads, groups * block_rows, chan), F32),
        V((heads, groups * block_rows, chan), LOW),
        V((heads, groups * block_rows, chan), LOW),
        V((groups * block_rows, chan), F32),
        V((groups, block_rows, chan), F32),
        V((block_rows, chan), F32),
        V((length, length), F32),
        V((8, length, length), LOW),
        V((8, width, length), LOW),
        V((4 * width, 8 * length), LOW),
        V((items, length, length), LOW),
        V((items, groups, rows, length), LOW),
        V((4 * width, chan), F32),
        V((1, chan), F32),
        V((groups, sh, chan), F32),
        V((sh, chan), F32),
        V((8, chan), F32),
        V((total, 8, chan), F32),
    ]
    scratch += [
        dma((items, rows // 8)),
        dma((items, 2)),
        dma((2,)),
        dma((3, 2)),
        dma((items, 2)),
        dma((items, 2)),
        dma((items, 2)),
        dma((2,)),
        dma((2,)),
        dma((2,)),
        dma((items, 2)),
        dma((2,)),
        dma((2,)),
        dma((2,)),
    ]
    grads = pl.pallas_call(
        partial(step_kernel, groups, heads),
        out_shape=[
            jax.ShapeDtypeStruct((groups, sh, chan), F32),
            jax.ShapeDtypeStruct((groups, block_rows, chan), F32),
            jax.ShapeDtypeStruct((nbins, chan), F32),
            jax.ShapeDtypeStruct((8, chan), F32),
        ],
        in_specs=[pl.BlockSpec(memory_space=pl.ANY), pl.BlockSpec(memory_space=pltpu.SMEM)] + [vmem] * 8,
        out_specs=[vmem] * 4,
        scratch_shapes=scratch,
        compiler_params=pltpu.CompilerParams(
            collective_id=0, has_side_effects=True, vmem_limit_bytes=60 * 2**20
        ),
        name="step",
    )(pair_input, lengths, distogram_bins, *weights)
    like = lambda group: [jax.ShapeDtypeStruct(w.shape, F32) for w in group]
    outs = pl.pallas_call(
        partial(update_kernel, groups),
        out_shape=[jax.ShapeDtypeStruct((1, 1), F32)] * 2 + like(weights) * 3,
        in_specs=[vmem] * 25,
        out_specs=[vmem] * 23,
        name="update",
    )(*grads, *weights, *momenta, *averages)
    outs = list(outs)
    outs[0], outs[1] = outs[0].reshape(()), outs[1].reshape(())
    for k in (2, 9, 16):
        outs[k + 1] = outs[k + 1].reshape(chan, 1)
        outs[k + 5] = outs[k + 5].T
    return tuple(outs)


def body(groups, heads, *args):
    items, rows, length, channels = args[0].shape
    own = rows // heads
    if own == 8 and rows % 16 == 0 and length % 128 == 0:
        return fused_body(groups, heads, *args)
    return general_body(*args)


def solution(mesh):
    in_specs = (
        P(None, "res", None, None),
        P(),
        P(None, "res", None),
        P(None, "head"),
        P(None, "head"),
        P("head", None),
        P(None, "head"),
        P("head", None),
        P(),
        P(),
        P(None, "head"),
        P(None, "head"),
        P("head", None),
        P(None, "head"),
        P("head", None),
        P(),
        P(),
        P(None, "head"),
        P(None, "head"),
        P("head", None),
        P(None, "head"),
        P("head", None),
        P(),
        P(),
    )
    out_specs = (
        P(),
        P(),
        P(None, "head"),
        P(None, "head"),
        P("head", None),
        P(None, "head"),
        P("head", None),
        P(),
        P(),
        P(None, "head"),
        P(None, "head"),
        P("head", None),
        P(None, "head"),
        P("head", None),
        P(),
        P(),
        P(None, "head"),
        P(None, "head"),
        P("head", None),
        P(None, "head"),
        P("head", None),
        P(),
        P(),
    )
    return jax.shard_map(
        partial(body, mesh.shape["res"], mesh.shape["head"]), mesh=mesh, in_specs=in_specs, out_specs=out_specs, check_vma=False)
```

```python
from functools import partial

import jax
import jax.numpy as jnp
from jax import lax
from jax.experimental import pallas as pl
from jax.experimental.pallas import tpu as pltpu
from jax.sharding import PartitionSpec as P

EPS = 1e-05
NEG = -1000000000.0
MOMENTUM = 0.9
RATE = 20000.0
KEEP = 0.9
CLIP = 0.002


def project(values, weight):
    return jnp.einsum("rjc,cd->rjd", values, weight, preferred_element_type=jnp.float32)


def layer_norm(values, gain):
    center = values - jnp.mean(values, -1, keepdims=True)
    spread = jnp.mean(center * center, -1, keepdims=True)
    return center * lax.rsqrt(spread + EPS) * gain


def norm_back(values, gain, grad_out):
    result, pull = jax.vjp(layer_norm, values, gain)
    return pull(grad_out)


def row_scores(query, key, bias_full, penalty, scale):
    scores = jnp.dot(query, key.T, preferred_element_type=jnp.float32) * scale
    return scores + bias_full.astype(jnp.float32) + penalty[None, :]


def forward_row(bias_full, penalty, scale, row):
    query, key, value, gate = row
    scores = row_scores(query, key, bias_full, penalty, scale)
    peak = jnp.max(scores, -1, keepdims=True)
    expo = jnp.exp(scores - peak)
    summed = jnp.sum(expo, -1, keepdims=True)
    probs = (expo / summed).astype(jnp.bfloat16)
    mixed = jnp.dot(probs, value, preferred_element_type=jnp.float32)
    gated = (mixed * jax.nn.sigmoid(gate)).astype(jnp.bfloat16)
    return (gated, (peak + jnp.log(summed))[:, 0])


def backward_row(bias_full, penalty, scale, carry, row):
    query, key, value, gate, dgated, logsum = row
    scores = row_scores(query, key, bias_full, penalty, scale)
    exact = jnp.exp(scores - logsum[:, None])
    probs = exact.astype(jnp.bfloat16)
    mixed = jnp.dot(probs, value, preferred_element_type=jnp.float32)
    sigma = jax.nn.sigmoid(gate)
    dmixed = (dgated * sigma).astype(jnp.bfloat16)
    dgate = dgated * mixed * sigma * (1.0 - sigma)
    dvalue = jnp.dot(probs.T, dmixed, preferred_element_type=jnp.float32)
    dprobs = jnp.dot(dmixed, value.T, preferred_element_type=jnp.float32)
    inner = jnp.sum(dprobs * exact, -1, keepdims=True)
    dscores = (exact * (dprobs - inner)).astype(jnp.bfloat16)
    dquery = jnp.dot(dscores, key, preferred_element_type=jnp.float32) * scale
    dkey = jnp.dot(dscores.T, query, preferred_element_type=jnp.float32) * scale
    grads = jnp.concatenate([dquery, dkey, dvalue, dgate], -1)
    return (carry + dscores.astype(jnp.float32), grads)


def advance(weight, moment, average, grad):
    velocity = MOMENTUM * moment + grad
    fresh = weight - RATE * (grad + MOMENTUM * velocity)
    return (fresh, velocity, KEEP * average + (1.0 - KEEP) * fresh)


def general_body(
    pair_input,
    lengths,
    distogram_bins,
    head_proj,
    bias_proj,
    output_proj,
    expand_proj,
    reduce_proj,
    distogram_proj,
    small_params,
    momentum_head,
    momentum_bias,
    momentum_output,
    momentum_expand,
    momentum_reduce,
    momentum_distogram,
    momentum_small,
    average_head,
    average_bias,
    average_output,
    average_expand,
    average_reduce,
    average_distogram,
    average_small,
):
    weights = (
        head_proj,
        bias_proj,
        output_proj,
        expand_proj,
        reduce_proj,
        distogram_proj,
        small_params,
    )
    momenta = (
        momentum_head,
        momentum_bias,
        momentum_output,
        momentum_expand,
        momentum_reduce,
        momentum_distogram,
        momentum_small,
    )
    averages = (
        average_head,
        average_bias,
        average_output,
        average_expand,
        average_reduce,
        average_distogram,
        average_small,
    )
    head_w, bias_w, out_w, expand_w, reduce_w, dist_w = [
        w.astype(jnp.bfloat16) for w in weights[:6]
    ]
    items, rows, length, channels = pair_input.shape
    width = output_proj.shape[0]
    scale = width ** (-0.5)
    gain_one = small_params[:channels]
    gain_two = small_params[channels : 2 * channels]
    dist_bias = small_params[2 * channels :]
    positions = jnp.arange(length)
    first_row = lax.axis_index("res") * rows
    size_f = lengths.astype(jnp.float32)
    count = jnp.sum(size_f * size_f)
    grads = [jnp.zeros_like(w) for w in weights]
    loss_part = jnp.zeros((), jnp.float32)
    for item in range(items):
        live = (positions < lengths[item]).astype(jnp.float32)
        penalty = (1.0 - live) * NEG
        row_live = lax.dynamic_slice_in_dim(live, first_row, rows)
        start = pair_input[item].astype(jnp.float32)
        normed = layer_norm(start, gain_one).astype(jnp.bfloat16)
        proj = project(normed, head_w)
        query = proj[..., :width].astype(jnp.bfloat16)
        key = proj[..., width : 2 * width].astype(jnp.bfloat16)
        value = proj[..., 2 * width : 3 * width].astype(jnp.bfloat16)
        gate = proj[..., 3 * width :]
        bias_local = project(normed, bias_w)[..., 0].astype(jnp.bfloat16)
        bias_full = lax.all_gather(bias_local, "res", axis=0, tiled=True)
        gated, logsum = lax.map(
            partial(forward_row, bias_full, penalty, scale), (query, key, value, gate)
        )
        first = start + lax.psum(project(gated, out_w), "head")
        widened = layer_norm(first, gain_two).astype(jnp.bfloat16)
        pre = project(widened, expand_w)
        hidden = jnp.maximum(pre, 0.0).astype(jnp.bfloat16)
        second = first + lax.psum(project(hidden, reduce_w).astype(jnp.bfloat16), "head").astype(
            jnp.float32
        )
        second_low = second.astype(jnp.bfloat16)
        half = project(second_low, dist_w)
        mirror = lax.all_to_all(
            half.astype(jnp.bfloat16), "res", split_axis=1, concat_axis=0, tiled=True
        ).astype(half.dtype)
        logits = half + jnp.transpose(mirror, (1, 0, 2)) + dist_bias
        peak = jnp.max(logits, -1, keepdims=True)
        logp = logits - peak - jnp.log(jnp.sum(jnp.exp(logits - peak), -1, keepdims=True))
        onehot = (distogram_bins[item][:, :, None] == jnp.arange(logits.shape[2])).astype(
            jnp.float32
        )
        weight = (row_live[:, None] * live[None, :])[:, :, None]
        loss_part = loss_part - jnp.sum(logp * onehot * weight) / count
        dlogits = (jnp.exp(logp) - onehot) * weight / count
        back = lax.all_to_all(
            dlogits.astype(jnp.bfloat16), "res", split_axis=1, concat_axis=0, tiled=True
        ).astype(dlogits.dtype)
        dhalf = (dlogits + jnp.transpose(back, (1, 0, 2))).astype(jnp.bfloat16)
        grads[5] = grads[5] + jnp.einsum(
            "rjc,rjb->cb", second_low, dhalf, preferred_element_type=jnp.float32
        )
        dist_grad = jnp.sum(dlogits, (0, 1))
        dsecond = jnp.einsum("rjb,cb->rjc", dhalf, dist_w, preferred_element_type=jnp.float32)
        dtrans = dsecond.astype(jnp.bfloat16)
        grads[4] = grads[4] + jnp.einsum(
            "rjh,rjc->hc", hidden, dtrans, preferred_element_type=jnp.float32
        )
        dhidden = jnp.einsum("rjc,hc->rjh", dtrans, reduce_w, preferred_element_type=jnp.float32)
        dpre = jnp.where(pre > 0, dhidden, 0.0).astype(jnp.bfloat16)
        grads[3] = grads[3] + jnp.einsum(
            "rjc,rjh->ch", widened, dpre, preferred_element_type=jnp.float32
        )
        dwidened = lax.psum(
            jnp.einsum("rjh,ch->rjc", dpre, expand_w, preferred_element_type=jnp.float32).astype(
                jnp.bfloat16
            ),
            "head",
        ).astype(jnp.float32)
        dfirst_norm, gain_two_grad = norm_back(first, gain_two, dwidened)
        dout = (dsecond + dfirst_norm).astype(jnp.bfloat16)
        grads[2] = grads[2] + jnp.einsum(
            "rjd,rjc->dc", gated, dout, preferred_element_type=jnp.float32
        )
        dgated = jnp.einsum("rjc,dc->rjd", dout, out_w, preferred_element_type=jnp.float32)
        bias_terms, dproj = lax.scan(
            partial(backward_row, bias_full, penalty, scale),
            jnp.zeros((length, length), jnp.float32),
            (query, key, value, gate, dgated, logsum),
        )
        dproj = dproj.astype(jnp.bfloat16)
        dbias = lax.psum_scatter(bias_terms, "res", scatter_dimension=0, tiled=True).astype(
            jnp.bfloat16
        )
        grads[0] = grads[0] + jnp.einsum(
            "rjc,rjd->cd", normed, dproj, preferred_element_type=jnp.float32
        )
        grads[1] = (
            grads[1]
            + jnp.einsum("rjc,rj->c", normed, dbias, preferred_element_type=jnp.float32)[:, None]
        )
        dnormed_part = jnp.einsum("rjd,cd->rjc", dproj, head_w, preferred_element_type=jnp.float32)
        dnormed_part = dnormed_part + dbias.astype(jnp.float32)[:, :, None] * bias_w[:, 0].astype(
            jnp.float32
        )
        dnormed = lax.psum(dnormed_part.astype(jnp.bfloat16), "head").astype(jnp.float32)
        unused, gain_one_grad = norm_back(start, gain_one, dnormed)
        grads[6] = grads[6] + jnp.concatenate([gain_one_grad, gain_two_grad, dist_grad])
    summed = lax.psum(
        (grads[0], grads[1], grads[2], grads[3], grads[4], grads[5], grads[6], loss_part), "res"
    )
    total_grads = summed[:7]
    total_loss = summed[7]
    owned = jnp.zeros((), jnp.float32)
    for grad in total_grads[:5]:
        owned = owned + jnp.sum(grad * grad)
    shared = jnp.sum(total_grads[5] * total_grads[5]) + jnp.sum(total_grads[6] * total_grads[6])
    grad_norm = jnp.sqrt(shared + lax.psum(owned, "head"))
    factor = CLIP / jnp.maximum(grad_norm, CLIP)
    results = [
        advance(w, m, a, g * factor) for w, m, a, g in zip(weights, momenta, averages, total_grads)
    ]
    new_w = [r[0] for r in results]
    new_m = [r[1] for r in results]
    new_a = [r[2] for r in results]
    return (
        total_loss,
        grad_norm,
        new_w[0],
        new_w[1],
        new_w[2],
        new_w[3],
        new_w[4],
        new_w[5],
        new_w[6],
        new_m[0],
        new_m[1],
        new_m[2],
        new_m[3],
        new_m[4],
        new_m[5],
        new_m[6],
        new_a[0],
        new_a[1],
        new_a[2],
        new_a[3],
        new_a[4],
        new_a[5],
        new_a[6],
    )


NT = (((1,), (1,)), ((), ()))
NN = (((1,), (0,)), ((), ()))
F32 = jnp.float32
LOW = jnp.bfloat16
LOG2E = 1.4426950408889634


def dot(left, right, dims=NN):
    return lax.dot_general(left, right, dims, preferred_element_type=F32)


def iota(shape, dim):
    return lax.broadcasted_iota(jnp.int32, shape, dim)


def eye(size):
    return (iota((size, size), 0) == iota((size, size), 1)).astype(F32).astype(LOW)


def sigmoid(x):
    return 0.5 * jnp.tanh(0.5 * x) + 0.5


def staged(count, stages, lag):
    for step in range(count + lag * (len(stages) - 1)):
        for k, stage in enumerate(stages):
            if 0 <= step - k * lag < count:
                stage(step - k * lag)


def step_kernel(groups, heads, *refs):
    (
        pair_hbm, lengths, bins, head_w, bias_w, out_w, exp_w, red_w, dist_w, small,
        o_head, o_block, o_dist, o_small,
        pair, normed, tok, qkv, sig, expo, mixed, rinv,
        wc, wt, we, wet, wr, wrt, wo, wot, wd, wdt, gain_col, dist_col, sel_a, sel_b,
        bias_f, bias_send, bias_all, bias_t, bins_low, bins_in, bins_own, bins_t,
        gated, gall, xhat, rstd, widened, hidden, slow, halves, pack_f, half_send, half_in, mirror,
        dpre_s, first_s, dh_s, dsec_s, dtr_s, dout_s, dg_send, dg_in,
        g_out, g_red, g_exp, g_dist, loss_acc, dist_acc,
        block_own, core_send, core_in, core_sum, block_send, block_in, part_own, part_in, block_sum, block_low,
        db_acc, ds_s, dm_s, dproj_s, db_send, db_in, g_head, g_bias, head_in, head_low, card, card_in,
        sem_pair, sem_bias, sem_bins, sem_w, sem_gat, sem_half, sem_dg,
        sem_core, sem_blk, sem_part, sem_gath, sem_db, sem_head, sem_card, sem_fin,
    ) = refs
    items, rows, length, chan = pair.shape
    group_rows = 8
    width = out_w.shape[0]
    nbins = dist_w.shape[0]
    unit = exp_w.shape[1]
    own = rows // heads
    half_own = own // 2
    total = groups * heads
    scale = width ** (-0.5)
    my_r = lax.axis_index("res")
    my_h = lax.axis_index("head")
    me = my_r * heads + my_h

    def device(r, h):
        return {"res": r, "head": h}

    def send(src, dst, sem, r, h):
        return pltpu.make_async_remote_copy(
            src_ref=src, dst_ref=dst, send_sem=sem.at[0], recv_sem=sem.at[1],
            device_id=device(r, h), device_id_type=pl.DeviceIdType.MESH,
        )

    def res_peer(o):
        return lax.rem(my_r + o, groups)

    def head_peer(o):
        flip, cross = o // 2 % 2, (o + 1) // 2 % 2
        return lax.rem(my_h + flip * (1 - 2 * lax.rem(my_h, 2)) + 2 * cross, heads)

    def any_peer(o):
        d = lax.rem(me + o, total)
        return d, d // heads, lax.rem(d, heads)

    def start(count, make):
        def one(o, carry):
            make(o).start()
            return carry
        lax.fori_loop(1, count, one, 0)

    def wait_in(ref, sem):
        send(ref, ref, sem, res_peer(1), my_h).wait_recv()

    def wait_out(ref, sem):
        send(ref, ref, sem, res_peer(1), my_h).wait_send()

    def load(item, t):
        at = pl.ds(t * group_rows, group_rows)
        return pltpu.make_async_copy(pair_hbm.at[item, at], pair.at[item, at], sem_pair.at[item, t])

    barrier = pltpu.get_barrier_semaphore()

    def greet(o, carry):
        d, r, h = any_peer(o)
        pl.semaphore_signal(barrier, inc=1, device_id=device(r, h), device_id_type=pl.DeviceIdType.MESH)
        return carry

    lax.fori_loop(1, total, greet, 0)

    for item in range(items):
        for t in range(rows // group_rows):
            load(item, t).start()

    brow = bias_w[...].astype(LOW).astype(F32)
    gain_one = small[0:chan].reshape(1, chan)
    gain_two = small[chan : 2 * chan].reshape(1, chan)
    ident = eye(chan)
    ident_l = eye(length)
    center_by = (ident.astype(F32) - 1.0 / chan).astype(LOW)
    one_lane = (iota((1, 4 * width), 1) >= 3 * width).astype(F32)

    def prepare_first():
        hw = head_w[...]
        wc[0 : 4 * width] = jnp.transpose(hw).astype(LOW)
        wc[4 * width :] = jnp.where(iota((16, chan), 0) == 0, brow, 0.0).astype(LOW)
        src_col = iota((4 * width, 4 * width), 0)
        dst_col = iota((4 * width, 4 * width), 1)
        want = jnp.where(
            dst_col < width, dst_col + width, jnp.where(dst_col < 3 * width, dst_col, -1)
        )
        wt[...] = dot(hw.astype(LOW), (src_col == want).astype(F32).astype(LOW)).astype(LOW)

    def prepare_weights():
        we[:, pl.ds(pl.multiple_of(my_h * unit, unit), unit)] = exp_w[...].astype(LOW)
        wr[pl.ds(pl.multiple_of(my_h * unit, unit), unit), :] = red_w[...].astype(LOW)
        wo[pl.ds(pl.multiple_of(my_h * width, width), width), :] = out_w[...].astype(LOW)

    def prepare_rest():
        bins_row = jnp.concatenate(
            [small[2 * chan : 2 * chan + nbins].reshape(1, nbins), jnp.zeros((1, chan - nbins), F32)], 1
        )
        gain_col[...] = jnp.transpose(jnp.broadcast_to(gain_two, (chan, chan)))
        dist_col[...] = jnp.transpose(jnp.broadcast_to(bins_row, (chan, chan)))[:nbins]
        wdt[...] = dist_w[...].astype(LOW)
        wd[...] = dot(ident, wdt[...], NT).astype(LOW)
        bins_low[...] = bins[...].astype(F32).astype(LOW)
        bins_own[...] = bins[:, pl.ds(pl.multiple_of(my_h * own, own), own), :].astype(F32)
        sel_row = iota((total * half_own, length), 0)
        sel_col = iota((total * half_own, length), 1)
        sel_at = sel_row // half_own * own + lax.rem(sel_row, half_own)
        sel_a[...] = (sel_col == sel_at).astype(F32).astype(LOW)
        sel_b[...] = (sel_col == sel_at + half_own).astype(F32).astype(LOW)
        for ref in (g_out, g_red, g_exp, g_dist, loss_acc, dist_acc, g_head, g_bias, db_acc):
            ref[...] = jnp.zeros_like(ref)

    def before(item):
        def norm(r):
            center = dot(pair[item, r], center_by)
            spread = jnp.mean(center * center, -1, keepdims=True)
            normed[item, r] = (center * lax.rsqrt(spread + EPS) * gain_one).astype(LOW)

        def mult(r):
            low = normed[item, r]
            ch = dot(wc[...], low, NT)
            qkv[item, r] = ch[: 3 * width].astype(LOW)
            sig[item, r] = sigmoid(ch[3 * width : 4 * width])
            bias_f[pl.ds(r, 1), :] = ch[4 * width : 4 * width + 1]
            tok[item, r] = (dot(low, wt[...]) + one_lane).astype(LOW)

        def group(t, carry):
            load(item, t).wait()
            for k in range(8 + 8):
                if k < 8:
                    norm(t * 8 + k)
                if k >= 8:
                    mult(t * 8 + k - 8)
            return carry
        lax.fori_loop(0, rows // 8, group, 0)
        bias_send[item] = bias_f[...].astype(LOW)
        bias_all[item, pl.ds(pl.multiple_of(my_r * rows, rows), rows), :] = bias_f[...].astype(LOW)

    def bias_copy(item):
        def make(o):
            return send(
                bias_send.at[item],
                bias_all.at[item, pl.ds(pl.multiple_of(my_r * rows, rows), rows), :],
                sem_bias.at[item], res_peer(o), my_h,
            )
        return make

    def bins_block(r):
        return pl.ds(pl.multiple_of((r * rows) // 128 * 128, 128), 128)

    def bins_copy(o):
        return send(
            bins_low.at[:, :, bins_block(res_peer(o))], bins_in.at[my_r],
            sem_bins, res_peer(o), my_h,
        )

    def we_copy(o):
        at = (slice(None), pl.ds(pl.multiple_of(my_h * unit, unit), unit))
        return send(we.at[at], we.at[at], sem_w.at[0], my_r, head_peer(o))

    def wr_copy(o):
        at = pl.ds(pl.multiple_of(my_h * unit, unit), unit)
        return send(wr.at[at], wr.at[at], sem_w.at[1], my_r, head_peer(o))

    def wo_copy(o):
        at = pl.ds(pl.multiple_of(my_h * width, width), width)
        return send(wo.at[at], wo.at[at], sem_w.at[2], my_r, head_peer(o))

    def gated_copy(item):
        def make(o):
            p = head_peer(o)
            return send(
                gated.at[item, pl.ds(p * own, own)],
                gall.at[item, :, pl.ds(pl.multiple_of(my_h * width, width), width), :],
                sem_gat.at[item], my_r, p,
            )
        return make

    def attend(item):
        live = iota((length, length), 0) < lengths[item]
        bt = dot(ident_l, bias_all[item], NT) * LOG2E
        bias_t[...] = bt + jnp.where(live, 0.0, NEG * LOG2E)

        def scores(r):
            q = qkv[item, r, 0:width].astype(F32) * (scale * LOG2E)
            hi = q.astype(LOW)
            lo = (q - hi.astype(F32)).astype(LOW)
            rhs = jnp.concatenate([hi, lo, jnp.zeros((2 * width, length), LOW)], 0)
            s = dot(tok[item, r], rhs) + bias_t[...]
            expo[item, r] = jnp.exp2(s - jnp.max(s, 0, keepdims=True)).astype(LOW)

        def gather(r):
            lhs = jnp.concatenate(
                [qkv[item, r, 2 * width : 3 * width], jnp.ones((16, length), LOW)], 0
            )
            o = dot(lhs, expo[item, r])
            inv = 1.0 / o[width : width + 1]
            rinv[item, pl.ds(r, 1), :] = inv
            m = o[:width] * inv
            mixed[item, r] = m
            gated[item, r] = (m * sig[item, r]).astype(LOW)

        def chunk(o, carry):
            p = head_peer(o)
            base = p * own

            def one(t, c):
                for k in range(8 + 4):
                    if k < 8:
                        scores(base + t * 8 + k)
                    if k >= 4:
                        gather(base + t * 8 + k - 4)
                return c
            lax.fori_loop(0, own // 8, one, 0, unroll=1)

            @pl.when(o < heads)
            def _():
                gated_copy(item)(o).start()
            return carry
        lax.fori_loop(1, heads + 1, chunk, 0)
        gall[item, :, pl.ds(pl.multiple_of(my_h * width, width), width), :] = gated[
            item, pl.ds(my_h * own, own)
        ]

    def pair_of(ref, item, t):
        return jnp.concatenate([ref[item, t], ref[item, t + half_own]], 1)

    def forward(item):
        gc = jnp.concatenate([gain_col[...]] * (2 * length // chan), 1)
        zero = jnp.zeros((nbins, length), LOW)

        def enter(t):
            g2 = pair_of(gall, item, t)
            base = my_h * own + t
            first = jnp.concatenate(
                [dot(ident, pair[item, base], NT), dot(ident, pair[item, base + half_own], NT)], 1
            ) + dot(wot[...], g2)
            first_s[t] = first
            center = first - jnp.mean(first, 0, keepdims=True)
            rs = lax.rsqrt(jnp.mean(center * center, 0, keepdims=True) + EPS)
            xh = center * rs
            xhat[item, t] = xh
            rstd[item, t] = jnp.broadcast_to(rs, (8, 2 * length))
            widened[item, t] = (xh * gc).astype(LOW)

        def expand(t):
            for b in range(heads):
                hidden[item, t, b * unit : (b + 1) * unit] = jnp.maximum(
                    dot(wet[b * unit : (b + 1) * unit], widened[item, t]), 0.0
                ).astype(LOW)

        def reduce(t):
            slow[item, t] = (first_s[t] + dot(wrt[...], hidden[item, t])).astype(LOW)

        def project_half(t):
            half = dot(wdt[...], slow[item, t])
            halves[item, t] = half[:, :length]
            halves[item, t + half_own] = half[:, length:]

        def pack(t):
            for k in range(2):
                part = halves[item, t + k * half_own].astype(LOW)
                packed = dot(sel_a[...], jnp.concatenate([part, zero], 0), NT) + dot(
                    sel_b[...], jnp.concatenate([zero, part], 0), NT
                )
                pack_f[pl.ds(t + k * half_own, total * half_own, own), :] = packed

        staged(half_own, (enter, expand, reduce, project_half, pack), 2)
        half_send[item] = pack_f[...].reshape(half_send.shape[1:]).astype(LOW)
        half_in[item, me] = half_send[item, me]

    def half_copy(item):
        def make(o):
            d, r, h = any_peer(o)
            return send(
                half_send.at[item, d], half_in.at[item, me],
                sem_half.at[item], r, h,
            )
        return make

    size_sum = jnp.zeros((1, length), F32)
    for item in range(items):
        size = lengths[item]
        size_sum = size_sum + (jnp.zeros((1, length), jnp.int32) + size * size).astype(F32)

    def backward(item):
        mirror[...] = half_in[item].astype(F32)
        live = (iota((1, length), 1) < lengths[item]).astype(F32) / size_sum
        levels = iota((nbins, length), 0).astype(F32)[None]

        gc = jnp.concatenate([gain_col[...]] * (2 * length // chan), 1)
        dist_c = jnp.concatenate([dist_col[...]] * (length // chan), 1)[None]

        def two(ref, t):
            return jnp.concatenate(
                [ref[item, pl.ds(t, 1), :][None], ref[item, pl.ds(t + half_own, 1), :][None]], 0
            )

        def loss_grad(t):
            flip = mirror[:, t * own : (t + 1) * own, :].reshape(length, 2 * nbins)
            flip = dot(eye(2 * nbins), flip.astype(LOW), NT)
            here = jnp.concatenate([halves[item, t], halves[item, t + half_own]], 0)
            logits = (here + flip).reshape(2, nbins, length) + dist_c
            peak = jnp.max(logits, 1, keepdims=True)
            ex = jnp.exp(logits - peak)
            tot = jnp.sum(ex, 1, keepdims=True)
            prob = ex * (1.0 / tot)
            hot = (two(bins_own, t) == levels).astype(F32)
            hot_t = (two(bins_t, t) == levels).astype(F32)
            at = me * own + t + iota((2, 1, length), 0) * half_own
            weight = jnp.where(at < lengths[item], 1.0, 0.0) * live[None]
            picked = jnp.sum(hot * logits, 1, keepdims=True)
            lost = weight * (peak + jnp.log(tot) - picked)
            loss_acc[...] += lost[0] + lost[1]
            short = prob - hot
            dl = short * weight
            dist_acc[...] += dl[0] + dl[1]
            dh = ((short + prob - hot_t) * weight).astype(LOW)
            dh_s[t] = jnp.concatenate([dh[0], dh[1]], 1)

        def enter(t):
            dsec = dot(wd[...], dh_s[t])
            dsec_s[t] = dsec
            dtr_s[t] = dsec.astype(LOW)
            g_dist[...] += dot(dh_s[t], slow[item, t], NT)

        def through(t):
            for b in range(heads):
                at_b = slice(b * unit, (b + 1) * unit)
                hid = hidden[item, t, at_b]
                dpre_s[t, at_b] = jnp.where(
                    hid.astype(F32) > 0.0, dot(wr[at_b], dtr_s[t]), 0.0
                ).astype(LOW)

        def weights_back(t):
            for b in range(heads):
                at_b = slice(b * unit, (b + 1) * unit)
                g_red[at_b] += dot(hidden[item, t, at_b], dtr_s[t], NT)
                g_exp[at_b] += dot(dpre_s[t, at_b], widened[item, t], NT)

        def leave(t):
            dxh = dot(we[...], dpre_s[t]) * gc
            xh = xhat[item, t]
            m1 = jnp.mean(dxh, 0, keepdims=True)
            m2 = jnp.mean(dxh * xh, 0, keepdims=True)
            dout_s[t] = (dsec_s[t] + rstd[item, t, 0:1] * (dxh - m1 - xh * m2)).astype(LOW)

        def output_back(t):
            dg = dot(wo[...], dout_s[t]).astype(LOW)
            for h in range(heads):
                for k in range(2):
                    dg_send[item, h, t + k * half_own] = dg[
                        h * width : (h + 1) * width, k * length : (k + 1) * length
                    ]
            g_out[...] += dot(pair_of(gall, item, t), dout_s[t], NT)

        staged(half_own, (loss_grad, enter, through, weights_back, leave, output_back), 2)
        dg_in[item, pl.ds(my_h * own, own)] = dg_send[item, my_h]

    def dg_copy(item):
        def make(o):
            p = head_peer(o)
            return send(
                dg_send.at[item, p], dg_in.at[item, pl.ds(my_h * own, own)],
                sem_dg.at[item, o // (heads - 1)], my_r, p,
            )
        return make

    def attend_back(item, first_o, last_o):
        tail_row = iota((16, length), 0)

        def first(r, k, tot):
            s = sig[item, r]
            m = mixed[item, r]
            dg = dg_in[item, r].astype(F32)
            dm = (dg * s * rinv[item, pl.ds(r, 1), :]).astype(LOW)
            inner = -jnp.sum(dm.astype(F32) * m, 0, keepdims=True)
            hi = inner.astype(LOW).astype(F32)
            lo = inner - hi
            tail = jnp.where(tail_row == 0, hi, jnp.where(tail_row == 1, lo, 0.0)).astype(LOW)
            rhs = jnp.concatenate(
                [jnp.zeros((2 * width, length), LOW), dm, tail, jnp.zeros((width - 16, length), LOW)], 0
            )
            dm_s[k] = dm
            dproj_s[3 * width :, k * length : (k + 1) * length] = (dg * m * s * (1.0 - s)).astype(LOW)
            ds = expo[item, r].astype(F32) * dot(tok[item, r], rhs)
            db_acc[item] += ds
            ds_s[k] = ds.astype(LOW)
            return None

        def second(r, k):
            at = slice(k * length, (k + 1) * length)
            ds = ds_s[k]
            dproj_s[0:width, at] = (dot(qkv[item, r, width : 2 * width], ds) * scale).astype(LOW)
            dproj_s[width : 2 * width, at] = (dot(qkv[item, r, 0:width], ds, NT) * scale).astype(LOW)
            dproj_s[2 * width : 3 * width, at] = dot(dm_s[k], expo[item, r], NT).astype(LOW)

        def group(o, carry):
            t = head_peer(o)
            tot = None
            for k in range(8 + 4):
                if k < 8:
                    tot = first(t * 8 + k, k, tot)
                if k >= 4:
                    second(t * 8 + k - 4, k - 4)
            g_head[...] += dot(dproj_s[...], normed[item, pl.ds(t * 8, 8)].reshape(8 * length, chan))
            return carry
        lax.fori_loop(first_o, last_o, group, 0)

    def pair_bias_back(item):
        db_send[item] = dot(ident_l, db_acc[item].astype(LOW), NT).astype(LOW)
        db_in[item, my_r] = db_send[item, pl.ds(pl.multiple_of(my_r * rows, rows), rows), :]

    def db_copy(item):
        def make(o):
            p = res_peer(o)
            return send(
                db_send.at[item, pl.ds(pl.multiple_of(p * rows, rows), rows), :], db_in.at[item, my_r],
                sem_db.at[item], p, my_h,
            )
        return make

    def bias_back(item):
        db = db_in[item, 0].astype(F32)
        for s in range(1, groups):
            db = db + db_in[item, s].astype(F32)
        db = db.astype(LOW).astype(F32)
        at = iota((8, length), 0)
        acc = jnp.zeros((8, chan), F32)
        for g in range(rows // 8):
            part = db[8 * g : 8 * g + 8]
            spread = jnp.concatenate([jnp.where(at == q, part, 0.0) for q in range(8)], 1)
            acc = acc + dot(
                spread.astype(LOW), normed[item, 8 * g : 8 * g + 8].reshape(8 * length, chan)
            )
        g_bias[...] += jnp.sum(acc, 0, keepdims=True)

    ru, rw, rb = unit // groups, width // groups, nbins // total
    piece = 2 * ru + 8

    side, mate = my_h // 2, lax.rem(my_h, 2)

    def core_copy():
        return send(core_send, core_in, sem_core, my_r, head_peer(heads - 1))

    def block_copy(o):
        p = res_peer(o)
        return send(block_send.at[p], block_in.at[my_r], sem_blk, p, my_h)

    def part_copy():
        at = pl.ds(pl.multiple_of((1 - side) * piece, 8), piece)
        return send(part_own.at[at, :], part_in, sem_part, my_r, head_peer(1))

    def gather_copy(o):
        return send(block_low, o_block.at[my_r], sem_gath, res_peer(o), my_h)

    def block_make():
        for r in range(groups):
            for h in range(heads):
                c, base = h % 2, h // 2 * piece
                at = h * unit + r * ru
                block_own[c, r, base : base + ru] = g_red[at : at + ru]
                block_own[c, r, base + ru : base + 2 * ru] = g_exp[at : at + ru]
                at = h * width + r * rw
                base += 2 * ru
                block_own[c, r, base : base + rw] = g_out[at : at + rw]
                at = (r * heads + h) * rb
                block_own[c, r, base + rw : base + rw + rb] = g_dist[at : at + rb]
                block_own[c, r, base + rw + rb : base + 8] = jnp.zeros((8 - rw - rb, chan), F32)
        core_send[...] = block_own[1 - mate].astype(LOW)

    def core_add():
        both = block_own[mate] + core_in[...].astype(F32)
        core_sum[...] = both
        block_send[...] = both.astype(LOW)

    def part_make():
        acc = core_sum[my_r]
        for o in range(1, groups):
            acc = acc + block_in[res_peer(o)].astype(F32)
        part_own[...] = acc

    def block_add():
        acc = part_own[pl.ds(pl.multiple_of(side * piece, 8), piece), :] + part_in[...]
        block_sum[...] = acc
        low = jnp.concatenate([acc, jnp.zeros((8, chan), F32)], 0).astype(LOW)
        block_low[...] = low
        o_block[my_r] = low

    def head_copy(o):
        p = res_peer(o)
        return send(
            g_head.at[pl.ds(pl.multiple_of(p * (4 * width // groups), 4 * width // groups), 4 * width // groups), :],
            head_in.at[my_r], sem_head, p, my_h,
        )

    def card_copy(o):
        d, r, h = any_peer(o)
        return send(card, card_in.at[me], sem_card, r, h)

    def fin_copy(o):
        return send(head_low, o_head.at[my_r], sem_fin, res_peer(o), my_h)

    all_but = lambda ref, item, count: ref.at[item, pl.ds(0, count)]
    bias_part = lambda item: all_but(bias_all, item, (groups - 1) * rows)
    gat_part = lambda item: all_but(gated, item, (heads - 1) * own)
    dg_near = lambda item: all_but(dg_in, item, own)
    dg_far = lambda item: all_but(dg_in, item, (heads - 2) * own)
    half_part = lambda item: all_but(half_in, item, total - 1)
    db_part = lambda item: all_but(db_in, item, groups - 1)
    bins_part = bins_in.at[pl.ds(0, groups - 1)]
    w_parts = (
        we.at[:, pl.ds(0, (heads - 1) * unit)], wr.at[pl.ds(0, (heads - 1) * unit)],
        wo.at[pl.ds(0, (heads - 1) * width)],
    )
    blk_part = block_in.at[pl.ds(0, groups - 1)]
    gath_part = o_block.at[pl.ds(0, groups - 1)]
    head_part = head_in.at[pl.ds(0, groups - 1)]
    fin_part = o_head.at[pl.ds(0, groups - 1)]
    card_part = card_in.at[pl.ds(0, total - 1)]

    prepare_first()
    before(0)
    pl.semaphore_wait(barrier, total - 1)
    start(groups, bias_copy(0))
    prepare_weights()
    for make in (we_copy, wr_copy, wo_copy):
        start(heads, make)
    for item in range(1, items):
        before(item)
        start(groups, bias_copy(item))
    prepare_rest()
    bins_in[my_r] = bins_low[:, :, bins_block(my_r)]
    for item in range(items):
        wait_in(bias_part(item), sem_bias.at[item])
        attend(item)
        if item == 0:
            start(groups, bins_copy)
    for k in range(3):
        wait_in(w_parts[k], sem_w.at[k])
    for b in range(heads):
        at = slice(b * unit, (b + 1) * unit)
        wet[at] = dot(ident, we[:, at], NT).astype(LOW)
        wrt[:, at] = dot(ident, wr[at], NT).astype(LOW)
    wot[...] = dot(ident, wo[...], NT).astype(LOW)
    for item in range(items):
        wait_in(gat_part(item), sem_gat.at[item])
        forward(item)
        start(total, half_copy(item))
    wait_in(bins_part, sem_bins)
    lane = my_r * rows + my_h * own - (my_r * rows) // 128 * 128
    pick = (iota((16, 128), 1) == iota((16, 128), 0) + lane).astype(F32).astype(LOW)
    for item in range(items):
        bins_t[item] = dot(pick, bins_in[:, item].reshape(groups * rows, 128), NT)
    last = items - 1
    for item in range(items):
        wait_in(half_part(item), sem_half.at[item])
        backward(item)
        start(heads, dg_copy(item))
        if item == last:
            block_make()
            core_copy().start()
        wait_in(dg_near(item), sem_dg.at[item, 1])
        attend_back(item, heads - 1, heads + 1)
    wait_in(core_in, sem_core)
    core_add()
    start(groups, block_copy)
    for item in range(items):
        wait_in(dg_far(item), sem_dg.at[item, 0])
        attend_back(item, 1, heads - 1)
        pair_bias_back(item)
        start(groups, db_copy(item))
    start(groups, head_copy)
    sh = 4 * width // groups
    head_in[my_r] = g_head[pl.ds(pl.multiple_of(my_r * sh, sh), sh), :]
    wait_in(blk_part, sem_blk)
    part_make()
    part_copy().start()
    for item in range(last):
        wait_in(db_part(item), sem_db.at[item])
        bias_back(item)
    wait_in(head_part, sem_head)
    acc = head_in[0]
    for r in range(1, groups):
        acc = acc + head_in[r]
    head_low[...] = acc.astype(LOW)
    o_head[my_r] = acc.astype(LOW)
    wait_in(part_in, sem_part)
    block_add()
    start(groups, fin_copy)
    start(groups, gather_copy)
    up_one = jnp.sum(wc[0 : 4 * width].astype(F32) * g_head[...], 0, keepdims=True)
    up_two = jnp.sum(wet[...].astype(F32) * g_exp[...], 0, keepdims=True)
    dacc = dist_acc[:, 0:chan]
    lacc = loss_acc[:, 0:chan]
    for k in range(1, length // chan):
        dacc = dacc + dist_acc[:, k * chan : (k + 1) * chan]
        lacc = lacc + loss_acc[:, k * chan : (k + 1) * chan]
    dacc = jnp.transpose(jnp.concatenate([dacc, jnp.zeros((chan - nbins, chan), F32)], 0))
    blocks = block_sum[...]
    card[2:3] = up_two / gain_two
    card[3:4] = jnp.sum(dacc, 0, keepdims=True)
    card[4:5] = lacc
    card[5:6] = jnp.sum(acc * acc, 0, keepdims=True) + jnp.sum(blocks * blocks, 0, keepdims=True)
    card[6:8] = blocks[2 * ru + rw : 2 * ru + rw + rb]
    wait_in(db_part(last), sem_db.at[last])
    bias_back(last)
    gb = g_bias[...]
    card[0:1] = gb
    card[1:2] = (up_one + brow * gb) / gain_one
    card_in[me] = card[...]
    start(total, card_copy)
    wait_in(card_part, sem_card)
    by_head = [card_in[h] for h in range(heads)]
    for r in range(1, groups):
        by_head = [a + card_in[r * heads + h] for h, a in enumerate(by_head)]
    every = by_head[0]
    bias_sq = by_head[0] * by_head[0]
    for a in by_head[1:]:
        every = every + a
        bias_sq = bias_sq + a * a
    norm_sq = every[5:6] + bias_sq[0:1]
    for k in (1, 2, 3):
        norm_sq = norm_sq + every[k : k + 1] * every[k : k + 1]
    norm = jnp.sqrt(jnp.sum(norm_sq, -1, keepdims=True))
    o_small[...] = every
    mine = card_in[my_h]
    for r in range(1, groups):
        mine = mine + card_in[r * heads + my_h]
    o_small[0:1] = mine[0:1]
    o_small[4:5] = jnp.broadcast_to(jnp.sum(every[4:5], -1, keepdims=True), (1, chan))
    o_small[5:6] = jnp.broadcast_to(norm, (1, chan))
    o_small[6:7] = jnp.broadcast_to(CLIP / jnp.maximum(norm, CLIP), (1, chan))
    for d in range(total):
        o_dist[d * rb : (d + 1) * rb] = card_in[d, 6 : 6 + rb]
    wait_in(gath_part, sem_gath)
    wait_in(fin_part, sem_fin)
    for item in range(items):
        wait_out(bias_part(item), sem_bias.at[item])
        wait_out(gat_part(item), sem_gat.at[item])
        wait_out(half_part(item), sem_half.at[item])
        wait_out(dg_far(item), sem_dg.at[item, 0])
        wait_out(dg_near(item), sem_dg.at[item, 1])
        wait_out(db_part(item), sem_db.at[item])
    for k in range(3):
        wait_out(w_parts[k], sem_w.at[k])
    for ref, sem in (
        (bins_part, sem_bins), (core_in, sem_core), (blk_part, sem_blk), (part_in, sem_part), (gath_part, sem_gath),
        (head_part, sem_head), (fin_part, sem_fin), (card_part, sem_card),
    ):
        wait_out(ref, sem)


def update_kernel(groups, *refs):
    g_head, g_block, g_dist, g_small = refs[:4]
    weights, momenta, averages = refs[4:11], refs[11:18], refs[18:25]
    loss, norm = refs[25:27]
    new_w, new_m, new_a = refs[27:34], refs[34:41], refs[41:48]
    loss[...] = g_small[4:5, 0:1]
    norm[...] = g_small[5:6, 0:1]
    factor = g_small[6:7, 0:1]
    unit = weights[4].shape[0]
    width = weights[2].shape[0]
    ru, rw = unit // groups, width // groups
    chan = g_small.shape[1]

    def put(k, grad, at=(slice(None), slice(None))):
        fresh, velocity, average = advance(
            weights[k][at], momenta[k][at], averages[k][at], grad * (factor if grad.ndim > 1 else factor[0])
        )
        new_w[k][at] = fresh
        new_m[k][at] = velocity
        new_a[k][at] = average

    put(0, jnp.transpose(g_head[...].astype(F32).reshape(weights[0].shape[1], chan)))
    put(1, g_small[0:1])
    block = g_block[...].astype(F32)
    put(3, jnp.transpose(block[:, ru : 2 * ru].reshape(unit, chan)))
    put(4, block[:, 0:ru].reshape(unit, chan))
    for r in range(groups):
        put(2, block[r, 2 * ru : 2 * ru + rw], (slice(r * rw, (r + 1) * rw), slice(None)))
    nbins = weights[5].shape[0]
    put(5, g_dist[...])
    put(6, g_small[1], (slice(0, chan),))
    put(6, g_small[2], (slice(chan, 2 * chan),))
    put(6, g_small[3, 0:nbins], (slice(2 * chan, 2 * chan + nbins),))


def fused_body(groups, heads, *args):
    pair_input, lengths, distogram_bins = args[:3]
    weights, momenta, averages = list(args[3:10]), list(args[10:17]), list(args[17:24])
    items, rows, length, chan = pair_input.shape
    width = weights[2].shape[0]
    unit = weights[3].shape[1]
    nbins = weights[5].shape[1]
    own, total = rows // heads, groups * heads
    half_own = own // 2
    for group in (weights, momenta, averages):
        group[1] = group[1].reshape(1, chan)
        group[5] = group[5].T
    vmem = pl.BlockSpec(memory_space=pltpu.VMEM)
    block_rows = 2 * (unit // groups) + 8
    sh = 4 * width // groups
    V = pltpu.VMEM
    dma = pltpu.SemaphoreType.DMA
    scratch = [
        V((items, rows, length, chan), LOW),
        V((items, rows, length, chan), LOW),
        V((items, rows, length, 4 * width), LOW),
        V((items, rows, 3 * width, length), LOW),
        V((items, rows, width, length), F32),
        V((items, rows, length, length), LOW),
        V((items, rows, width, length), F32),
        V((items, rows, length), F32),
        V((4 * width + 16, chan), LOW),
        V((chan, 4 * width), LOW),
        V((chan, heads * unit), LOW),
        V((heads * unit, chan), LOW),
        V((heads * unit, chan), LOW),
        V((chan, heads * unit), LOW),
        V((heads * width, chan), LOW),
        V((chan, heads * width), LOW),
        V((chan, nbins), LOW),
        V((nbins, chan), LOW),
        V((chan, chan), F32),
        V((nbins, chan), F32),
        V((total * half_own, length), LOW),
        V((total * half_own, length), LOW),
        V((rows, length), F32),
        V((items, rows, length), LOW),
        V((items, length, length), LOW),
        V((length, length), F32),
        V((items, rows, length), LOW),
        V((groups, items, rows, 128), LOW),
        V((items, own, length), F32),
        V((items, 16, length), F32),
        V((items, rows, width, length), LOW),
        V((items, own, heads * width, length), LOW),
        V((items, half_own, chan, 2 * length), F32),
        V((items, half_own, 8, 2 * length), F32),
        V((items, half_own, chan, 2 * length), LOW),
        V((items, half_own, heads * unit, 2 * length), LOW),
        V((items, half_own, chan, 2 * length), LOW),
        V((items, own, nbins, length), F32),
        V((total * half_own * own, 2 * nbins), F32),
        V((items, total, half_own * own, 2 * nbins), LOW),
        V((items, total, half_own * own, 2 * nbins), LOW),
        V((total, half_own * own, 2 * nbins), F32),
        V((half_own, heads * unit, 2 * length), LOW),
        V((half_own, chan, 2 * length), F32),
        V((half_own, nbins, 2 * length), LOW),
        V((half_own, chan, 2 * length), F32),
        V((half_own, chan, 2 * length), LOW),
        V((half_own, chan, 2 * length), LOW),
        V((items, heads, own, width, length), LOW),
        V((items, rows, width, length), LOW),
        V((heads * width, chan), F32),
        V((heads * unit, chan), F32),
        V((heads * unit, chan), F32),
        V((nbins, chan), F32),
        V((1, length), F32),
        V((nbins, length), F32),
        V((2, groups, 2 * block_rows, chan), F32),
        V((groups, 2 * block_rows, chan), LOW),
        V((groups, 2 * block_rows, chan), LOW),
        V((groups, 2 * block_rows, chan), F32),
        V((groups, 2 * block_rows, chan), LOW),
        V((groups, 2 * block_rows, chan), LOW),
        V((2 * block_rows, chan), F32),
        V((block_rows, chan), F32),
        V((block_rows, chan), F32),
        V((block_rows + 8, chan), LOW),
        V((items, length, length), F32),
        V((8, length, length), LOW),
        V((8, width, length), LOW),
        V((4 * width, 8 * length), LOW),
        V((items, length, length), LOW),
        V((items, groups, rows, length), LOW),
        V((4 * width, chan), F32),
        V((1, chan), F32),
        V((groups, sh, chan), F32),
        V((sh, chan), LOW),
        V((8, chan), F32),
        V((total, 8, chan), F32),
    ]
    scratch += [
        dma((items, rows // 8)),
        dma((items, 2)),
        dma((2,)),
        dma((3, 2)),
        dma((items, 2)),
        dma((items, 2)),
        dma((items, 2, 2)),
        dma((2,)),
        dma((2,)),
        dma((2,)),
        dma((2,)),
        dma((items, 2)),
        dma((2,)),
        dma((2,)),
        dma((2,)),
    ]
    grads = pl.pallas_call(
        partial(step_kernel, groups, heads),
        out_shape=[
            jax.ShapeDtypeStruct((groups, sh, chan), LOW),
            jax.ShapeDtypeStruct((groups, block_rows + 8, chan), LOW),
            jax.ShapeDtypeStruct((nbins, chan), F32),
            jax.ShapeDtypeStruct((8, chan), F32),
        ],
        in_specs=[pl.BlockSpec(memory_space=pl.ANY), pl.BlockSpec(memory_space=pltpu.SMEM)] + [vmem] * 8,
        out_specs=[vmem] * 4,
        scratch_shapes=scratch,
        compiler_params=pltpu.CompilerParams(
            collective_id=0, has_side_effects=True, vmem_limit_bytes=60 * 2**20
        ),
        name="step",
    )(pair_input, lengths, distogram_bins, *weights)
    like = lambda group: [jax.ShapeDtypeStruct(w.shape, F32) for w in group]
    outs = pl.pallas_call(
        partial(update_kernel, groups),
        out_shape=[jax.ShapeDtypeStruct((1, 1), F32)] * 2 + like(weights) * 3,
        in_specs=[vmem] * 25,
        out_specs=[vmem] * 23,
        name="update",
    )(*grads, *weights, *momenta, *averages)
    outs = list(outs)
    outs[0], outs[1] = outs[0].reshape(()), outs[1].reshape(())
    for k in (2, 9, 16):
        outs[k + 1] = outs[k + 1].reshape(chan, 1)
        outs[k + 5] = outs[k + 5].T
    return tuple(outs)


def body(groups, heads, *args):
    items, rows, length, channels = args[0].shape
    own = rows // heads
    if heads == 4 and own == 8 and rows % 16 == 0 and length % 128 == 0:
        return fused_body(groups, heads, *args)
    return general_body(*args)


def solution(mesh):
    in_specs = (
        P(None, "res", None, None),
        P(),
        P(None, "res", None),
        P(None, "head"),
        P(None, "head"),
        P("head", None),
        P(None, "head"),
        P("head", None),
        P(),
        P(),
        P(None, "head"),
        P(None, "head"),
        P("head", None),
        P(None, "head"),
        P("head", None),
        P(),
        P(),
        P(None, "head"),
        P(None, "head"),
        P("head", None),
        P(None, "head"),
        P("head", None),
        P(),
        P(),
    )
    out_specs = (
        P(),
        P(),
        P(None, "head"),
        P(None, "head"),
        P("head", None),
        P(None, "head"),
        P("head", None),
        P(),
        P(),
        P(None, "head"),
        P(None, "head"),
        P("head", None),
        P(None, "head"),
        P("head", None),
        P(),
        P(),
        P(None, "head"),
        P(None, "head"),
        P("head", None),
        P(None, "head"),
        P("head", None),
        P(),
        P(),
    )
    return jax.shard_map(
        partial(body, mesh.shape["res"], mesh.shape["head"]), mesh=mesh, in_specs=in_specs, out_specs=out_specs, check_vma=False)
```

```python
from functools import partial

import jax
import jax.numpy as jnp
from jax import lax
from jax.experimental import pallas as pl
from jax.experimental.pallas import tpu as pltpu
from jax.sharding import PartitionSpec as P

EPS = 1e-05
NEG = -1000000000.0
MOMENTUM = 0.9
RATE = 20000.0
KEEP = 0.9
CLIP = 0.002


def project(values, weight):
    return jnp.einsum("rjc,cd->rjd", values, weight, preferred_element_type=jnp.float32)


def layer_norm(values, gain):
    center = values - jnp.mean(values, -1, keepdims=True)
    spread = jnp.mean(center * center, -1, keepdims=True)
    return center * lax.rsqrt(spread + EPS) * gain


def norm_back(values, gain, grad_out):
    result, pull = jax.vjp(layer_norm, values, gain)
    return pull(grad_out)


def row_scores(query, key, bias_full, penalty, scale):
    scores = jnp.dot(query, key.T, preferred_element_type=jnp.float32) * scale
    return scores + bias_full.astype(jnp.float32) + penalty[None, :]


def forward_row(bias_full, penalty, scale, row):
    query, key, value, gate = row
    scores = row_scores(query, key, bias_full, penalty, scale)
    peak = jnp.max(scores, -1, keepdims=True)
    expo = jnp.exp(scores - peak)
    summed = jnp.sum(expo, -1, keepdims=True)
    probs = (expo / summed).astype(jnp.bfloat16)
    mixed = jnp.dot(probs, value, preferred_element_type=jnp.float32)
    gated = (mixed * jax.nn.sigmoid(gate)).astype(jnp.bfloat16)
    return (gated, (peak + jnp.log(summed))[:, 0])


def backward_row(bias_full, penalty, scale, carry, row):
    query, key, value, gate, dgated, logsum = row
    scores = row_scores(query, key, bias_full, penalty, scale)
    exact = jnp.exp(scores - logsum[:, None])
    probs = exact.astype(jnp.bfloat16)
    mixed = jnp.dot(probs, value, preferred_element_type=jnp.float32)
    sigma = jax.nn.sigmoid(gate)
    dmixed = (dgated * sigma).astype(jnp.bfloat16)
    dgate = dgated * mixed * sigma * (1.0 - sigma)
    dvalue = jnp.dot(probs.T, dmixed, preferred_element_type=jnp.float32)
    dprobs = jnp.dot(dmixed, value.T, preferred_element_type=jnp.float32)
    inner = jnp.sum(dprobs * exact, -1, keepdims=True)
    dscores = (exact * (dprobs - inner)).astype(jnp.bfloat16)
    dquery = jnp.dot(dscores, key, preferred_element_type=jnp.float32) * scale
    dkey = jnp.dot(dscores.T, query, preferred_element_type=jnp.float32) * scale
    grads = jnp.concatenate([dquery, dkey, dvalue, dgate], -1)
    return (carry + dscores.astype(jnp.float32), grads)


def advance(weight, moment, average, grad):
    velocity = MOMENTUM * moment + grad
    fresh = weight - RATE * (grad + MOMENTUM * velocity)
    return (fresh, velocity, KEEP * average + (1.0 - KEEP) * fresh)


def general_body(
    pair_input,
    lengths,
    distogram_bins,
    head_proj,
    bias_proj,
    output_proj,
    expand_proj,
    reduce_proj,
    distogram_proj,
    small_params,
    momentum_head,
    momentum_bias,
    momentum_output,
    momentum_expand,
    momentum_reduce,
    momentum_distogram,
    momentum_small,
    average_head,
    average_bias,
    average_output,
    average_expand,
    average_reduce,
    average_distogram,
    average_small,
):
    weights = (
        head_proj,
        bias_proj,
        output_proj,
        expand_proj,
        reduce_proj,
        distogram_proj,
        small_params,
    )
    momenta = (
        momentum_head,
        momentum_bias,
        momentum_output,
        momentum_expand,
        momentum_reduce,
        momentum_distogram,
        momentum_small,
    )
    averages = (
        average_head,
        average_bias,
        average_output,
        average_expand,
        average_reduce,
        average_distogram,
        average_small,
    )
    head_w, bias_w, out_w, expand_w, reduce_w, dist_w = [
        w.astype(jnp.bfloat16) for w in weights[:6]
    ]
    items, rows, length, channels = pair_input.shape
    width = output_proj.shape[0]
    scale = width ** (-0.5)
    gain_one = small_params[:channels]
    gain_two = small_params[channels : 2 * channels]
    dist_bias = small_params[2 * channels :]
    positions = jnp.arange(length)
    first_row = lax.axis_index("res") * rows
    size_f = lengths.astype(jnp.float32)
    count = jnp.sum(size_f * size_f)
    grads = [jnp.zeros_like(w) for w in weights]
    loss_part = jnp.zeros((), jnp.float32)
    for item in range(items):
        live = (positions < lengths[item]).astype(jnp.float32)
        penalty = (1.0 - live) * NEG
        row_live = lax.dynamic_slice_in_dim(live, first_row, rows)
        start = pair_input[item].astype(jnp.float32)
        normed = layer_norm(start, gain_one).astype(jnp.bfloat16)
        proj = project(normed, head_w)
        query = proj[..., :width].astype(jnp.bfloat16)
        key = proj[..., width : 2 * width].astype(jnp.bfloat16)
        value = proj[..., 2 * width : 3 * width].astype(jnp.bfloat16)
        gate = proj[..., 3 * width :]
        bias_local = project(normed, bias_w)[..., 0].astype(jnp.bfloat16)
        bias_full = lax.all_gather(bias_local, "res", axis=0, tiled=True)
        gated, logsum = lax.map(
            partial(forward_row, bias_full, penalty, scale), (query, key, value, gate)
        )
        first = start + lax.psum(project(gated, out_w), "head")
        widened = layer_norm(first, gain_two).astype(jnp.bfloat16)
        pre = project(widened, expand_w)
        hidden = jnp.maximum(pre, 0.0).astype(jnp.bfloat16)
        second = first + lax.psum(project(hidden, reduce_w).astype(jnp.bfloat16), "head").astype(
            jnp.float32
        )
        second_low = second.astype(jnp.bfloat16)
        half = project(second_low, dist_w)
        mirror = lax.all_to_all(
            half.astype(jnp.bfloat16), "res", split_axis=1, concat_axis=0, tiled=True
        ).astype(half.dtype)
        logits = half + jnp.transpose(mirror, (1, 0, 2)) + dist_bias
        peak = jnp.max(logits, -1, keepdims=True)
        logp = logits - peak - jnp.log(jnp.sum(jnp.exp(logits - peak), -1, keepdims=True))
        onehot = (distogram_bins[item][:, :, None] == jnp.arange(logits.shape[2])).astype(
            jnp.float32
        )
        weight = (row_live[:, None] * live[None, :])[:, :, None]
        loss_part = loss_part - jnp.sum(logp * onehot * weight) / count
        dlogits = (jnp.exp(logp) - onehot) * weight / count
        back = lax.all_to_all(
            dlogits.astype(jnp.bfloat16), "res", split_axis=1, concat_axis=0, tiled=True
        ).astype(dlogits.dtype)
        dhalf = (dlogits + jnp.transpose(back, (1, 0, 2))).astype(jnp.bfloat16)
        grads[5] = grads[5] + jnp.einsum(
            "rjc,rjb->cb", second_low, dhalf, preferred_element_type=jnp.float32
        )
        dist_grad = jnp.sum(dlogits, (0, 1))
        dsecond = jnp.einsum("rjb,cb->rjc", dhalf, dist_w, preferred_element_type=jnp.float32)
        dtrans = dsecond.astype(jnp.bfloat16)
        grads[4] = grads[4] + jnp.einsum(
            "rjh,rjc->hc", hidden, dtrans, preferred_element_type=jnp.float32
        )
        dhidden = jnp.einsum("rjc,hc->rjh", dtrans, reduce_w, preferred_element_type=jnp.float32)
        dpre = jnp.where(pre > 0, dhidden, 0.0).astype(jnp.bfloat16)
        grads[3] = grads[3] + jnp.einsum(
            "rjc,rjh->ch", widened, dpre, preferred_element_type=jnp.float32
        )
        dwidened = lax.psum(
            jnp.einsum("rjh,ch->rjc", dpre, expand_w, preferred_element_type=jnp.float32).astype(
                jnp.bfloat16
            ),
            "head",
        ).astype(jnp.float32)
        dfirst_norm, gain_two_grad = norm_back(first, gain_two, dwidened)
        dout = (dsecond + dfirst_norm).astype(jnp.bfloat16)
        grads[2] = grads[2] + jnp.einsum(
            "rjd,rjc->dc", gated, dout, preferred_element_type=jnp.float32
        )
        dgated = jnp.einsum("rjc,dc->rjd", dout, out_w, preferred_element_type=jnp.float32)
        bias_terms, dproj = lax.scan(
            partial(backward_row, bias_full, penalty, scale),
            jnp.zeros((length, length), jnp.float32),
            (query, key, value, gate, dgated, logsum),
        )
        dproj = dproj.astype(jnp.bfloat16)
        dbias = lax.psum_scatter(bias_terms, "res", scatter_dimension=0, tiled=True).astype(
            jnp.bfloat16
        )
        grads[0] = grads[0] + jnp.einsum(
            "rjc,rjd->cd", normed, dproj, preferred_element_type=jnp.float32
        )
        grads[1] = (
            grads[1]
            + jnp.einsum("rjc,rj->c", normed, dbias, preferred_element_type=jnp.float32)[:, None]
        )
        dnormed_part = jnp.einsum("rjd,cd->rjc", dproj, head_w, preferred_element_type=jnp.float32)
        dnormed_part = dnormed_part + dbias.astype(jnp.float32)[:, :, None] * bias_w[:, 0].astype(
            jnp.float32
        )
        dnormed = lax.psum(dnormed_part.astype(jnp.bfloat16), "head").astype(jnp.float32)
        unused, gain_one_grad = norm_back(start, gain_one, dnormed)
        grads[6] = grads[6] + jnp.concatenate([gain_one_grad, gain_two_grad, dist_grad])
    summed = lax.psum(
        (grads[0], grads[1], grads[2], grads[3], grads[4], grads[5], grads[6], loss_part), "res"
    )
    total_grads = summed[:7]
    total_loss = summed[7]
    owned = jnp.zeros((), jnp.float32)
    for grad in total_grads[:5]:
        owned = owned + jnp.sum(grad * grad)
    shared = jnp.sum(total_grads[5] * total_grads[5]) + jnp.sum(total_grads[6] * total_grads[6])
    grad_norm = jnp.sqrt(shared + lax.psum(owned, "head"))
    factor = CLIP / jnp.maximum(grad_norm, CLIP)
    results = [
        advance(w, m, a, g * factor) for w, m, a, g in zip(weights, momenta, averages, total_grads)
    ]
    new_w = [r[0] for r in results]
    new_m = [r[1] for r in results]
    new_a = [r[2] for r in results]
    return (
        total_loss,
        grad_norm,
        new_w[0],
        new_w[1],
        new_w[2],
        new_w[3],
        new_w[4],
        new_w[5],
        new_w[6],
        new_m[0],
        new_m[1],
        new_m[2],
        new_m[3],
        new_m[4],
        new_m[5],
        new_m[6],
        new_a[0],
        new_a[1],
        new_a[2],
        new_a[3],
        new_a[4],
        new_a[5],
        new_a[6],
    )


NT = (((1,), (1,)), ((), ()))
NN = (((1,), (0,)), ((), ()))
F32 = jnp.float32
LOW = jnp.bfloat16
LOG2E = 1.4426950408889634


def dot(left, right, dims=NN):
    return lax.dot_general(left, right, dims, preferred_element_type=F32)


def iota(shape, dim):
    return lax.broadcasted_iota(jnp.int32, shape, dim)


def eye(size):
    return (iota((size, size), 0) == iota((size, size), 1)).astype(F32).astype(LOW)


def sigmoid(x):
    return 0.5 * jnp.tanh(0.5 * x) + 0.5


def staged(count, stages, lag):
    for step in range(count + lag * (len(stages) - 1)):
        for k, stage in enumerate(stages):
            if 0 <= step - k * lag < count:
                stage(step - k * lag)


def step_kernel(groups, heads, *refs):
    (
        pair_hbm, lengths, bins, head_w, bias_w, out_w, exp_w, red_w, dist_w, small,
        o_head, o_block, o_dist, o_small,
        pair, normed, tok, qkv, sig, expo, mixed, rinv,
        wc, wt, we, wet, wr, wrt, wo, wot, wd, wdt, gain_col, dist_col, sel_a, sel_b,
        bias_f, bias_send, bias_all, bias_t, bins_low, bins_in, bins_own, bins_t,
        gated, gall, xhat, rstd, widened, hidden, slow, halves, pack_f, half_send, half_in, mirror,
        dpre_s, first_s, dh_s, dsec_s, dtr_s, dout_s, dg_send, dg_in,
        g_out, g_red, g_exp, g_dist, loss_acc, dist_acc,
        block_own, core_send, core_in, core_sum, block_send, block_in, part_own, part_in, block_sum, block_low,
        db_acc, ds_s, dm_s, dproj_s, db_send, db_in, g_head, g_bias, head_in, head_low, card, card_in,
        sem_pair, sem_bias, sem_bins, sem_w, sem_gat, sem_half, sem_dg,
        sem_core, sem_blk, sem_part, sem_gath, sem_db, sem_head, sem_card, sem_fin,
    ) = refs
    items, rows, length, chan = pair.shape
    group_rows = 8
    width = out_w.shape[0]
    nbins = dist_w.shape[0]
    unit = exp_w.shape[1]
    own = rows // heads
    half_own = own // 2
    total = groups * heads
    scale = width ** (-0.5)
    my_r = lax.axis_index("res")
    my_h = lax.axis_index("head")
    me = my_r * heads + my_h

    def device(r, h):
        return {"res": r, "head": h}

    def send(src, dst, sem, r, h):
        return pltpu.make_async_remote_copy(
            src_ref=src, dst_ref=dst, send_sem=sem.at[0], recv_sem=sem.at[1],
            device_id=device(r, h), device_id_type=pl.DeviceIdType.MESH,
        )

    def res_peer(o):
        return lax.rem(my_r + o, groups)

    def head_peer(o):
        flip, cross = o // 2 % 2, (o + 1) // 2 % 2
        return lax.rem(my_h + flip * (1 - 2 * lax.rem(my_h, 2)) + 2 * cross, heads)

    def any_peer(o):
        d = lax.rem(me + o, total)
        return d, d // heads, lax.rem(d, heads)

    def start(count, make):
        def one(o, carry):
            make(o).start()
            return carry
        lax.fori_loop(1, count, one, 0)

    def wait_in(ref, sem):
        send(ref, ref, sem, res_peer(1), my_h).wait_recv()

    def wait_out(ref, sem):
        send(ref, ref, sem, res_peer(1), my_h).wait_send()

    def load(item, t):
        at = pl.ds(t * group_rows, group_rows)
        return pltpu.make_async_copy(pair_hbm.at[item, at], pair.at[item, at], sem_pair.at[item, t])

    barrier = pltpu.get_barrier_semaphore()

    def greet(o, carry):
        d, r, h = any_peer(o)
        pl.semaphore_signal(barrier, inc=1, device_id=device(r, h), device_id_type=pl.DeviceIdType.MESH)
        return carry

    lax.fori_loop(1, total, greet, 0)

    for item in range(items):
        for t in range(rows // group_rows):
            load(item, t).start()

    brow = bias_w[...].astype(LOW).astype(F32)
    gain_one = small[0:chan].reshape(1, chan)
    gain_two = small[chan : 2 * chan].reshape(1, chan)
    ident = eye(chan)
    ident_l = eye(length)
    center_by = (ident.astype(F32) - 1.0 / chan).astype(LOW)
    one_lane = (iota((1, 4 * width), 1) >= 3 * width).astype(F32)

    def prepare_first():
        hw = head_w[...]
        wc[0 : 4 * width] = jnp.transpose(hw).astype(LOW)
        wc[4 * width :] = jnp.where(iota((16, chan), 0) == 0, brow, 0.0).astype(LOW)
        src_col = iota((4 * width, 4 * width), 0)
        dst_col = iota((4 * width, 4 * width), 1)
        want = jnp.where(
            dst_col < width, dst_col + width, jnp.where(dst_col < 3 * width, dst_col, -1)
        )
        wt[...] = dot(hw.astype(LOW), (src_col == want).astype(F32).astype(LOW)).astype(LOW)

    def prepare_weights():
        we[:, pl.ds(pl.multiple_of(my_h * unit, unit), unit)] = exp_w[...].astype(LOW)
        wr[pl.ds(pl.multiple_of(my_h * unit, unit), unit), :] = red_w[...].astype(LOW)
        wo[pl.ds(pl.multiple_of(my_h * width, width), width), :] = out_w[...].astype(LOW)

    def prepare_rest():
        bins_row = jnp.concatenate(
            [small[2 * chan : 2 * chan + nbins].reshape(1, nbins), jnp.zeros((1, chan - nbins), F32)], 1
        )
        gain_col[...] = jnp.transpose(jnp.broadcast_to(gain_two, (chan, chan)))
        dist_col[...] = jnp.transpose(jnp.broadcast_to(bins_row, (chan, chan)))[:nbins]
        wdt[...] = dist_w[...].astype(LOW)
        wd[...] = dot(ident, wdt[...], NT).astype(LOW)
        bins_low[...] = bins[...].astype(F32).astype(LOW)
        bins_own[...] = bins[:, pl.ds(pl.multiple_of(my_h * own, own), own), :].astype(F32)
        sel_row = iota((total * half_own, length), 0)
        sel_col = iota((total * half_own, length), 1)
        sel_at = sel_row // half_own * own + lax.rem(sel_row, half_own)
        sel_a[...] = (sel_col == sel_at).astype(F32).astype(LOW)
        sel_b[...] = (sel_col == sel_at + half_own).astype(F32).astype(LOW)
        for ref in (g_out, g_red, g_exp, g_dist, loss_acc, dist_acc, g_head, g_bias, db_acc):
            ref[...] = jnp.zeros_like(ref)

    def before(item):
        def norm(r):
            center = dot(pair[item, r], center_by)
            spread = jnp.mean(center * center, -1, keepdims=True)
            normed[item, r] = (center * lax.rsqrt(spread + EPS) * gain_one).astype(LOW)

        def mult(r):
            low = normed[item, r]
            ch = dot(wc[...], low, NT)
            qkv[item, r] = ch[: 3 * width].astype(LOW)
            sig[item, r] = sigmoid(ch[3 * width : 4 * width])
            bias_f[pl.ds(r, 1), :] = ch[4 * width : 4 * width + 1]
            tok[item, r] = (dot(low, wt[...]) + one_lane).astype(LOW)

        def group(t, carry):
            load(item, t).wait()
            for k in range(8 + 8):
                if k < 8:
                    norm(t * 8 + k)
                if k >= 8:
                    mult(t * 8 + k - 8)
            return carry
        lax.fori_loop(0, rows // 8, group, 0)
        bias_send[item] = bias_f[...].astype(LOW)
        bias_all[item, pl.ds(pl.multiple_of(my_r * rows, rows), rows), :] = bias_f[...].astype(LOW)

    def bias_copy(item):
        def make(o):
            return send(
                bias_send.at[item],
                bias_all.at[item, pl.ds(pl.multiple_of(my_r * rows, rows), rows), :],
                sem_bias.at[item], res_peer(o), my_h,
            )
        return make

    def bins_block(r):
        return pl.ds(pl.multiple_of((r * rows) // 128 * 128, 128), 128)

    def bins_copy(o):
        return send(
            bins_low.at[:, :, bins_block(res_peer(o))], bins_in.at[my_r],
            sem_bins, res_peer(o), my_h,
        )

    def we_copy(o):
        at = (slice(None), pl.ds(pl.multiple_of(my_h * unit, unit), unit))
        return send(we.at[at], we.at[at], sem_w.at[0], my_r, head_peer(o))

    def wr_copy(o):
        at = pl.ds(pl.multiple_of(my_h * unit, unit), unit)
        return send(wr.at[at], wr.at[at], sem_w.at[1], my_r, head_peer(o))

    def wo_copy(o):
        at = pl.ds(pl.multiple_of(my_h * width, width), width)
        return send(wo.at[at], wo.at[at], sem_w.at[2], my_r, head_peer(o))

    def gated_copy(item):
        def make(o):
            p = head_peer(o)
            return send(
                gated.at[item, pl.ds(p * own, own)],
                gall.at[item, :, pl.ds(pl.multiple_of(my_h * width, width), width), :],
                sem_gat.at[item], my_r, p,
            )
        return make

    def attend(item):
        live = iota((length, length), 0) < lengths[item]
        bt = dot(ident_l, bias_all[item], NT) * LOG2E
        bias_t[...] = bt + jnp.where(live, 0.0, NEG * LOG2E)

        def scores(r):
            q = qkv[item, r, 0:width].astype(F32) * (scale * LOG2E)
            hi = q.astype(LOW)
            lo = (q - hi.astype(F32)).astype(LOW)
            rhs = jnp.concatenate([hi, lo, jnp.zeros((2 * width, length), LOW)], 0)
            s = dot(tok[item, r], rhs) + bias_t[...]
            expo[item, r] = jnp.exp2(s - jnp.max(s, 0, keepdims=True)).astype(LOW)

        def gather(r):
            lhs = jnp.concatenate(
                [qkv[item, r, 2 * width : 3 * width], jnp.ones((16, length), LOW)], 0
            )
            o = dot(lhs, expo[item, r])
            inv = 1.0 / o[width : width + 1]
            rinv[item, pl.ds(r, 1), :] = inv
            m = o[:width] * inv
            mixed[item, r] = m
            gated[item, r] = (m * sig[item, r]).astype(LOW)

        def chunk(o, carry):
            p = head_peer(o)
            base = p * own

            def one(t, c):
                for k in range(8 + 4):
                    if k < 8:
                        scores(base + t * 8 + k)
                    if k >= 4:
                        gather(base + t * 8 + k - 4)
                return c
            lax.fori_loop(0, own // 8, one, 0, unroll=1)

            @pl.when(o < heads)
            def _():
                gated_copy(item)(o).start()
            return carry
        lax.fori_loop(1, heads + 1, chunk, 0)
        gall[item, :, pl.ds(pl.multiple_of(my_h * width, width), width), :] = gated[
            item, pl.ds(my_h * own, own)
        ]

    def pair_of(ref, item, t):
        return jnp.concatenate([ref[item, t], ref[item, t + half_own]], 1)

    def forward(item):
        gc = jnp.concatenate([gain_col[...]] * (2 * length // chan), 1)
        zero = jnp.zeros((nbins, length), LOW)

        def enter(t):
            g2 = pair_of(gall, item, t)
            base = my_h * own + t
            first = jnp.concatenate(
                [dot(ident, pair[item, base], NT), dot(ident, pair[item, base + half_own], NT)], 1
            ) + dot(wot[...], g2)
            first_s[t] = first
            center = first - jnp.mean(first, 0, keepdims=True)
            rs = lax.rsqrt(jnp.mean(center * center, 0, keepdims=True) + EPS)
            xh = center * rs
            xhat[item, t] = xh
            rstd[item, t] = jnp.broadcast_to(rs, (8, 2 * length))
            widened[item, t] = (xh * gc).astype(LOW)

        def expand(t):
            for b in range(heads):
                hidden[item, t, b * unit : (b + 1) * unit] = jnp.maximum(
                    dot(wet[b * unit : (b + 1) * unit], widened[item, t]), 0.0
                ).astype(LOW)

        def reduce(t):
            slow[item, t] = (first_s[t] + dot(wrt[...], hidden[item, t])).astype(LOW)

        def project_half(t):
            half = dot(wdt[...], slow[item, t])
            halves[item, t] = half[:, :length]
            halves[item, t + half_own] = half[:, length:]

        def pack(t):
            for k in range(2):
                part = halves[item, t + k * half_own].astype(LOW)
                packed = dot(sel_a[...], jnp.concatenate([part, zero], 0), NT) + dot(
                    sel_b[...], jnp.concatenate([zero, part], 0), NT
                )
                pack_f[pl.ds(t + k * half_own, total * half_own, own), :] = packed

        staged(half_own, (enter, expand, reduce, project_half, pack), 2)
        half_send[item] = pack_f[...].reshape(half_send.shape[1:]).astype(LOW)
        half_in[item, me] = half_send[item, me]

    def half_copy(item):
        def make(o):
            d, r, h = any_peer(o)
            return send(
                half_send.at[item, d], half_in.at[item, me],
                sem_half.at[item], r, h,
            )
        return make

    size_sum = jnp.zeros((1, length), F32)
    for item in range(items):
        size = lengths[item]
        size_sum = size_sum + (jnp.zeros((1, length), jnp.int32) + size * size).astype(F32)

    def backward(item):
        mirror[...] = half_in[item].astype(F32)
        live = (iota((1, length), 1) < lengths[item]).astype(F32) / size_sum
        levels = iota((nbins, length), 0).astype(F32)[None]

        gc = jnp.concatenate([gain_col[...]] * (2 * length // chan), 1)
        dist_c = jnp.concatenate([dist_col[...]] * (length // chan), 1)[None]

        def two(ref, t):
            return jnp.concatenate(
                [ref[item, pl.ds(t, 1), :][None], ref[item, pl.ds(t + half_own, 1), :][None]], 0
            )

        def loss_grad(t):
            flip = mirror[:, t * own : (t + 1) * own, :].reshape(length, 2 * nbins)
            flip = dot(eye(2 * nbins), flip.astype(LOW), NT)
            here = jnp.concatenate([halves[item, t], halves[item, t + half_own]], 0)
            logits = (here + flip).reshape(2, nbins, length) + dist_c
            peak = jnp.max(logits, 1, keepdims=True)
            ex = jnp.exp(logits - peak)
            tot = jnp.sum(ex, 1, keepdims=True)
            prob = ex * (1.0 / tot)
            hot = (two(bins_own, t) == levels).astype(F32)
            hot_t = (two(bins_t, t) == levels).astype(F32)
            at = me * own + t + iota((2, 1, length), 0) * half_own
            weight = jnp.where(at < lengths[item], 1.0, 0.0) * live[None]
            picked = jnp.sum(hot * logits, 1, keepdims=True)
            lost = weight * (peak + jnp.log(tot) - picked)
            loss_acc[...] += lost[0] + lost[1]
            short = prob - hot
            dl = short * weight
            dist_acc[...] += dl[0] + dl[1]
            dh = ((short + prob - hot_t) * weight).astype(LOW)
            dh_s[t] = jnp.concatenate([dh[0], dh[1]], 1)

        def enter(t):
            dsec = dot(wd[...], dh_s[t])
            dsec_s[t] = dsec
            dtr_s[t] = dsec.astype(LOW)
            g_dist[...] += dot(dh_s[t], slow[item, t], NT)

        def through(t):
            for b in range(heads):
                at_b = slice(b * unit, (b + 1) * unit)
                hid = hidden[item, t, at_b]
                dpre_s[t, at_b] = jnp.where(
                    hid.astype(F32) > 0.0, dot(wr[at_b], dtr_s[t]), 0.0
                ).astype(LOW)

        def weights_back(t):
            for b in range(heads):
                at_b = slice(b * unit, (b + 1) * unit)
                g_red[at_b] += dot(hidden[item, t, at_b], dtr_s[t], NT)
                g_exp[at_b] += dot(dpre_s[t, at_b], widened[item, t], NT)

        def leave(t):
            dxh = dot(we[...], dpre_s[t]) * gc
            xh = xhat[item, t]
            m1 = jnp.mean(dxh, 0, keepdims=True)
            m2 = jnp.mean(dxh * xh, 0, keepdims=True)
            dout_s[t] = (dsec_s[t] + rstd[item, t, 0:1] * (dxh - m1 - xh * m2)).astype(LOW)

        def output_back(t):
            dg = dot(wo[...], dout_s[t]).astype(LOW)
            for h in range(heads):
                for k in range(2):
                    dg_send[item, h, t + k * half_own] = dg[
                        h * width : (h + 1) * width, k * length : (k + 1) * length
                    ]
            g_out[...] += dot(pair_of(gall, item, t), dout_s[t], NT)

        staged(half_own, (loss_grad, enter, through, weights_back, leave, output_back), 2)
        dg_in[item, pl.ds(my_h * own, own)] = dg_send[item, my_h]

    def dg_copy(item):
        def make(o):
            p = head_peer(o)
            return send(
                dg_send.at[item, p], dg_in.at[item, pl.ds(my_h * own, own)],
                sem_dg.at[item, o // (heads - 1)], my_r, p,
            )
        return make

    def attend_back(item, first_o, last_o):
        tail_row = iota((16, length), 0)

        def first(r, k, tot):
            s = sig[item, r]
            m = mixed[item, r]
            dg = dg_in[item, r].astype(F32)
            dm = (dg * s * rinv[item, pl.ds(r, 1), :]).astype(LOW)
            inner = -jnp.sum(dm.astype(F32) * m, 0, keepdims=True)
            hi = inner.astype(LOW).astype(F32)
            lo = inner - hi
            tail = jnp.where(tail_row == 0, hi, jnp.where(tail_row == 1, lo, 0.0)).astype(LOW)
            rhs = jnp.concatenate(
                [jnp.zeros((2 * width, length), LOW), dm, tail, jnp.zeros((width - 16, length), LOW)], 0
            )
            dm_s[k] = dm
            dproj_s[3 * width :, k * length : (k + 1) * length] = (dg * m * s * (1.0 - s)).astype(LOW)
            ds = expo[item, r].astype(F32) * dot(tok[item, r], rhs)
            db_acc[item] += ds
            ds_s[k] = ds.astype(LOW)
            return None

        def second(r, k):
            at = slice(k * length, (k + 1) * length)
            ds = ds_s[k]
            dproj_s[0:width, at] = (dot(qkv[item, r, width : 2 * width], ds) * scale).astype(LOW)
            dproj_s[width : 2 * width, at] = (dot(qkv[item, r, 0:width], ds, NT) * scale).astype(LOW)
            dproj_s[2 * width : 3 * width, at] = dot(dm_s[k], expo[item, r], NT).astype(LOW)

        def group(o, carry):
            t = head_peer(o)
            tot = None
            for k in range(8 + 4):
                if k < 8:
                    tot = first(t * 8 + k, k, tot)
                if k >= 4:
                    second(t * 8 + k - 4, k - 4)
            g_head[...] += dot(dproj_s[...], normed[item, pl.ds(t * 8, 8)].reshape(8 * length, chan))
            return carry
        lax.fori_loop(first_o, last_o, group, 0)

    def pair_bias_back(item):
        db_send[item] = dot(ident_l, db_acc[item].astype(LOW), NT).astype(LOW)
        db_in[item, my_r] = db_send[item, pl.ds(pl.multiple_of(my_r * rows, rows), rows), :]

    def db_copy(item):
        def make(o):
            p = res_peer(o)
            return send(
                db_send.at[item, pl.ds(pl.multiple_of(p * rows, rows), rows), :], db_in.at[item, my_r],
                sem_db.at[item], p, my_h,
            )
        return make

    def bias_back(item):
        db = db_in[item, 0].astype(F32)
        for s in range(1, groups):
            db = db + db_in[item, s].astype(F32)
        db = db.astype(LOW).astype(F32)
        at = iota((8, length), 0)
        acc = jnp.zeros((8, chan), F32)
        for g in range(rows // 8):
            part = db[8 * g : 8 * g + 8]
            spread = jnp.concatenate([jnp.where(at == q, part, 0.0) for q in range(8)], 1)
            acc = acc + dot(
                spread.astype(LOW), normed[item, 8 * g : 8 * g + 8].reshape(8 * length, chan)
            )
        g_bias[...] += jnp.sum(acc, 0, keepdims=True)

    ru, rw, rb = unit // groups, width // groups, nbins // total
    piece = 2 * ru + 8

    side, mate = my_h // 2, lax.rem(my_h, 2)

    def core_copy():
        return send(core_send, core_in, sem_core, my_r, head_peer(heads - 1))

    def block_copy(o):
        p = res_peer(o)
        return send(block_send.at[p], block_in.at[my_r], sem_blk, p, my_h)

    def part_copy():
        at = pl.ds(pl.multiple_of((1 - side) * piece, 8), piece)
        return send(part_own.at[at, :], part_in, sem_part, my_r, head_peer(1))

    def gather_copy(o):
        return send(block_low, o_block.at[my_r], sem_gath, res_peer(o), my_h)

    def block_make():
        for r in range(groups):
            for h in range(heads):
                c, base = h % 2, h // 2 * piece
                at = h * unit + r * ru
                block_own[c, r, base : base + ru] = g_red[at : at + ru]
                block_own[c, r, base + ru : base + 2 * ru] = g_exp[at : at + ru]
                at = h * width + r * rw
                base += 2 * ru
                block_own[c, r, base : base + rw] = g_out[at : at + rw]
                at = (r * heads + h) * rb
                block_own[c, r, base + rw : base + rw + rb] = g_dist[at : at + rb]
                block_own[c, r, base + rw + rb : base + 8] = jnp.zeros((8 - rw - rb, chan), F32)
        core_send[...] = block_own[1 - mate].astype(LOW)

    def core_add():
        both = block_own[mate] + core_in[...].astype(F32)
        core_sum[...] = both
        block_send[...] = both.astype(LOW)

    def part_make():
        acc = core_sum[my_r]
        for o in range(1, groups):
            acc = acc + block_in[res_peer(o)].astype(F32)
        part_own[...] = acc

    def block_add():
        acc = part_own[pl.ds(pl.multiple_of(side * piece, 8), piece), :] + part_in[...]
        block_sum[...] = acc
        low = jnp.concatenate([acc, jnp.zeros((8, chan), F32)], 0).astype(LOW)
        block_low[...] = low
        o_block[my_r] = low

    def head_copy(o):
        p = res_peer(o)
        return send(
            g_head.at[pl.ds(pl.multiple_of(p * (4 * width // groups), 4 * width // groups), 4 * width // groups), :],
            head_in.at[my_r], sem_head, p, my_h,
        )

    def card_copy(o):
        d, r, h = any_peer(o)
        return send(card, card_in.at[me], sem_card, r, h)

    def fin_copy(o):
        return send(head_low, o_head.at[my_r], sem_fin, res_peer(o), my_h)

    all_but = lambda ref, item, count: ref.at[item, pl.ds(0, count)]
    bias_part = lambda item: all_but(bias_all, item, (groups - 1) * rows)
    gat_part = lambda item: all_but(gated, item, (heads - 1) * own)
    dg_near = lambda item: all_but(dg_in, item, own)
    dg_far = lambda item: all_but(dg_in, item, (heads - 2) * own)
    half_part = lambda item: all_but(half_in, item, total - 1)
    db_part = lambda item: all_but(db_in, item, groups - 1)
    bins_part = bins_in.at[pl.ds(0, groups - 1)]
    w_parts = (
        we.at[:, pl.ds(0, (heads - 1) * unit)], wr.at[pl.ds(0, (heads - 1) * unit)],
        wo.at[pl.ds(0, (heads - 1) * width)],
    )
    blk_part = block_in.at[pl.ds(0, groups - 1)]
    gath_part = o_block.at[pl.ds(0, groups - 1)]
    head_part = head_in.at[pl.ds(0, groups - 1)]
    fin_part = o_head.at[pl.ds(0, groups - 1)]
    card_part = card_in.at[pl.ds(0, total - 1)]

    prepare_first()
    before(0)
    pl.semaphore_wait(barrier, total - 1)
    start(groups, bias_copy(0))
    prepare_weights()
    for make in (we_copy, wr_copy, wo_copy):
        start(heads, make)
    for item in range(1, items):
        before(item)
        start(groups, bias_copy(item))
    prepare_rest()
    bins_in[my_r] = bins_low[:, :, bins_block(my_r)]
    for item in range(items):
        wait_in(bias_part(item), sem_bias.at[item])
        attend(item)
        if item == 0:
            start(groups, bins_copy)
    for k in range(3):
        wait_in(w_parts[k], sem_w.at[k])
    for b in range(heads):
        at = slice(b * unit, (b + 1) * unit)
        wet[at] = dot(ident, we[:, at], NT).astype(LOW)
        wrt[:, at] = dot(ident, wr[at], NT).astype(LOW)
    wot[...] = dot(ident, wo[...], NT).astype(LOW)
    for item in range(items):
        wait_in(gat_part(item), sem_gat.at[item])
        forward(item)
        start(total, half_copy(item))
    wait_in(bins_part, sem_bins)
    lane = my_r * rows + my_h * own - (my_r * rows) // 128 * 128
    pick = (iota((16, 128), 1) == iota((16, 128), 0) + lane).astype(F32).astype(LOW)
    for item in range(items):
        bins_t[item] = dot(pick, bins_in[:, item].reshape(groups * rows, 128), NT)
    last = items - 1
    for item in range(items):
        wait_in(half_part(item), sem_half.at[item])
        backward(item)
        dg_copy(item)(heads - 1).start()
        if item == last:
            block_make()
            core_copy().start()
        start(heads - 1, dg_copy(item))
        wait_in(dg_near(item), sem_dg.at[item, 1])
        attend_back(item, heads - 1, heads + 1)
    wait_in(core_in, sem_core)
    core_add()
    start(groups, block_copy)
    for item in range(items):
        wait_in(dg_far(item), sem_dg.at[item, 0])
        attend_back(item, 1, heads - 1)
        pair_bias_back(item)
        start(groups, db_copy(item))
    start(groups, head_copy)
    sh = 4 * width // groups
    head_in[my_r] = g_head[pl.ds(pl.multiple_of(my_r * sh, sh), sh), :]
    wait_in(blk_part, sem_blk)
    part_make()
    part_copy().start()
    for item in range(last):
        wait_in(db_part(item), sem_db.at[item])
        bias_back(item)
    wait_in(head_part, sem_head)
    acc = head_in[0]
    for r in range(1, groups):
        acc = acc + head_in[r]
    head_low[...] = acc.astype(LOW)
    o_head[my_r] = acc.astype(LOW)
    wait_in(part_in, sem_part)
    block_add()
    start(groups, fin_copy)
    start(groups, gather_copy)
    up_one = jnp.sum(wc[0 : 4 * width].astype(F32) * g_head[...], 0, keepdims=True)
    up_two = jnp.sum(wet[...].astype(F32) * g_exp[...], 0, keepdims=True)
    dacc = dist_acc[:, 0:chan]
    lacc = loss_acc[:, 0:chan]
    for k in range(1, length // chan):
        dacc = dacc + dist_acc[:, k * chan : (k + 1) * chan]
        lacc = lacc + loss_acc[:, k * chan : (k + 1) * chan]
    dacc = jnp.transpose(jnp.concatenate([dacc, jnp.zeros((chan - nbins, chan), F32)], 0))
    blocks = block_sum[...]
    card[2:3] = up_two / gain_two
    card[3:4] = jnp.sum(dacc, 0, keepdims=True)
    card[4:5] = lacc
    card[5:6] = jnp.sum(acc * acc, 0, keepdims=True) + jnp.sum(blocks * blocks, 0, keepdims=True)
    card[6:8] = blocks[2 * ru + rw : 2 * ru + rw + rb]
    wait_in(db_part(last), sem_db.at[last])
    bias_back(last)
    gb = g_bias[...]
    card[0:1] = gb
    card[1:2] = (up_one + brow * gb) / gain_one
    card_in[me] = card[...]
    start(total, card_copy)
    wait_in(card_part, sem_card)
    by_head = [card_in[h] for h in range(heads)]
    for r in range(1, groups):
        by_head = [a + card_in[r * heads + h] for h, a in enumerate(by_head)]
    every = by_head[0]
    bias_sq = by_head[0] * by_head[0]
    for a in by_head[1:]:
        every = every + a
        bias_sq = bias_sq + a * a
    norm_sq = every[5:6] + bias_sq[0:1]
    for k in (1, 2, 3):
        norm_sq = norm_sq + every[k : k + 1] * every[k : k + 1]
    norm = jnp.sqrt(jnp.sum(norm_sq, -1, keepdims=True))
    o_small[...] = every
    mine = card_in[my_h]
    for r in range(1, groups):
        mine = mine + card_in[r * heads + my_h]
    o_small[0:1] = mine[0:1]
    o_small[4:5] = jnp.broadcast_to(jnp.sum(every[4:5], -1, keepdims=True), (1, chan))
    o_small[5:6] = jnp.broadcast_to(norm, (1, chan))
    o_small[6:7] = jnp.broadcast_to(CLIP / jnp.maximum(norm, CLIP), (1, chan))
    for d in range(total):
        o_dist[d * rb : (d + 1) * rb] = card_in[d, 6 : 6 + rb]
    wait_in(gath_part, sem_gath)
    wait_in(fin_part, sem_fin)
    for item in range(items):
        wait_out(bias_part(item), sem_bias.at[item])
        wait_out(gat_part(item), sem_gat.at[item])
        wait_out(half_part(item), sem_half.at[item])
        wait_out(dg_far(item), sem_dg.at[item, 0])
        wait_out(dg_near(item), sem_dg.at[item, 1])
        wait_out(db_part(item), sem_db.at[item])
    for k in range(3):
        wait_out(w_parts[k], sem_w.at[k])
    for ref, sem in (
        (bins_part, sem_bins), (core_in, sem_core), (blk_part, sem_blk), (part_in, sem_part), (gath_part, sem_gath),
        (head_part, sem_head), (fin_part, sem_fin), (card_part, sem_card),
    ):
        wait_out(ref, sem)


def update_kernel(groups, *refs):
    g_head, g_block, g_dist, g_small = refs[:4]
    weights, momenta, averages = refs[4:11], refs[11:18], refs[18:25]
    loss, norm = refs[25:27]
    new_w, new_m, new_a = refs[27:34], refs[34:41], refs[41:48]
    loss[...] = g_small[4:5, 0:1]
    norm[...] = g_small[5:6, 0:1]
    factor = g_small[6:7, 0:1]
    unit = weights[4].shape[0]
    width = weights[2].shape[0]
    ru, rw = unit // groups, width // groups
    chan = g_small.shape[1]

    def put(k, grad, at=(slice(None), slice(None))):
        fresh, velocity, average = advance(
            weights[k][at], momenta[k][at], averages[k][at], grad * (factor if grad.ndim > 1 else factor[0])
        )
        new_w[k][at] = fresh
        new_m[k][at] = velocity
        new_a[k][at] = average

    put(0, jnp.transpose(g_head[...].astype(F32).reshape(weights[0].shape[1], chan)))
    put(1, g_small[0:1])
    block = g_block[...].astype(F32)
    put(3, jnp.transpose(block[:, ru : 2 * ru].reshape(unit, chan)))
    put(4, block[:, 0:ru].reshape(unit, chan))
    for r in range(groups):
        put(2, block[r, 2 * ru : 2 * ru + rw], (slice(r * rw, (r + 1) * rw), slice(None)))
    nbins = weights[5].shape[0]
    put(5, g_dist[...])
    put(6, g_small[1], (slice(0, chan),))
    put(6, g_small[2], (slice(chan, 2 * chan),))
    put(6, g_small[3, 0:nbins], (slice(2 * chan, 2 * chan + nbins),))


def fused_body(groups, heads, *args):
    pair_input, lengths, distogram_bins = args[:3]
    weights, momenta, averages = list(args[3:10]), list(args[10:17]), list(args[17:24])
    items, rows, length, chan = pair_input.shape
    width = weights[2].shape[0]
    unit = weights[3].shape[1]
    nbins = weights[5].shape[1]
    own, total = rows // heads, groups * heads
    half_own = own // 2
    for group in (weights, momenta, averages):
        group[1] = group[1].reshape(1, chan)
        group[5] = group[5].T
    vmem = pl.BlockSpec(memory_space=pltpu.VMEM)
    block_rows = 2 * (unit // groups) + 8
    sh = 4 * width // groups
    V = pltpu.VMEM
    dma = pltpu.SemaphoreType.DMA
    scratch = [
        V((items, rows, length, chan), LOW),
        V((items, rows, length, chan), LOW),
        V((items, rows, length, 4 * width), LOW),
        V((items, rows, 3 * width, length), LOW),
        V((items, rows, width, length), F32),
        V((items, rows, length, length), LOW),
        V((items, rows, width, length), F32),
        V((items, rows, length), F32),
        V((4 * width + 16, chan), LOW),
        V((chan, 4 * width), LOW),
        V((chan, heads * unit), LOW),
        V((heads * unit, chan), LOW),
        V((heads * unit, chan), LOW),
        V((chan, heads * unit), LOW),
        V((heads * width, chan), LOW),
        V((chan, heads * width), LOW),
        V((chan, nbins), LOW),
        V((nbins, chan), LOW),
        V((chan, chan), F32),
        V((nbins, chan), F32),
        V((total * half_own, length), LOW),
        V((total * half_own, length), LOW),
        V((rows, length), F32),
        V((items, rows, length), LOW),
        V((items, length, length), LOW),
        V((length, length), F32),
        V((items, rows, length), LOW),
        V((groups, items, rows, 128), LOW),
        V((items, own, length), F32),
        V((items, 16, length), F32),
        V((items, rows, width, length), LOW),
        V((items, own, heads * width, length), LOW),
        V((items, half_own, chan, 2 * length), F32),
        V((items, half_own, 8, 2 * length), F32),
        V((items, half_own, chan, 2 * length), LOW),
        V((items, half_own, heads * unit, 2 * length), LOW),
        V((items, half_own, chan, 2 * length), LOW),
        V((items, own, nbins, length), F32),
        V((total * half_own * own, 2 * nbins), F32),
        V((items, total, half_own * own, 2 * nbins), LOW),
        V((items, total, half_own * own, 2 * nbins), LOW),
        V((total, half_own * own, 2 * nbins), F32),
        V((half_own, heads * unit, 2 * length), LOW),
        V((half_own, chan, 2 * length), F32),
        V((half_own, nbins, 2 * length), LOW),
        V((half_own, chan, 2 * length), F32),
        V((half_own, chan, 2 * length), LOW),
        V((half_own, chan, 2 * length), LOW),
        V((items, heads, own, width, length), LOW),
        V((items, rows, width, length), LOW),
        V((heads * width, chan), F32),
        V((heads * unit, chan), F32),
        V((heads * unit, chan), F32),
        V((nbins, chan), F32),
        V((1, length), F32),
        V((nbins, length), F32),
        V((2, groups, 2 * block_rows, chan), F32),
        V((groups, 2 * block_rows, chan), LOW),
        V((groups, 2 * block_rows, chan), LOW),
        V((groups, 2 * block_rows, chan), F32),
        V((groups, 2 * block_rows, chan), LOW),
        V((groups, 2 * block_rows, chan), LOW),
        V((2 * block_rows, chan), F32),
        V((block_rows, chan), F32),
        V((block_rows, chan), F32),
        V((block_rows + 8, chan), LOW),
        V((items, length, length), F32),
        V((8, length, length), LOW),
        V((8, width, length), LOW),
        V((4 * width, 8 * length), LOW),
        V((items, length, length), LOW),
        V((items, groups, rows, length), LOW),
        V((4 * width, chan), F32),
        V((1, chan), F32),
        V((groups, sh, chan), F32),
        V((sh, chan), LOW),
        V((8, chan), F32),
        V((total, 8, chan), F32),
    ]
    scratch += [
        dma((items, rows // 8)),
        dma((items, 2)),
        dma((2,)),
        dma((3, 2)),
        dma((items, 2)),
        dma((items, 2)),
        dma((items, 2, 2)),
        dma((2,)),
        dma((2,)),
        dma((2,)),
        dma((2,)),
        dma((items, 2)),
        dma((2,)),
        dma((2,)),
        dma((2,)),
    ]
    grads = pl.pallas_call(
        partial(step_kernel, groups, heads),
        out_shape=[
            jax.ShapeDtypeStruct((groups, sh, chan), LOW),
            jax.ShapeDtypeStruct((groups, block_rows + 8, chan), LOW),
            jax.ShapeDtypeStruct((nbins, chan), F32),
            jax.ShapeDtypeStruct((8, chan), F32),
        ],
        in_specs=[pl.BlockSpec(memory_space=pl.ANY), pl.BlockSpec(memory_space=pltpu.SMEM)] + [vmem] * 8,
        out_specs=[vmem] * 4,
        scratch_shapes=scratch,
        compiler_params=pltpu.CompilerParams(
            collective_id=0, has_side_effects=True, vmem_limit_bytes=60 * 2**20
        ),
        name="step",
    )(pair_input, lengths, distogram_bins, *weights)
    like = lambda group: [jax.ShapeDtypeStruct(w.shape, F32) for w in group]
    outs = pl.pallas_call(
        partial(update_kernel, groups),
        out_shape=[jax.ShapeDtypeStruct((1, 1), F32)] * 2 + like(weights) * 3,
        in_specs=[vmem] * 25,
        out_specs=[vmem] * 23,
        name="update",
    )(*grads, *weights, *momenta, *averages)
    outs = list(outs)
    outs[0], outs[1] = outs[0].reshape(()), outs[1].reshape(())
    for k in (2, 9, 16):
        outs[k + 1] = outs[k + 1].reshape(chan, 1)
        outs[k + 5] = outs[k + 5].T
    return tuple(outs)


def body(groups, heads, *args):
    items, rows, length, channels = args[0].shape
    own = rows // heads
    if heads == 4 and own == 8 and rows % 16 == 0 and length % 128 == 0:
        return fused_body(groups, heads, *args)
    return general_body(*args)


def solution(mesh):
    in_specs = (
        P(None, "res", None, None),
        P(),
        P(None, "res", None),
        P(None, "head"),
        P(None, "head"),
        P("head", None),
        P(None, "head"),
        P("head", None),
        P(),
        P(),
        P(None, "head"),
        P(None, "head"),
        P("head", None),
        P(None, "head"),
        P("head", None),
        P(),
        P(),
        P(None, "head"),
        P(None, "head"),
        P("head", None),
        P(None, "head"),
        P("head", None),
        P(),
        P(),
    )
    out_specs = (
        P(),
        P(),
        P(None, "head"),
        P(None, "head"),
        P("head", None),
        P(None, "head"),
        P("head", None),
        P(),
        P(),
        P(None, "head"),
        P(None, "head"),
        P("head", None),
        P(None, "head"),
        P("head", None),
        P(),
        P(),
        P(None, "head"),
        P(None, "head"),
        P("head", None),
        P(None, "head"),
        P("head", None),
        P(),
        P(),
    )
    return jax.shard_map(
        partial(body, mesh.shape["res"], mesh.shape["head"]), mesh=mesh, in_specs=in_specs, out_specs=out_specs, check_vma=False)
```
